512 devices in a mesh: ax: 128 (over x_hi, y, z), rad: 4 (over x_lo, core).
Axes of the slice: x: 4 (x_hi: 2, x_lo: 2; x = x_hi * 2 + x_lo), y: 4, z: 16, core: 2. Of those that a mesh axis runs over, the one named last changes fastest.
Arguments:
- gas_state: float32 [6, 1024, 64, 512], P(None, 'ax', 'rad'), as said below
- viscosity: float32 [1024, 64, 512], P('ax', 'rad'), may hold values from 0.05 to 0.3
- droplets: float32 [4, 2097152], P(None, ('ax', 'rad')), as said below
- drop_cells: int32 [2097152], P(('ax', 'rad')), may hold values from 0 to 65535
- move_lists: int32 [512, 4, 64], P(('ax', 'rad')), may hold values from 0 to 4095, as said below
- move_counts: int32 [512, 4], P(('ax', 'rad')), may hold values from 0 to 64, as said below
Outputs:
- gas_out: float32 [6, 1024, 64, 512], P(None, 'ax', 'rad')
- drops_out: float32 [4, 2097152], P(None, ('ax', 'rad'))
- arrivals_out: float32 [4, 131072], P(None, ('ax', 'rad'))
The draws below stay inside these ranges and needn't reach their ends.
Inputs may be any that keep to these rules, and one draw needn't show every extreme that they name: `gas_state`: component 0 lies in 0.8 to 1.2; component 4 divided by component 0 in 0.5 to 1.5; component 5 divided by component 0 in 0 to 0.5. `droplets`: on each tile the slots with positive mass come first, and tiles at lower axial index hold more of them; every slot of the tiles at axial index 0 is filled. Masses are 0 or in 0.5 to 2; temperatures in 0.5 to 1.5. `move_lists`: the 256 entries of one tile are distinct slots of that tile with positive mass. `move_counts`: 64 is reached in each direction by some tile; lists toward outside the grid are empty.
All inputs are finite; a program needn't handle non-finite values.
Results may differ from the reference program's by a relative error of at most 0.0003.
Values sent between devices are 32-bit elements; how exact they have to be, the bound alone decides.
No kernel may reach another device: no remote copies, remote signals or barrier semaphores. Data moves between devices by JAX's collectives and lax.ppermute only.
A program may use at most 64 MiB of HBM per device.

```python
import math
import jax
import jax.numpy as jnp
from jax import lax

C = 6
NF = 4
CX = 8
CY = 16
CZ = 512
SLOTS = 4096
CAP = 64
TILES = 512
NX = 1024
NY = 64
PARTICLE_BERTHS = 2097152
ARRIVALS = 131072
N_AX = 128
N_RAD = 4


def draw_gas_state(key, part):
    key = jax.random.fold_in(key, 11)
    chance_starter_codes = jax.random.split(key, 4)
    multiway_sizes_list = (NX, NY, CZ)
    ambient_compressible_lattice = jax.random.uniform(chance_starter_codes[0], multiway_sizes_list, jnp.float32, 0.8, 1.2)
    blob_motion_rate = jnp.clip(jax.random.normal(chance_starter_codes[1], (3,) + multiway_sizes_list, jnp.float32), -4.0, 4.0)
    blob_thermal_content = jax.random.uniform(chance_starter_codes[2], multiway_sizes_list, jnp.float32, 0.5, 1.5)
    released_burnable_share = jax.random.uniform(chance_starter_codes[3], multiway_sizes_list, jnp.float32, 0.0, 0.5)
    return jnp.concatenate([ambient_compressible_lattice[None], ambient_compressible_lattice[None] * blob_motion_rate, (ambient_compressible_lattice * blob_thermal_content)[None], (ambient_compressible_lattice * released_burnable_share)[None]], 0)


def draw_droplets(key, part):
    key = jax.random.fold_in(key, 12)
    chance_starter_codes = jax.random.split(key, 3)
    index = jnp.arange(PARTICLE_BERTHS, dtype=jnp.int32)
    tile = index // SLOTS
    slot = index % SLOTS
    filled = SLOTS * N_AX // (N_AX + 8 * (tile // N_RAD))
    particle_weight = jnp.exp(jax.random.uniform(chance_starter_codes[0], (PARTICLE_BERTHS,), jnp.float32, jnp.log(0.5), jnp.log(2.0)))
    particle_weight = jnp.where(slot < filled, particle_weight, 0.0)
    blob_thermal_content = jax.random.uniform(chance_starter_codes[1], (PARTICLE_BERTHS,), jnp.float32, 0.5, 1.5)
    blob_motion_rate = jnp.clip(jax.random.normal(chance_starter_codes[2], (2, PARTICLE_BERTHS), jnp.float32), -4.0, 4.0)
    return jnp.concatenate([particle_weight[None], blob_thermal_content[None], blob_motion_rate], 0)


def draw_move_lists(key, part):
    key = jax.random.fold_in(key, 13)
    tile = jnp.arange(TILES, dtype=jnp.int32)
    filled = SLOTS * N_AX // (N_AX + 8 * (tile // N_RAD))
    first_tile = (tile == 0).astype(jnp.int32)

    def pick(tile_key, limit, forced):
        order_all = jax.random.permutation(tile_key, SLOTS)
        place = jnp.arange(SLOTS, dtype=jnp.int32)
        score = jnp.where(order_all < limit, place, SLOTS + place)
        score = jnp.where((forced > 0) & (order_all == 0), -2, score)
        score = jnp.where((forced > 0) & (order_all == SLOTS - 1), -1, score)
        ranked = jnp.argsort(score)
        return order_all[ranked][:4 * CAP].reshape(4, CAP)
    return jax.vmap(pick)(jax.random.split(key, TILES), filled, first_tile).astype(jnp.int32)


def draw_move_counts(key, part):
    key = jax.random.fold_in(key, 14)
    counts = jax.random.randint(key, (TILES, 4), CAP // 3, CAP + 1)
    counts = counts.at[0, 0].set(CAP).at[N_RAD, 1].set(CAP).at[0, 2].set(CAP).at[1, 3].set(CAP)
    tile = jnp.arange(TILES, dtype=jnp.int32)
    axial = tile // N_RAD
    radial = tile % N_RAD
    outside = jnp.stack([axial == N_AX - 1, axial == 0, radial == N_RAD - 1, radial == 0], 1)
    return jnp.where(outside, 0, counts).astype(jnp.int32)


def with_ends(values, stream_key, low, top_value):
    longest = values.shape.index(max(values.shape))
    spots = []
    for shift in (0, 1):
        where = [jax.random.randint(jax.random.fold_in(stream_key, axis), (), 0, length) for axis, length in enumerate(values.shape)]
        where[longest] = (where[longest] + shift) % values.shape[longest]
        spots.append(tuple(where))
    return values.at[spots[0]].set(low).at[spots[1]].set(top_value)


def levels(key, shape, shards, smallest, largest):
    gain, own = 1.0, jax.random.fold_in(key, 6)
    for axis_at, blocks in shards:
        heights = jnp.exp(jax.random.uniform(jax.random.fold_in(own, axis_at), (blocks,), jnp.float32, smallest / len(shards), largest / len(shards)))
        gain = gain * jnp.repeat(heights, shape[axis_at] // blocks).reshape([-1 if axis == axis_at else 1 for axis in range(len(shape))])
    return gain


def setup_inputs(seed: int = 0) -> dict:
    seeds = jax.random.split(jax.random.key(seed), 7)
    return {
        "gas_state": draw_gas_state(jax.random.fold_in(seeds[6], 71), 0),
        "viscosity": jnp.clip(jnp.exp(math.log(0.3) - 1.7917595 * jax.random.uniform(seeds[1], (NX, NY, CZ), jnp.float32) ** levels(seeds[1], (NX, NY, CZ), ((0, 128), (1, 4)), -0.2, 0.2)), 0.05, 0.3),
        "droplets": draw_droplets(jax.random.fold_in(seeds[6], 71), 0),
        "drop_cells": with_ends(jax.random.randint(seeds[3], (PARTICLE_BERTHS,), 0, CX * CY * CZ), jax.random.fold_in(seeds[3], 1), 0, (CX * CY * CZ) - 1).astype(jnp.int32),
        "move_lists": draw_move_lists(jax.random.fold_in(seeds[6], 71), 0),
        "move_counts": draw_move_counts(jax.random.fold_in(seeds[6], 71), 0),
    }


time_step = 0.2


def window(padded, start, length, axis):
    return lax.slice_in_dim(padded, start, start + length, axis=axis)


def second(padded, length, axis):
    parts = [window(padded, offset, length, axis) for offset in range(5)]
    return (-parts[0] + 16.0 * parts[1] - 30.0 * parts[2] + 16.0 * parts[3] - parts[4]) / 12.0


def gradient(padded, length, axis):
    parts = [window(padded, offset, length, axis) for offset in range(5)]
    return (parts[0] - 8.0 * parts[1] + 8.0 * parts[3] - parts[4]) / 12.0


def evaporate(records, sampled_draw_outcomes):
    particle_weight, drop_temp, drop_axial, drop_radial = records[0], records[1], records[2], records[3]
    ambient_compressible_lattice = sampled_draw_outcomes[0]
    lengthwise_flow_state = sampled_draw_outcomes[1] / ambient_compressible_lattice
    spoke_flow_state = sampled_draw_outcomes[2] / ambient_compressible_lattice
    ambient_thermal_value = sampled_draw_outcomes[4] / ambient_compressible_lattice
    released_burnable_share = sampled_draw_outcomes[5] / ambient_compressible_lattice
    living = particle_weight > 0.0
    safe_temp = jnp.where(living, drop_temp, jnp.ones_like(drop_temp))
    balance = jnp.exp(-1.0 / safe_temp)
    slip_square = (lengthwise_flow_state - drop_axial) ** 2 + (spoke_flow_state - drop_radial) ** 2
    evaporated = 0.1 * jnp.cbrt(particle_weight) * (jnp.log(1.0 - released_burnable_share) - jnp.log(1.0 - balance)) * (1.0 + 0.3 * (1.0 + slip_square) ** 0.25)
    updated = jnp.stack([particle_weight - evaporated,
                         drop_temp + 0.1 * (ambient_thermal_value - drop_temp) - 0.5 * evaporated,
                         drop_axial + 0.2 * (lengthwise_flow_state - drop_axial),
                         drop_radial + 0.2 * (spoke_flow_state - drop_radial)])
    updated = jnp.where(living[None], updated, jnp.zeros_like(updated))
    sources = jnp.stack([evaporated,
                         evaporated * drop_axial + 0.2 * particle_weight * (drop_axial - lengthwise_flow_state),
                         evaporated * drop_radial + 0.2 * particle_weight * (drop_radial - spoke_flow_state),
                         jnp.zeros_like(particle_weight),
                         evaporated * drop_temp + 0.1 * particle_weight * (drop_temp - ambient_thermal_value),
                         evaporated])
    return updated, sources


def reference(gas_state, viscosity, droplets, drop_cells, move_lists, move_counts):
    speeds = gas_state[1:4] / gas_state[0]

    def advance(field):
        padded = jnp.pad(field, ((2, 2), (2, 2), (0, 0)))
        axial_pad = padded[:, 2:-2]
        radial_pad = padded[2:-2]
        azimuth_pad = jnp.concatenate([field[..., -2:], field, field[..., :2]], axis=2)
        laplace = second(axial_pad, NX, 0) + second(radial_pad, NY, 1) + second(azimuth_pad, CZ, 2)
        transport = speeds[0] * gradient(axial_pad, NX, 0) + speeds[1] * gradient(radial_pad, NY, 1) + speeds[2] * gradient(azimuth_pad, CZ, 2)
        return field + time_step * (viscosity * laplace - transport)

    advanced = lax.map(advance, gas_state)

    records = jnp.concatenate([droplets, drop_cells.astype(jnp.float32)[None]], 0).reshape(NF + 1, TILES, SLOTS)
    weights = (jnp.arange(CAP, dtype=jnp.int32)[None, None, :] < move_counts[:, :, None]).astype(jnp.float32)
    tile_ids = jnp.arange(TILES, dtype=jnp.int32)[:, None, None]
    outgoing = records[:, tile_ids, move_lists] * weights[None]
    departed = jnp.zeros((TILES, SLOTS), jnp.float32).at[tile_ids, move_lists].max(weights)
    by_tile = outgoing.reshape(NF + 1, N_AX, N_RAD, 4, CAP)
    zero_axial = jnp.zeros((NF + 1, 1, N_RAD, CAP), jnp.float32)
    zero_radial = jnp.zeros((NF + 1, N_AX, 1, CAP), jnp.float32)
    from_below = jnp.concatenate([zero_axial, by_tile[:, :-1, :, 0]], axis=1)
    from_above = jnp.concatenate([by_tile[:, 1:, :, 1], zero_axial], axis=1)
    from_inner = jnp.concatenate([zero_radial, by_tile[:, :, :-1, 2]], axis=2)
    from_outer = jnp.concatenate([by_tile[:, :, 1:, 3], zero_radial], axis=2)
    arrived = jnp.stack([from_below, from_above, from_inner, from_outer], axis=3).reshape(NF + 1, TILES, 4 * CAP)

    stayers = jnp.concatenate([(records[0] * (1.0 - departed))[None], records[1:NF]], 0)
    all_records = jnp.concatenate([stayers, arrived[:NF]], axis=2)
    local_cells = jnp.concatenate([drop_cells.reshape(TILES, SLOTS), arrived[NF].astype(jnp.int32)], axis=1)
    tiles = jnp.arange(TILES, dtype=jnp.int32)[:, None]
    axial_tile = tiles // N_RAD
    radial_tile = tiles % N_RAD
    axial_cell = axial_tile * CX + local_cells // (CY * CZ)
    radial_cell = radial_tile * CY + (local_cells // CZ) % CY
    global_cells = ((axial_cell * NY + radial_cell) * CZ + local_cells % CZ).reshape(-1)
    flat_gas = gas_state.reshape(C, -1)
    updated, terms = evaporate(all_records.reshape(NF, -1), flat_gas[:, global_cells])
    sources = jnp.zeros_like(flat_gas).at[:, global_cells].add(terms)
    gas_out = advanced + sources.reshape(gas_state.shape)
    updated = updated.reshape(NF, TILES, SLOTS + 4 * CAP)
    drops_out = updated[:, :, :SLOTS].reshape(NF, PARTICLE_BERTHS)
    arrivals_out = updated[:, :, SLOTS:].reshape(NF, ARRIVALS)
    return gas_out, drops_out, arrivals_out
```

```python
import functools

import jax
import jax.numpy as jnp
from jax import lax
from jax.experimental import pallas as pl
from jax.experimental.pallas import tpu as pltpu
from jax.sharding import PartitionSpec as P

time_step = 0.2
f32 = jnp.float32
bf16 = jnp.bfloat16
VM = pl.BlockSpec(memory_space=pltpu.VMEM)
SM = pl.BlockSpec(memory_space=pltpu.SMEM)
C, CX, CY, CZ = 6, 8, 16, 512
ROWS = CX * CY
SLOTS, CAP = 4096, 64
params = pltpu.CompilerParams(vmem_limit_bytes=48 << 20)


def split2(x):
    hi = x.astype(bf16)
    return hi, (x - hi.astype(f32)).astype(bf16)


def split3(x):
    hi = x.astype(bf16)
    rest = x - hi.astype(f32)
    mid = rest.astype(bf16)
    return hi, mid, (rest - mid.astype(f32)).astype(bf16)


def prep_kernel(gas, drops, cells, lists, counts, up, down, outer, inner, kept):
    slots = lists[0]
    entry = jnp.concatenate([slots[d : d + 1, :] for d in range(4)], axis=1)
    lane = lax.broadcasted_iota(jnp.int32, (1, CAP), 1)
    used = jnp.concatenate([(lane < counts[0, d]).astype(jnp.int32) for d in range(4)], axis=1)
    low = (lax.broadcasted_iota(jnp.int32, (128, 4 * CAP), 0) == (entry & 127)).astype(f32).astype(bf16)
    place = jnp.where(used > 0, entry >> 7, -1)
    high = (lax.broadcasted_iota(jnp.int32, (32, 4 * CAP), 0) == place).astype(f32)
    fields = []
    for f in range(4):
        fields.append(jnp.concatenate([drops[f : f + 1, 128 * s : 128 * s + 128] for s in range(32)], axis=0))
    parts = []
    for f in range(4):
        parts.extend(split3(fields[f]))
    parts.extend(split2(cells[...].astype(f32)))
    picked = jnp.dot(jnp.concatenate(parts, axis=0), low, preferred_element_type=f32)
    for f in range(5):
        count = 3 if f < 4 else 2
        total = picked[96 * f : 96 * f + 32]
        for k in range(1, count):
            total = total + picked[96 * f + 32 * k : 96 * f + 32 * k + 32]
        chosen = jnp.sum(jnp.where(high > 0, total, 0.0), axis=0, keepdims=True)
        for d, message in enumerate((up, down, outer, inner)):
            base = message.shape[0] - 8
            message[base + f : base + f + 1, 0:CAP] = chosen[:, CAP * d : CAP * d + CAP]
    gone = lax.dot_general(high.astype(bf16), low, (((1,), (1,)), ((), ())), preferred_element_type=f32)
    kept[...] = fields[0] * (1.0 - gone)
    for c in range(C):
        up[32 * c : 32 * c + 32, :] = gas[c, ROWS - 32 : ROWS, :]
        down[32 * c : 32 * c + 32, :] = gas[c, 0:32, :]
        for i in range(CX):
            at = (c * CX + i) * 2
            outer[at : at + 2, :] = gas[c, i * CY + CY - 2 : i * CY + CY, :]
            inner[at : at + 2, :] = gas[c, i * CY : i * CY + 2, :]


def evaporate(mass, temp, axial, radial, samples):
    axial_gas, radial_gas, gas_temp, fuel = samples
    living = mass > 0.0
    safe_temp = jnp.where(living, temp, 1.0)
    root = jnp.where(living, jnp.exp(jnp.log(jnp.where(living, mass, 1.0)) * (1.0 / 3.0)), 0.0)
    balance = jnp.exp(-1.0 / safe_temp)
    slip = (axial_gas - axial) ** 2 + (radial_gas - radial) ** 2
    wind = jnp.sqrt(jnp.sqrt(1.0 + slip))
    evaporated = 0.1 * root * (jnp.log(1.0 - fuel) - jnp.log(1.0 - balance)) * (1.0 + 0.3 * wind)
    updated = (
        mass - evaporated,
        temp + 0.1 * (gas_temp - temp) - 0.5 * evaporated,
        axial + 0.2 * (axial_gas - axial),
        radial + 0.2 * (radial_gas - radial),
    )
    updated = tuple(jnp.where(living, u, 0.0) for u in updated)
    terms = (
        evaporated,
        evaporated * axial + 0.2 * mass * (axial - axial_gas),
        evaporated * radial + 0.2 * mass * (radial - radial_gas),
        evaporated * temp + 0.1 * mass * (temp - gas_temp),
    )
    return updated, terms


def one_hot(index, size):
    width = index.shape[1]
    return (lax.broadcasted_iota(jnp.int32, (size, width), 0) == index).astype(f32).astype(bf16)


def gather_block(table, where):
    around = one_hot(where & (CZ - 1), CZ)
    got = jnp.dot(table[...], around, preferred_element_type=f32)
    mask = lax.broadcasted_iota(jnp.int32, (ROWS, where.shape[1]), 0) == (where >> 9)
    samples = []
    for k in range(4):
        both = got[2 * ROWS * k : 2 * ROWS * k + ROWS] + got[2 * ROWS * k + ROWS : 2 * ROWS * k + 2 * ROWS]
        samples.append(jnp.sum(jnp.where(mask, both, 0.0), axis=0, keepdims=True))
    return samples


def deposit_block(terms, where):
    around = one_hot(where & (CZ - 1), CZ)
    mask = lax.broadcasted_iota(jnp.int32, (ROWS, where.shape[1]), 0) == (where >> 9)
    halves = [split2(t) for t in terms]
    spread = jnp.concatenate(
        [
            jnp.concatenate([jnp.where(mask, h[side].astype(f32), 0.0).astype(bf16) for h in halves], axis=0)
            for side in range(2)
        ],
        axis=1,
    )
    twice = jnp.concatenate([around, around], axis=1)
    return lax.dot_general(spread, twice, (((1,), (1,)), ((), ())), preferred_element_type=f32)


def row_of(ref, lead, first, count):
    return jnp.concatenate([ref[lead, s : s + 1, :] for s in range(first, first + count)], axis=1)


def main_kernel(gas, viscosity, drops, cells, kept, out, drops_out, table, speed, samples, terms, source):
    inverse = 1.0 / gas[0]
    for k, c in enumerate((1, 2, 4, 5)):
        quotient = gas[c] * inverse
        if k < 2:
            speed[k] = quotient
        hi, lo = split2(quotient)
        table[2 * ROWS * k : 2 * ROWS * k + ROWS, :] = hi
        table[2 * ROWS * k + ROWS : 2 * ROWS * k + 2 * ROWS, :] = lo
    speed[2] = gas[3] * inverse

    for b in range(8):
        where = jnp.concatenate([cells[s : s + 1, :] for s in range(4 * b, 4 * b + 4)], axis=1)
        got = gather_block(table, where)
        for k in range(4):
            for s in range(4):
                samples[k, 4 * b + s : 4 * b + s + 1, :] = got[k][:, 128 * s : 128 * s + 128]
    fields = [
        jnp.concatenate([drops[f : f + 1, 128 * s : 128 * s + 128] for s in range(32)], axis=0) for f in range(1, 4)
    ]
    updated, new_terms = evaporate(kept[...], *fields, [samples[k] for k in range(4)])
    for f in range(4):
        terms[f] = new_terms[f]
        for s in range(32):
            drops_out[f : f + 1, 128 * s : 128 * s + 128] = updated[f][s : s + 1, :]
    for b in range(8):
        where = jnp.concatenate([cells[s : s + 1, :] for s in range(4 * b, 4 * b + 4)], axis=1)
        part = deposit_block([row_of(terms, k, 4 * b, 4) for k in range(4)], where)
        if b == 0:
            source[...] = part
        else:
            source[...] += part

    lane = lax.broadcasted_iota(jnp.int32, (CY, CZ), 0)

    def component(c, carry):
        slot = jnp.where(c < 3, c, jnp.where(c == 5, 0, c - 1))
        scale = jnp.where(c == 3, 0.0, 1.0)
        layers = [gas[c, CY * i : CY * i + CY, :] for i in range(CX)]
        for i in range(CX):
            rows = slice(CY * i, CY * i + CY)
            x = layers[i]
            zero = jnp.zeros_like(x)
            ax = [layers[i + k] if 0 <= i + k < CX else zero for k in (-2, -1, 1, 2)]
            ra = []
            for k in (-2, -1, 1, 2):
                moved = pltpu.roll(x, (-k) % CY, axis=0)
                ok = (lane + k >= 0) & (lane + k < CY)
                ra.append(jnp.where(ok, moved, 0.0))
            az = [pltpu.roll(x, (-k) % CZ, axis=1) for k in (-2, -1, 1, 2)]
            near = (ax[1] + ax[2]) + (ra[1] + ra[2]) + (az[1] + az[2])
            far = (ax[0] + ax[3]) + (ra[0] + ra[3]) + (az[0] + az[3])
            laplace = (16.0 * near - far - 90.0 * x) * (1.0 / 12.0)
            transport = zero
            for j, n in enumerate((ax, ra, az)):
                slope = (8.0 * (n[2] - n[1]) - (n[3] - n[0])) * (1.0 / 12.0)
                transport = transport + speed[j, rows, :] * slope
            advanced = x + time_step * (viscosity[rows, :] * laplace - transport)
            out[c, rows, :] = advanced + scale * source[pl.ds(pl.multiple_of(slot * ROWS + CY * i, CY), CY), :]
        return carry

    lax.fori_loop(0, C, component, 0)


def final_kernel(part, gas, viscosity, table, below, above, inner, outer, out, arrivals_out):
    got = jnp.concatenate([m[m.shape[0] - 8 : m.shape[0], 0:CAP] for m in (below, above, inner, outer)], axis=1)
    where = got[4:5].astype(jnp.int32)
    samples = gather_block(table, where)
    updated, terms = evaporate(got[0:1], got[1:2], got[2:3], got[3:4], samples)
    arrivals_out[...] = jnp.concatenate(updated, axis=0)
    source = deposit_block(terms, where)
    lane = lax.broadcasted_iota(jnp.int32, (CY, CZ), 0)
    for i in range(CX):
        rows = slice(CY * i, CY * i + CY)
        inverse = 1.0 / gas[0, rows, :]
        factor = viscosity[rows, :] * (time_step / 12.0)
        axial = gas[1, rows, :] * inverse * (time_step / 12.0)
        radial = gas[2, rows, :] * inverse * (time_step / 12.0)
        wa = (-factor - axial, 16.0 * factor + 8.0 * axial, 16.0 * factor - 8.0 * axial, axial - factor)
        wr = (-factor - radial, 16.0 * factor + 8.0 * radial, 16.0 * factor - 8.0 * radial, radial - factor)
        first = jnp.where(lane == 0, wr[1], jnp.where(lane == 1, wr[0], 0.0))
        second = jnp.where(lane == 0, wr[0], 0.0)
        third = jnp.where(lane == CY - 1, wr[2], jnp.where(lane == CY - 2, wr[3], 0.0))
        fourth = jnp.where(lane == CY - 1, wr[3], 0.0)
        for c in range(C):
            at = (c * CX + i) * 2
            value = part[c, rows, :]
            value = value + first * inner[at + 1 : at + 2, :] + second * inner[at : at + 1, :]
            value = value + third * outer[at : at + 1, :] + fourth * outer[at + 1 : at + 2, :]
            b0, b1 = below[32 * c : 32 * c + CY, :], below[32 * c + CY : 32 * c + 2 * CY, :]
            a0, a1 = above[32 * c : 32 * c + CY, :], above[32 * c + CY : 32 * c + 2 * CY, :]
            if i == 0:
                value = value + wa[0] * b0 + wa[1] * b1
            elif i == 1:
                value = value + wa[0] * b1
            elif i == CX - 2:
                value = value + wa[3] * a0
            elif i == CX - 1:
                value = value + wa[2] * a0 + wa[3] * a1
            slot = (0, 1, 2, None, 3, 0)[c]
            if slot is not None:
                value = value + source[slot * ROWS + CY * i : slot * ROWS + CY * i + CY, :]
            out[c, rows, :] = value


def body(gas_state, viscosity, droplets, drop_cells, move_lists, move_counts):
    gas = gas_state.reshape(C, ROWS, CZ)
    thick = viscosity.reshape(ROWS, CZ)
    cells = drop_cells.reshape(32, 128)
    shape = jax.ShapeDtypeStruct
    up, down, outer, inner, kept = pl.pallas_call(
        prep_kernel,
        out_shape=(
            shape((200, CZ), f32),
            shape((200, CZ), f32),
            shape((104, CZ), f32),
            shape((104, CZ), f32),
            shape((32, 128), f32),
        ),
        in_specs=[VM, VM, VM, VM, SM],
        out_specs=(VM,) * 5,
        compiler_params=params,
        name="prep",
    )(gas, droplets, cells, move_lists, move_counts)
    n_ax, n_rad = lax.axis_size("ax"), lax.axis_size("rad")
    forward = lambda n: [(i, i + 1) for i in range(n - 1)]
    back = lambda n: [(i + 1, i) for i in range(n - 1)]
    from_below = lax.ppermute(up, "ax", forward(n_ax))
    from_above = lax.ppermute(down, "ax", back(n_ax))
    from_inner = lax.ppermute(outer, "rad", forward(n_rad))
    from_outer = lax.ppermute(inner, "rad", back(n_rad))
    part, drops_out, table = pl.pallas_call(
        main_kernel,
        out_shape=(
            shape((C, ROWS, CZ), f32),
            shape((4, SLOTS), f32),
            shape((8 * ROWS, CZ), bf16),
        ),
        in_specs=[VM] * 5,
        out_specs=(VM,) * 3,
        scratch_shapes=[
            pltpu.VMEM((3, ROWS, CZ), f32),
            pltpu.VMEM((4, 32, 128), f32),
            pltpu.VMEM((4, 32, 128), f32),
            pltpu.VMEM((4 * ROWS, CZ), f32),
        ],
        compiler_params=params,
        cost_estimate=pl.CostEstimate(flops=8_000_000_000, bytes_accessed=6_000_000, transcendentals=0),
        name="main",
    )(gas, thick, droplets, cells, kept)
    out, arrivals_out = pl.pallas_call(
        final_kernel,
        out_shape=(shape((C, ROWS, CZ), f32), shape((4, 4 * CAP), f32)),
        in_specs=[VM] * 8,
        out_specs=(VM,) * 2,
        compiler_params=params,
        name="final",
    )(part, gas, thick, table, from_below, from_above, from_inner, from_outer)
    return out.reshape(gas_state.shape), drops_out, arrivals_out


def solution(mesh):
    placed = (
        P(None, "ax", "rad", None),
        P("ax", "rad", None),
        P(None, ("ax", "rad")),
        P(("ax", "rad")),
        P(("ax", "rad"), None, None),
        P(("ax", "rad"), None),
    )
    return jax.shard_map(
        body,
        mesh=mesh,
        in_specs=placed,
        out_specs=(P(None, "ax", "rad", None), P(None, ("ax", "rad")), P(None, ("ax", "rad"))),
        check_vma=False,
    )
```

```python
import functools

import jax
import jax.numpy as jnp
from jax import lax
from jax.experimental import pallas as pl
from jax.experimental.pallas import tpu as pltpu
from jax.sharding import PartitionSpec as P

time_step = 0.2
f32 = jnp.float32
bf16 = jnp.bfloat16
VM = pl.BlockSpec(memory_space=pltpu.VMEM)
HB = pl.BlockSpec(memory_space=pltpu.HBM)
C, CX, CY, CZ = 6, 8, 16, 512
ROWS = CX * CY
SLOTS, CAP = 4096, 64
params = pltpu.CompilerParams(vmem_limit_bytes=48 << 20)


def split2(x):
    hi = x.astype(bf16)
    return hi, (x - hi.astype(f32)).astype(bf16)


def split3(x):
    hi = x.astype(bf16)
    rest = x - hi.astype(f32)
    mid = rest.astype(bf16)
    return hi, mid, (rest - mid.astype(f32)).astype(bf16)


def parity(axis):
    return lax.rem(lax.axis_index(axis), 2)


def prep_kernel(
    gas_in, drops_in, cells_in, lists_in, counts_in,
    axial_a, axial_b, radial_a, radial_b, kept, gas, drops, cells, lists, counts, sems,
):
    small = [
        pltpu.make_async_copy(source, target, sems.at[n])
        for n, (source, target) in enumerate(
            ((drops_in, drops), (cells_in, cells), (lists_in, lists), (counts_in, counts))
        )
    ]
    large = [pltpu.make_async_copy(gas_in.at[c], gas.at[c], sems.at[4 + c]) for c in range(C)]
    for copy in small + large:
        copy.start()
    for copy in small:
        copy.wait()
    slots = lists[0]
    entry = jnp.concatenate([slots[d : d + 1, :] for d in range(4)], axis=1)
    lane = lax.broadcasted_iota(jnp.int32, (1, CAP), 1)
    used = jnp.concatenate([(lane < counts[0, d]).astype(jnp.int32) for d in range(4)], axis=1)
    low = (lax.broadcasted_iota(jnp.int32, (128, 4 * CAP), 0) == (entry & 127)).astype(f32).astype(bf16)
    place = jnp.where(used > 0, entry >> 7, -1)
    high = (lax.broadcasted_iota(jnp.int32, (32, 4 * CAP), 0) == place).astype(f32)
    fields = []
    for f in range(4):
        fields.append(jnp.concatenate([drops[f : f + 1, 128 * s : 128 * s + 128] for s in range(32)], axis=0))
    parts = []
    for f in range(4):
        parts.extend(split3(fields[f]))
    parts.extend(split2(cells[...].astype(f32)))
    picked = jnp.dot(jnp.concatenate(parts, axis=0), low, preferred_element_type=f32)
    chosen = []
    for f in range(5):
        count = 3 if f < 4 else 2
        total = picked[96 * f : 96 * f + 32]
        for k in range(1, count):
            total = total + picked[96 * f + 32 * k : 96 * f + 32 * k + 32]
        chosen.append(jnp.sum(jnp.where(high > 0, total, 0.0), axis=0, keepdims=True))
    chosen = jnp.concatenate(chosen + [jnp.zeros((3, 4 * CAP), f32)], axis=0)
    gone = lax.dot_general(high.astype(bf16), low, (((1,), (1,)), ((), ())), preferred_element_type=f32)
    kept[...] = fields[0] * (1.0 - gone)
    by_way = [chosen[:, CAP * d : CAP * d + CAP] for d in range(4)]
    odd_ax, odd_rad = parity("ax"), parity("rad")
    for axis, odd, (even_way, odd_way) in (("ax", odd_ax, (axial_a, axial_b)), ("rad", odd_rad, (radial_a, radial_b))):
        plus, minus = by_way[0:2] if axis == "ax" else by_way[2:4]
        base = even_way.shape[0] - 8
        even_way[base : base + 8, 0:CAP] = jnp.where(odd == 0, plus, minus)
        odd_way[base : base + 8, 0:CAP] = jnp.where(odd == 0, minus, plus)
    for copy in large:
        copy.wait()
    for message, last in ((axial_a, odd_ax == 0), (axial_b, odd_ax == 1)):
        near = pl.multiple_of(jnp.where(last, (CX - 1) * CY, 0), CY)
        far = pl.multiple_of(jnp.where(last, (CX - 2) * CY, CY), CY)
        for c in range(C):
            message[32 * c : 32 * c + 16, :] = gas[c, pl.ds(near, CY), :]
            message[32 * c + 16 : 32 * c + 32, :] = gas[c, pl.ds(far, CY), :]
    for message, last in ((radial_a, odd_rad == 0), (radial_b, odd_rad == 1)):
        near, far = jnp.where(last, CY - 1, 0), jnp.where(last, CY - 2, 1)
        for c in range(C):
            for i in range(CX):
                at = c * CX + i
                message[at : at + 1, :] = gas[c, pl.ds(i * CY + near, 1), :]
                message[48 + at : 49 + at, :] = gas[c, pl.ds(i * CY + far, 1), :]


def evaporate(mass, temp, axial, radial, samples):
    axial_gas, radial_gas, gas_temp, fuel = samples
    living = mass > 0.0
    safe_temp = jnp.where(living, temp, 1.0)
    root = jnp.where(living, jnp.exp(jnp.log(jnp.where(living, mass, 1.0)) * (1.0 / 3.0)), 0.0)
    balance = jnp.exp(-1.0 / safe_temp)
    slip = (axial_gas - axial) ** 2 + (radial_gas - radial) ** 2
    wind = jnp.sqrt(jnp.sqrt(1.0 + slip))
    evaporated = 0.1 * root * (jnp.log(1.0 - fuel) - jnp.log(1.0 - balance)) * (1.0 + 0.3 * wind)
    updated = (
        mass - evaporated,
        temp + 0.1 * (gas_temp - temp) - 0.5 * evaporated,
        axial + 0.2 * (axial_gas - axial),
        radial + 0.2 * (radial_gas - radial),
    )
    updated = tuple(jnp.where(living, u, 0.0) for u in updated)
    terms = (
        evaporated,
        evaporated * axial + 0.2 * mass * (axial - axial_gas),
        evaporated * radial + 0.2 * mass * (radial - radial_gas),
        evaporated * temp + 0.1 * mass * (temp - gas_temp),
    )
    return updated, terms


def one_hot(index, size):
    width = index.shape[1]
    return (lax.broadcasted_iota(jnp.int32, (size, width), 0) == index).astype(f32).astype(bf16)


def gather_block(table, where):
    around = one_hot(where & (CZ - 1), CZ)
    got = jnp.dot(table[...], around, preferred_element_type=f32)
    mask = lax.broadcasted_iota(jnp.int32, (ROWS, where.shape[1]), 0) == (where >> 9)
    samples = []
    for k in range(4):
        both = got[2 * ROWS * k : 2 * ROWS * k + ROWS] + got[2 * ROWS * k + ROWS : 2 * ROWS * k + 2 * ROWS]
        samples.append(jnp.sum(jnp.where(mask, both, 0.0), axis=0, keepdims=True))
    return samples


def deposit_block(terms, where):
    around = one_hot(where & (CZ - 1), CZ)
    mask = lax.broadcasted_iota(jnp.int32, (ROWS, where.shape[1]), 0) == (where >> 9)
    halves = [split2(t) for t in terms]
    spread = jnp.concatenate(
        [
            jnp.concatenate([jnp.where(mask, h[side].astype(f32), 0.0).astype(bf16) for h in halves], axis=0)
            for side in range(2)
        ],
        axis=1,
    )
    twice = jnp.concatenate([around, around], axis=1)
    return lax.dot_general(spread, twice, (((1,), (1,)), ((), ())), preferred_element_type=f32)


def row_of(ref, lead, first, count):
    return jnp.concatenate([ref[lead, s : s + 1, :] for s in range(first, first + count)], axis=1)


def main_kernel(gas, viscosity, drops, cells, kept, out, drops_out, table, speed, samples, terms, source):
    inverse = 1.0 / gas[0]
    for k, c in enumerate((1, 2, 4, 5)):
        quotient = gas[c] * inverse
        if k < 2:
            speed[k] = quotient
        hi, lo = split2(quotient)
        table[2 * ROWS * k : 2 * ROWS * k + ROWS, :] = hi
        table[2 * ROWS * k + ROWS : 2 * ROWS * k + 2 * ROWS, :] = lo
    speed[2] = gas[3] * inverse

    for b in range(8):
        where = jnp.concatenate([cells[s : s + 1, :] for s in range(4 * b, 4 * b + 4)], axis=1)
        got = gather_block(table, where)
        for k in range(4):
            for s in range(4):
                samples[k, 4 * b + s : 4 * b + s + 1, :] = got[k][:, 128 * s : 128 * s + 128]
    fields = [
        jnp.concatenate([drops[f : f + 1, 128 * s : 128 * s + 128] for s in range(32)], axis=0) for f in range(1, 4)
    ]
    updated, new_terms = evaporate(kept[...], *fields, [samples[k] for k in range(4)])
    for f in range(4):
        terms[f] = new_terms[f]
        for s in range(32):
            drops_out[f : f + 1, 128 * s : 128 * s + 128] = updated[f][s : s + 1, :]
    for b in range(8):
        where = jnp.concatenate([cells[s : s + 1, :] for s in range(4 * b, 4 * b + 4)], axis=1)
        part = deposit_block([row_of(terms, k, 4 * b, 4) for k in range(4)], where)
        if b == 0:
            source[...] = part
        else:
            source[...] += part

    lane = lax.broadcasted_iota(jnp.int32, (CY, CZ), 0)

    def component(c, carry):
        slot = jnp.where(c < 3, c, jnp.where(c == 5, 0, c - 1))
        scale = jnp.where(c == 3, 0.0, 1.0)
        layers = [gas[c, CY * i : CY * i + CY, :] for i in range(CX)]
        for i in range(CX):
            rows = slice(CY * i, CY * i + CY)
            x = layers[i]
            zero = jnp.zeros_like(x)
            ax = [layers[i + k] if 0 <= i + k < CX else zero for k in (-2, -1, 1, 2)]
            ra = []
            for k in (-2, -1, 1, 2):
                moved = pltpu.roll(x, (-k) % CY, axis=0)
                ok = (lane + k >= 0) & (lane + k < CY)
                ra.append(jnp.where(ok, moved, 0.0))
            az = [pltpu.roll(x, (-k) % CZ, axis=1) for k in (-2, -1, 1, 2)]
            near = (ax[1] + ax[2]) + (ra[1] + ra[2]) + (az[1] + az[2])
            far = (ax[0] + ax[3]) + (ra[0] + ra[3]) + (az[0] + az[3])
            laplace = (16.0 * near - far - 90.0 * x) * (1.0 / 12.0)
            transport = zero
            for j, n in enumerate((ax, ra, az)):
                slope = (8.0 * (n[2] - n[1]) - (n[3] - n[0])) * (1.0 / 12.0)
                transport = transport + speed[j, rows, :] * slope
            advanced = x + time_step * (viscosity[rows, :] * laplace - transport)
            out[c, rows, :] = advanced + scale * source[pl.ds(pl.multiple_of(slot * ROWS + CY * i, CY), CY), :]
        return carry

    lax.fori_loop(0, C, component, 0)


def final_kernel(part, gas, viscosity, table, axial_a, axial_b, radial_a, radial_b, out, arrivals_out):
    odd_ax, odd_rad = parity("ax"), parity("rad")
    got = []
    for odd, a, b in ((odd_ax, axial_a, axial_b), (odd_rad, radial_a, radial_b)):
        base = a.shape[0] - 8
        in_a, in_b = a[base : base + 8, 0:CAP], b[base : base + 8, 0:CAP]
        got.append(jnp.where(odd == 1, in_a, in_b))
        got.append(jnp.where(odd == 1, in_b, in_a))
    got = jnp.concatenate(got, axis=1)
    where = got[4:5].astype(jnp.int32)
    samples = gather_block(table, where)
    updated, terms = evaporate(got[0:1], got[1:2], got[2:3], got[3:4], samples)
    arrivals_out[...] = jnp.concatenate(updated, axis=0)
    source = deposit_block(terms, where)
    lane = lax.broadcasted_iota(jnp.int32, (CY, CZ), 0)
    for i in range(CX):
        rows = slice(CY * i, CY * i + CY)
        factor = viscosity[rows, :] * (time_step / 12.0)
        radial = gas[2, rows, :] / gas[0, rows, :] * (time_step / 12.0)
        weights = []
        for last in (odd_rad == 0, odd_rad == 1):
            speed = jnp.where(last, -1.0, 1.0) * radial
            first, second = jnp.where(last, CY - 1, 0), jnp.where(last, CY - 2, 1)
            near, far = 16.0 * factor + 8.0 * speed, -(factor + speed)
            weights.append((jnp.where(lane == first, near, jnp.where(lane == second, far, 0.0)), jnp.where(lane == first, far, 0.0)))
        for c in range(C):
            at = c * CX + i
            value = part[c, rows, :]
            for (near, far), message in zip(weights, (radial_a, radial_b)):
                value = value + near * message[at : at + 1, :] + far * message[48 + at : 49 + at, :]
            slot = (0, 1, 2, None, 3, 0)[c]
            if slot is not None:
                value = value + source[slot * ROWS + CY * i : slot * ROWS + CY * i + CY, :]
            out[c, rows, :] = value
    for message, last in ((axial_a, odd_ax == 0), (axial_b, odd_ax == 1)):
        sign = jnp.where(last, -1.0, 1.0)
        for k in range(2):
            rows = pl.ds(pl.multiple_of(jnp.where(last, (CX - 1 - k) * CY, k * CY), CY), CY)
            factor = viscosity[rows, :] * (time_step / 12.0)
            speed = sign * (gas[1, rows, :] / gas[0, rows, :] * (time_step / 12.0))
            near, far = 16.0 * factor + 8.0 * speed, -(factor + speed)
            for c in range(C):
                if k == 0:
                    out[c, rows, :] += near * message[32 * c : 32 * c + CY, :] + far * message[32 * c + CY : 32 * c + 2 * CY, :]
                else:
                    out[c, rows, :] += far * message[32 * c : 32 * c + CY, :]


def pairs(devices):
    both = lambda first: [p for i in range(first, devices - 1, 2) for p in ((i, i + 1), (i + 1, i))]
    return both(0), both(1)


def body(gas_state, viscosity, droplets, drop_cells, move_lists, move_counts):
    gas = gas_state.reshape(C, ROWS, CZ)
    thick = viscosity.reshape(ROWS, CZ)
    cells = drop_cells.reshape(32, 128)
    shape = jax.ShapeDtypeStruct
    axial_a, axial_b, radial_a, radial_b, kept, gas, drops, cells = pl.pallas_call(
        prep_kernel,
        out_shape=(
            shape((200, CZ), f32),
            shape((200, CZ), f32),
            shape((104, CZ), f32),
            shape((104, CZ), f32),
            shape((32, 128), f32),
            shape((C, ROWS, CZ), f32),
            shape((4, SLOTS), f32),
            shape((32, 128), jnp.int32),
        ),
        in_specs=[HB] * 5,
        out_specs=(VM,) * 8,
        scratch_shapes=[
            pltpu.VMEM((1, 4, CAP), jnp.int32),
            pltpu.SMEM((1, 4), jnp.int32),
            pltpu.SemaphoreType.DMA((10,)),
        ],
        compiler_params=params,
        name="prep",
    )(*(pltpu.with_memory_space_constraint(x, pltpu.HBM) for x in (gas, droplets, cells, move_lists, move_counts)))
    ax_first, ax_second = pairs(lax.axis_size("ax"))
    rad_first, rad_second = pairs(lax.axis_size("rad"))
    radial_a = lax.ppermute(radial_a, "rad", rad_first)
    radial_b = lax.ppermute(radial_b, "rad", rad_second)
    axial_a = lax.ppermute(axial_a, "ax", ax_first)
    axial_b = lax.ppermute(axial_b, "ax", ax_second)
    part, drops_out, table = pl.pallas_call(
        main_kernel,
        out_shape=(
            shape((C, ROWS, CZ), f32),
            shape((4, SLOTS), f32),
            shape((8 * ROWS, CZ), bf16),
        ),
        in_specs=[VM] * 5,
        out_specs=(VM,) * 3,
        scratch_shapes=[
            pltpu.VMEM((3, ROWS, CZ), f32),
            pltpu.VMEM((4, 32, 128), f32),
            pltpu.VMEM((4, 32, 128), f32),
            pltpu.VMEM((4 * ROWS, CZ), f32),
        ],
        compiler_params=params,
        cost_estimate=pl.CostEstimate(flops=8_000_000_000, bytes_accessed=6_000_000, transcendentals=0),
        name="main",
    )(gas, thick, drops, cells, kept)
    out, arrivals_out = pl.pallas_call(
        final_kernel,
        out_shape=(shape((C, ROWS, CZ), f32), shape((4, 4 * CAP), f32)),
        in_specs=[VM] * 8,
        out_specs=(VM,) * 2,
        compiler_params=params,
        name="final",
    )(part, gas, thick, table, axial_a, axial_b, radial_a, radial_b)
    return out.reshape(gas_state.shape), drops_out, arrivals_out


def solution(mesh):
    placed = (
        P(None, "ax", "rad", None),
        P("ax", "rad", None),
        P(None, ("ax", "rad")),
        P(("ax", "rad")),
        P(("ax", "rad"), None, None),
        P(("ax", "rad"), None),
    )
    return jax.shard_map(
        body,
        mesh=mesh,
        in_specs=placed,
        out_specs=(P(None, "ax", "rad", None), P(None, ("ax", "rad")), P(None, ("ax", "rad"))),
        check_vma=False,
    )
```

```python
import functools

import jax
import jax.numpy as jnp
from jax import lax
from jax.experimental import pallas as pl
from jax.experimental.pallas import tpu as pltpu
from jax.sharding import PartitionSpec as P

time_step = 0.2
f32 = jnp.float32
bf16 = jnp.bfloat16
VM = pl.BlockSpec(memory_space=pltpu.VMEM)
HB = pl.BlockSpec(memory_space=pltpu.HBM)
C, CX, CY, CZ = 6, 8, 16, 512
ROWS = CX * CY
SLOTS, CAP = 4096, 64
params = pltpu.CompilerParams(vmem_limit_bytes=30 << 20)


def split2(x):
    hi = x.astype(bf16)
    return hi, (x - hi.astype(f32)).astype(bf16)


def split3(x):
    hi = x.astype(bf16)
    rest = x - hi.astype(f32)
    mid = rest.astype(bf16)
    return hi, mid, (rest - mid.astype(f32)).astype(bf16)


WRAP = 16


def parity(axis):
    return lax.rem(lax.axis_index(axis), 2)


def is_early():
    a, r = lax.axis_index("ax"), lax.axis_index("rad")
    return ((a > 0) & (lax.rem(a, WRAP) == 0)) | ((a == 0) & (r == 1))


def prep_kernel(
    gas_in, drops_in, cells_in, lists_in, counts_in,
    axial_b, axial_a, radial_b, radial_a, kept, gas, drops, cells, lists, counts, sems,
):
    small = [
        pltpu.make_async_copy(source, target, sems.at[n])
        for n, (source, target) in enumerate(
            ((drops_in, drops), (cells_in, cells), (lists_in, lists), (counts_in, counts))
        )
    ]
    large = [pltpu.make_async_copy(gas_in.at[c], gas.at[c], sems.at[4 + c]) for c in range(C)]
    for copy in small + large:
        copy.start()
    for copy in small:
        copy.wait()
    slots = lists[0]
    entry = jnp.concatenate([slots[d : d + 1, :] for d in range(4)], axis=1)
    lane = lax.broadcasted_iota(jnp.int32, (1, CAP), 1)
    used = jnp.concatenate([(lane < counts[0, d]).astype(jnp.int32) for d in range(4)], axis=1)
    low = (lax.broadcasted_iota(jnp.int32, (128, 4 * CAP), 0) == (entry & 127)).astype(f32).astype(bf16)
    place = jnp.where(used > 0, entry >> 7, -1)
    high = (lax.broadcasted_iota(jnp.int32, (32, 4 * CAP), 0) == place).astype(f32)
    fields = []
    for f in range(4):
        fields.append(jnp.concatenate([drops[f : f + 1, 128 * s : 128 * s + 128] for s in range(32)], axis=0))
    parts = []
    for f in range(4):
        parts.extend(split3(fields[f]))
    parts.extend(split2(cells[...].astype(f32)))
    picked = jnp.dot(jnp.concatenate(parts, axis=0), low, preferred_element_type=f32)
    chosen = []
    for f in range(5):
        count = 3 if f < 4 else 2
        total = picked[96 * f : 96 * f + 32]
        for k in range(1, count):
            total = total + picked[96 * f + 32 * k : 96 * f + 32 * k + 32]
        chosen.append(jnp.sum(jnp.where(high > 0, total, 0.0), axis=0, keepdims=True))
    chosen = jnp.concatenate(chosen + [jnp.zeros((3, 4 * CAP), f32)], axis=0)
    gone = lax.dot_general(high.astype(bf16), low, (((1,), (1,)), ((), ())), preferred_element_type=f32)
    kept[...] = fields[0] * (1.0 - gone)
    by_way = [chosen[:, CAP * d : CAP * d + CAP] for d in range(4)]
    odd_ax, odd_rad = parity("ax"), parity("rad")
    for axis, odd, (even_way, odd_way) in (("ax", odd_ax, (axial_a, axial_b)), ("rad", odd_rad, (radial_a, radial_b))):
        plus, minus = by_way[0:2] if axis == "ax" else by_way[2:4]
        base = 192 if axis == "ax" else 96
        even_way[base : base + 8, 0:CAP] = jnp.where(odd == 0, plus, minus)
        odd_way[base : base + 8, 0:CAP] = jnp.where(odd == 0, minus, plus)
    for copy in large:
        copy.wait()
    for message, last in ((axial_a, odd_ax == 0), (axial_b, odd_ax == 1)):
        near = pl.multiple_of(jnp.where(last, (CX - 1) * CY, 0), CY)
        far = pl.multiple_of(jnp.where(last, (CX - 2) * CY, CY), CY)
        for c in range(C):
            message[32 * c : 32 * c + 16, :] = gas[c, pl.ds(near, CY), :]
            message[32 * c + 16 : 32 * c + 32, :] = gas[c, pl.ds(far, CY), :]
    for message, last in ((radial_a, odd_rad == 0), (radial_b, odd_rad == 1)):
        near, far = jnp.where(last, CY - 1, 0), jnp.where(last, CY - 2, 1)
        for c in range(C):
            for i in range(CX):
                at = c * CX + i
                message[at : at + 1, :] = gas[c, pl.ds(i * CY + near, 1), :]
                message[48 + at : 49 + at, :] = gas[c, pl.ds(i * CY + far, 1), :]


def evaporate(mass, temp, axial, radial, samples):
    axial_gas, radial_gas, gas_temp, fuel = samples
    living = mass > 0.0
    safe_temp = jnp.where(living, temp, 1.0)
    root = jnp.where(living, jnp.exp(jnp.log(jnp.where(living, mass, 1.0)) * (1.0 / 3.0)), 0.0)
    balance = jnp.exp(-1.0 / safe_temp)
    slip = (axial_gas - axial) ** 2 + (radial_gas - radial) ** 2
    wind = jnp.sqrt(jnp.sqrt(1.0 + slip))
    evaporated = 0.1 * root * (jnp.log(1.0 - fuel) - jnp.log(1.0 - balance)) * (1.0 + 0.3 * wind)
    updated = (
        mass - evaporated,
        temp + 0.1 * (gas_temp - temp) - 0.5 * evaporated,
        axial + 0.2 * (axial_gas - axial),
        radial + 0.2 * (radial_gas - radial),
    )
    updated = tuple(jnp.where(living, u, 0.0) for u in updated)
    terms = (
        evaporated,
        evaporated * axial + 0.2 * mass * (axial - axial_gas),
        evaporated * radial + 0.2 * mass * (radial - radial_gas),
        evaporated * temp + 0.1 * mass * (temp - gas_temp),
    )
    return updated, terms


def one_hot(index, size):
    width = index.shape[1]
    return (lax.broadcasted_iota(jnp.int32, (size, width), 0) == index).astype(f32).astype(bf16)


def gather_block(table, where):
    around = one_hot(where & (CZ - 1), CZ)
    got = jnp.dot(table[...], around, preferred_element_type=f32)
    mask = lax.broadcasted_iota(jnp.int32, (ROWS, where.shape[1]), 0) == (where >> 9)
    samples = []
    for k in range(4):
        both = got[2 * ROWS * k : 2 * ROWS * k + ROWS] + got[2 * ROWS * k + ROWS : 2 * ROWS * k + 2 * ROWS]
        samples.append(jnp.sum(jnp.where(mask, both, 0.0), axis=0, keepdims=True))
    return samples


def deposit_block(terms, where):
    around = one_hot(where & (CZ - 1), CZ)
    mask = lax.broadcasted_iota(jnp.int32, (ROWS, where.shape[1]), 0) == (where >> 9)
    halves = [split2(t) for t in terms]
    spread = jnp.concatenate(
        [
            jnp.concatenate([jnp.where(mask, h[side].astype(f32), 0.0).astype(bf16) for h in halves], axis=0)
            for side in range(2)
        ],
        axis=1,
    )
    twice = jnp.concatenate([around, around], axis=1)
    return lax.dot_general(spread, twice, (((1,), (1,)), ((), ())), preferred_element_type=f32)


def row_of(ref, lead, first, count):
    return jnp.concatenate([ref[lead, s : s + 1, :] for s in range(first, first + count)], axis=1)


def early_kernel(gas, viscosity, drops, cells, kept, axial_b, radial_a, late, *refs):
    @pl.when(is_early())
    def _():
        late[...] = axial_b[...]

        @pl.when(lax.axis_index("ax") == 0)
        def _():
            late[0:104, :] = radial_a[0:104, :]

        main_kernel(gas, viscosity, drops, cells, kept, *refs)


def late_kernel(gas, viscosity, drops, cells, kept, out_in, drops_in, table_in, *refs):
    pl.when(jnp.logical_not(is_early()))(lambda: main_kernel(gas, viscosity, drops, cells, kept, *refs))


def main_kernel(gas, viscosity, drops, cells, kept, out, drops_out, table, speed, samples, terms, source):
    inverse = 1.0 / gas[0]
    for k, c in enumerate((1, 2, 4, 5)):
        quotient = gas[c] * inverse
        if k < 2:
            speed[k] = quotient
        hi, lo = split2(quotient)
        table[2 * ROWS * k : 2 * ROWS * k + ROWS, :] = hi
        table[2 * ROWS * k + ROWS : 2 * ROWS * k + 2 * ROWS, :] = lo
    speed[2] = gas[3] * inverse

    for b in range(8):
        where = jnp.concatenate([cells[s : s + 1, :] for s in range(4 * b, 4 * b + 4)], axis=1)
        got = gather_block(table, where)
        for k in range(4):
            for s in range(4):
                samples[k, 4 * b + s : 4 * b + s + 1, :] = got[k][:, 128 * s : 128 * s + 128]
    fields = [
        jnp.concatenate([drops[f : f + 1, 128 * s : 128 * s + 128] for s in range(32)], axis=0) for f in range(1, 4)
    ]
    updated, new_terms = evaporate(kept[...], *fields, [samples[k] for k in range(4)])
    for f in range(4):
        terms[f] = new_terms[f]
        for s in range(32):
            drops_out[f : f + 1, 128 * s : 128 * s + 128] = updated[f][s : s + 1, :]
    for b in range(8):
        where = jnp.concatenate([cells[s : s + 1, :] for s in range(4 * b, 4 * b + 4)], axis=1)
        part = deposit_block([row_of(terms, k, 4 * b, 4) for k in range(4)], where)
        if b == 0:
            source[...] = part
        else:
            source[...] += part

    lane = lax.broadcasted_iota(jnp.int32, (CY, CZ), 0)

    def component(c, carry):
        slot = jnp.where(c < 3, c, jnp.where(c == 5, 0, c - 1))
        scale = jnp.where(c == 3, 0.0, 1.0)
        layers = [gas[c, CY * i : CY * i + CY, :] for i in range(CX)]
        for i in range(CX):
            rows = slice(CY * i, CY * i + CY)
            x = layers[i]
            zero = jnp.zeros_like(x)
            ax = [layers[i + k] if 0 <= i + k < CX else zero for k in (-2, -1, 1, 2)]
            ra = []
            for k in (-2, -1, 1, 2):
                moved = pltpu.roll(x, (-k) % CY, axis=0)
                ok = (lane + k >= 0) & (lane + k < CY)
                ra.append(jnp.where(ok, moved, 0.0))
            az = [pltpu.roll(x, (-k) % CZ, axis=1) for k in (-2, -1, 1, 2)]
            near = (ax[1] + ax[2]) + (ra[1] + ra[2]) + (az[1] + az[2])
            far = (ax[0] + ax[3]) + (ra[0] + ra[3]) + (az[0] + az[3])
            laplace = (16.0 * near - far - 90.0 * x) * (1.0 / 12.0)
            transport = zero
            for j, n in enumerate((ax, ra, az)):
                slope = (8.0 * (n[2] - n[1]) - (n[3] - n[0])) * (1.0 / 12.0)
                transport = transport + speed[j, rows, :] * slope
            advanced = x + time_step * (viscosity[rows, :] * laplace - transport)
            out[c, rows, :] = advanced + scale * source[pl.ds(pl.multiple_of(slot * ROWS + CY * i, CY), CY), :]
        return carry

    lax.fori_loop(0, C, component, 0)


def final_kernel(
    part, updated_in, gas, viscosity, table, axial_a, axial_b, radial_a_in, radial_b, late,
    out, drops_out, arrivals_out, radial_a,
):
    odd_ax, odd_rad = parity("ax"), parity("rad")
    from_late = lax.rem(lax.axis_index("ax"), WRAP) == WRAP - 1
    corner = (lax.axis_index("ax") == 0) & (lax.axis_index("rad") == 0)
    drops_out[...] = updated_in[...]
    radial_a[...] = jnp.where(corner, late[0:104, :], radial_a_in[0:104, :])
    got = []
    for odd, a, b in ((odd_ax, axial_a, axial_b), (odd_rad, radial_a, radial_b)):
        base = 192 if a is axial_a else 96
        in_a, in_b = a[base : base + 8, 0:CAP], b[base : base + 8, 0:CAP]
        if b is axial_b:
            in_b = jnp.where(from_late, late[base : base + 8, 0:CAP], in_b)
        got.append(jnp.where(odd == 1, in_a, in_b))
        got.append(jnp.where(odd == 1, in_b, in_a))
    got = jnp.concatenate(got, axis=1)
    where = got[4:5].astype(jnp.int32)
    samples = gather_block(table, where)
    updated, terms = evaporate(got[0:1], got[1:2], got[2:3], got[3:4], samples)
    arrivals_out[...] = jnp.concatenate(updated, axis=0)
    source = deposit_block(terms, where)
    lane = lax.broadcasted_iota(jnp.int32, (CY, CZ), 0)
    for i in range(CX):
        rows = slice(CY * i, CY * i + CY)
        factor = viscosity[rows, :] * (time_step / 12.0)
        radial = gas[2, rows, :] / gas[0, rows, :] * (time_step / 12.0)
        weights = []
        for last in (odd_rad == 0, odd_rad == 1):
            speed = jnp.where(last, -1.0, 1.0) * radial
            first, second = jnp.where(last, CY - 1, 0), jnp.where(last, CY - 2, 1)
            near, far = 16.0 * factor + 8.0 * speed, -(factor + speed)
            weights.append((jnp.where(lane == first, near, jnp.where(lane == second, far, 0.0)), jnp.where(lane == first, far, 0.0)))
        for c in range(C):
            at = c * CX + i
            value = part[c, rows, :]
            for (near, far), message in zip(weights, (radial_a, radial_b)):
                value = value + near * message[at : at + 1, :] + far * message[48 + at : 49 + at, :]
            slot = (0, 1, 2, None, 3, 0)[c]
            if slot is not None:
                value = value + source[slot * ROWS + CY * i : slot * ROWS + CY * i + CY, :]
            out[c, rows, :] = value

    def correct(message, last):
        sign = jnp.where(last, -1.0, 1.0)
        for k in range(2):
            rows = pl.ds(pl.multiple_of(jnp.where(last, (CX - 1 - k) * CY, k * CY), CY), CY)
            factor = viscosity[rows, :] * (time_step / 12.0)
            speed = sign * (gas[1, rows, :] / gas[0, rows, :] * (time_step / 12.0))
            near, far = 16.0 * factor + 8.0 * speed, -(factor + speed)
            for c in range(C):
                if k == 0:
                    out[c, rows, :] += near * message[32 * c : 32 * c + CY, :] + far * message[32 * c + CY : 32 * c + 2 * CY, :]
                else:
                    out[c, rows, :] += far * message[32 * c : 32 * c + CY, :]

    correct(axial_a, odd_ax == 0)
    pl.when(jnp.logical_not(from_late))(lambda: correct(axial_b, odd_ax == 1))
    pl.when(from_late)(lambda: correct(late, odd_ax == 1))


def routes(n_ax, n_rad):
    flat = lambda a, r: a * n_rad + r
    axial_a, axial_b, radial_a, radial_b, late = [], [], [], [], []
    for a in range(n_ax):
        for r in range(n_rad):
            if a + 1 < n_ax:
                up = (flat(a, r), flat(a + 1, r))
                (axial_a if a % 2 == 0 else axial_b).append(up)
                down = late if (a + 1) % WRAP == 0 else axial_a if a % 2 == 0 else axial_b
                down.append(up[::-1])
            if r + 1 < n_rad:
                out = (flat(a, r), flat(a, r + 1))
                (radial_a if r % 2 == 0 else radial_b).append(out)
                back = late if a == 0 and r == 0 else radial_a if r % 2 == 0 else radial_b
                back.append(out[::-1])
    return axial_a, axial_b, radial_a, radial_b, late


def body(gas_state, viscosity, droplets, drop_cells, move_lists, move_counts):
    gas = gas_state.reshape(C, ROWS, CZ)
    thick = viscosity.reshape(ROWS, CZ)
    cells = drop_cells.reshape(32, 128)
    shape = jax.ShapeDtypeStruct
    axial_b, axial_a, radial_b, radial_a, kept, gas, drops, cells = pl.pallas_call(
        prep_kernel,
        out_shape=(
            shape((200, CZ), f32),
            shape((200, CZ), f32),
            shape((200, CZ), f32),
            shape((200, CZ), f32),
            shape((32, 128), f32),
            shape((C, ROWS, CZ), f32),
            shape((4, SLOTS), f32),
            shape((32, 128), jnp.int32),
        ),
        in_specs=[HB] * 5,
        out_specs=(VM,) * 8,
        scratch_shapes=[
            pltpu.VMEM((1, 4, CAP), jnp.int32),
            pltpu.SMEM((1, 4), jnp.int32),
            pltpu.SemaphoreType.DMA((10,)),
        ],
        compiler_params=params,
        name="prep",
    )(*(pltpu.with_memory_space_constraint(x, pltpu.HBM) for x in (gas, droplets, cells, move_lists, move_counts)))
    both = ("ax", "rad")
    to_a, to_b, to_c, to_d, to_late = routes(lax.axis_size("ax"), lax.axis_size("rad"))
    came_b = lax.ppermute(axial_b, both, to_b)
    came_a = lax.ppermute(axial_a, both, to_a)
    came_d = lax.ppermute(radial_b, both, to_d)
    came_c = lax.ppermute(radial_a, both, to_c)

    results = (shape((C, ROWS, CZ), f32), shape((4, SLOTS), f32), shape((8 * ROWS, CZ), bf16))
    scratch = [
        pltpu.VMEM((3, ROWS, CZ), f32),
        pltpu.VMEM((4, 32, 128), f32),
        pltpu.VMEM((4, 32, 128), f32),
        pltpu.VMEM((4 * ROWS, CZ), f32),
    ]
    late, *first = pl.pallas_call(
        early_kernel,
        out_shape=(shape((200, CZ), f32), *results),
        in_specs=[VM] * 7,
        out_specs=(VM,) * 4,
        scratch_shapes=scratch,
        compiler_params=params,
        cost_estimate=pl.CostEstimate(flops=40000000000, bytes_accessed=6_000_000, transcendentals=0),
        name="early",
    )(gas, thick, drops, cells, kept, axial_b, radial_a)
    came_late = lax.ppermute(late, both, to_late)
    part, updated, table = pl.pallas_call(
        late_kernel,
        out_shape=results,
        in_specs=[VM] * 8,
        out_specs=(VM,) * 3,
        scratch_shapes=scratch,
        compiler_params=params,
        input_output_aliases={5: 0, 6: 1, 7: 2},
        cost_estimate=pl.CostEstimate(flops=0, bytes_accessed=0, transcendentals=0),
        name="late",
    )(gas, thick, drops, cells, kept, *first)
    out, drops_out, arrivals_out = pl.pallas_call(
        final_kernel,
        out_shape=(shape((C, ROWS, CZ), f32), shape((4, SLOTS), f32), shape((4, 4 * CAP), f32)),
        in_specs=[VM] * 10,
        out_specs=(VM,) * 3,
        scratch_shapes=[pltpu.VMEM((104, CZ), f32)],
        compiler_params=params,
        name="final",
    )(part, updated, gas, thick, table, came_a, came_b, came_c, came_d, came_late)
    return out.reshape(gas_state.shape), drops_out, arrivals_out


def solution(mesh):
    placed = (
        P(None, "ax", "rad", None),
        P("ax", "rad", None),
        P(None, ("ax", "rad")),
        P(("ax", "rad")),
        P(("ax", "rad"), None, None),
        P(("ax", "rad"), None),
    )
    return jax.shard_map(
        body,
        mesh=mesh,
        in_specs=placed,
        out_specs=(P(None, "ax", "rad", None), P(None, ("ax", "rad")), P(None, ("ax", "rad"))),
        check_vma=False,
    )
```

```python
import functools

import jax
import jax.numpy as jnp
from jax import lax
from jax.experimental import pallas as pl
from jax.experimental.pallas import tpu as pltpu
from jax.sharding import PartitionSpec as P

time_step = 0.2
f32 = jnp.float32
bf16 = jnp.bfloat16
VM = pl.BlockSpec(memory_space=pltpu.VMEM)
HB = pl.BlockSpec(memory_space=pltpu.HBM)
C, CX, CY, CZ = 6, 8, 16, 512
ROWS = CX * CY
SLOTS, CAP = 4096, 64
params = pltpu.CompilerParams(vmem_limit_bytes=30 << 20)


def split2(x):
    hi = x.astype(bf16)
    return hi, (x - hi.astype(f32)).astype(bf16)


def split3(x):
    hi = x.astype(bf16)
    rest = x - hi.astype(f32)
    mid = rest.astype(bf16)
    return hi, mid, (rest - mid.astype(f32)).astype(bf16)


WRAP = 16


def parity(axis):
    return lax.rem(lax.axis_index(axis), 2)


def is_early():
    a, r = lax.axis_index("ax"), lax.axis_index("rad")
    return ((a > 0) & (lax.rem(a, WRAP) == 0)) | ((a == 0) & (r == 1))


def prep_kernel(
    gas_in, drops_in, cells_in, lists_in, counts_in,
    axial_b, axial_a, radial_b, radial_a, kept, gas, drops, cells, lists, counts, sems,
):
    small = [
        pltpu.make_async_copy(source, target, sems.at[n])
        for n, (source, target) in enumerate(
            ((drops_in, drops), (cells_in, cells), (lists_in, lists), (counts_in, counts))
        )
    ]
    large = [pltpu.make_async_copy(gas_in.at[c], gas.at[c], sems.at[4 + c]) for c in range(C)]
    for copy in small + large:
        copy.start()
    for copy in small:
        copy.wait()
    slots = lists[0]
    entry = jnp.concatenate([slots[d : d + 1, :] for d in range(4)], axis=1)
    lane = lax.broadcasted_iota(jnp.int32, (1, CAP), 1)
    used = jnp.concatenate([(lane < counts[0, d]).astype(jnp.int32) for d in range(4)], axis=1)
    low = (lax.broadcasted_iota(jnp.int32, (128, 4 * CAP), 0) == (entry & 127)).astype(f32).astype(bf16)
    place = jnp.where(used > 0, entry >> 7, -1)
    high = (lax.broadcasted_iota(jnp.int32, (32, 4 * CAP), 0) == place).astype(f32)
    fields = []
    for f in range(4):
        fields.append(jnp.concatenate([drops[f : f + 1, 128 * s : 128 * s + 128] for s in range(32)], axis=0))
    parts = []
    for f in range(4):
        parts.extend(split3(fields[f]))
    parts.extend(split2(cells[...].astype(f32)))
    picked = jnp.dot(jnp.concatenate(parts, axis=0), low, preferred_element_type=f32)
    chosen = []
    for f in range(5):
        count = 3 if f < 4 else 2
        total = picked[96 * f : 96 * f + 32]
        for k in range(1, count):
            total = total + picked[96 * f + 32 * k : 96 * f + 32 * k + 32]
        chosen.append(jnp.sum(jnp.where(high > 0, total, 0.0), axis=0, keepdims=True))
    chosen = jnp.concatenate(chosen + [jnp.zeros((3, 4 * CAP), f32)], axis=0)
    gone = lax.dot_general(high.astype(bf16), low, (((1,), (1,)), ((), ())), preferred_element_type=f32)
    kept[...] = fields[0] * (1.0 - gone)
    by_way = [chosen[:, CAP * d : CAP * d + CAP] for d in range(4)]
    odd_ax, odd_rad = parity("ax"), parity("rad")
    for axis, odd, (even_way, odd_way) in (("ax", odd_ax, (axial_a, axial_b)), ("rad", odd_rad, (radial_a, radial_b))):
        plus, minus = by_way[0:2] if axis == "ax" else by_way[2:4]
        base = 192 if axis == "ax" else 96
        even_way[base : base + 8, 0:CAP] = jnp.where(odd == 0, plus, minus)
        odd_way[base : base + 8, 0:CAP] = jnp.where(odd == 0, minus, plus)
    for copy in large:
        copy.wait()
    for message, last in ((axial_a, odd_ax == 0), (axial_b, odd_ax == 1)):
        near = pl.multiple_of(jnp.where(last, (CX - 1) * CY, 0), CY)
        far = pl.multiple_of(jnp.where(last, (CX - 2) * CY, CY), CY)
        for c in range(C):
            message[32 * c : 32 * c + 16, :] = gas[c, pl.ds(near, CY), :]
            message[32 * c + 16 : 32 * c + 32, :] = gas[c, pl.ds(far, CY), :]
    for message, last in ((radial_a, odd_rad == 0), (radial_b, odd_rad == 1)):
        near, far = jnp.where(last, CY - 1, 0), jnp.where(last, CY - 2, 1)
        for c in range(C):
            for i in range(CX):
                at = c * CX + i
                message[at : at + 1, :] = gas[c, pl.ds(i * CY + near, 1), :]
                message[48 + at : 49 + at, :] = gas[c, pl.ds(i * CY + far, 1), :]


def evaporate(mass, temp, axial, radial, samples):
    axial_gas, radial_gas, gas_temp, fuel = samples
    living = mass > 0.0
    safe_temp = jnp.where(living, temp, 1.0)
    root = jnp.where(living, jnp.exp(jnp.log(jnp.where(living, mass, 1.0)) * (1.0 / 3.0)), 0.0)
    balance = jnp.exp(-1.0 / safe_temp)
    slip = (axial_gas - axial) ** 2 + (radial_gas - radial) ** 2
    wind = jnp.sqrt(jnp.sqrt(1.0 + slip))
    evaporated = 0.1 * root * (jnp.log(1.0 - fuel) - jnp.log(1.0 - balance)) * (1.0 + 0.3 * wind)
    updated = (
        mass - evaporated,
        temp + 0.1 * (gas_temp - temp) - 0.5 * evaporated,
        axial + 0.2 * (axial_gas - axial),
        radial + 0.2 * (radial_gas - radial),
    )
    updated = tuple(jnp.where(living, u, 0.0) for u in updated)
    terms = (
        evaporated,
        evaporated * axial + 0.2 * mass * (axial - axial_gas),
        evaporated * radial + 0.2 * mass * (radial - radial_gas),
        evaporated * temp + 0.1 * mass * (temp - gas_temp),
    )
    return updated, terms


def one_hot(index, size):
    width = index.shape[1]
    return (lax.broadcasted_iota(jnp.int32, (size, width), 0) == index).astype(f32).astype(bf16)


def gather_block(table, where):
    around = one_hot(where & (CZ - 1), CZ)
    got = jnp.dot(table[...], around, preferred_element_type=f32)
    mask = lax.broadcasted_iota(jnp.int32, (ROWS, where.shape[1]), 0) == (where >> 9)
    samples = []
    for k in range(4):
        both = got[2 * ROWS * k : 2 * ROWS * k + ROWS] + got[2 * ROWS * k + ROWS : 2 * ROWS * k + 2 * ROWS]
        samples.append(jnp.sum(jnp.where(mask, both, 0.0), axis=0, keepdims=True))
    return samples


def deposit_block(terms, where):
    around = one_hot(where & (CZ - 1), CZ)
    mask = lax.broadcasted_iota(jnp.int32, (ROWS, where.shape[1]), 0) == (where >> 9)
    halves = [split2(t) for t in terms]
    spread = jnp.concatenate(
        [
            jnp.concatenate([jnp.where(mask, h[side].astype(f32), 0.0).astype(bf16) for h in halves], axis=0)
            for side in range(2)
        ],
        axis=1,
    )
    twice = jnp.concatenate([around, around], axis=1)
    return lax.dot_general(spread, twice, (((1,), (1,)), ((), ())), preferred_element_type=f32)


def early_kernel(gas, viscosity, drops, cells, kept, axial_b, radial_a, late, *refs):
    @pl.when(is_early())
    def _():
        late[...] = axial_b[...]

        @pl.when(lax.axis_index("ax") == 0)
        def _():
            late[0:104, :] = radial_a[0:104, :]

        main_kernel(gas, viscosity, drops, cells, kept, *refs)


def late_kernel(gas, viscosity, drops, cells, kept, out_in, drops_in, table_in, *refs):
    pl.when(jnp.logical_not(is_early()))(lambda: main_kernel(gas, viscosity, drops, cells, kept, *refs))


def main_kernel(gas, viscosity, drops, cells, kept, out, drops_out, table, speed, samples, terms, source):
    inverse = 1.0 / gas[0]
    for k, c in enumerate((1, 2, 4, 5)):
        quotient = gas[c] * inverse
        if k < 2:
            speed[k] = quotient
        hi, lo = split2(quotient)
        table[2 * ROWS * k : 2 * ROWS * k + ROWS, :] = hi
        table[2 * ROWS * k + ROWS : 2 * ROWS * k + 2 * ROWS, :] = lo
    speed[2] = gas[3] * inverse

    slot = lax.broadcasted_iota(jnp.int32, (1, SLOTS), 1)
    filled = jnp.max(jnp.where(drops[0:1, :] > 0.0, slot + 1, 0))
    blocks = lax.div(filled + 511, 512)

    def sample(b, carry):
        first = pl.multiple_of(4 * b, 4)
        where = jnp.concatenate([cells[pl.ds(first + s, 1), :] for s in range(4)], axis=1)
        got = gather_block(table, where)
        for k in range(4):
            for s in range(4):
                samples[k, pl.ds(first + s, 1), :] = got[k][:, 128 * s : 128 * s + 128]
        return carry

    lax.fori_loop(0, blocks, sample, 0)
    fields = [
        jnp.concatenate([drops[f : f + 1, 128 * s : 128 * s + 128] for s in range(32)], axis=0) for f in range(1, 4)
    ]
    updated, new_terms = evaporate(kept[...], *fields, [samples[k] for k in range(4)])
    for f in range(4):
        terms[f] = new_terms[f]
        for s in range(32):
            drops_out[f : f + 1, 128 * s : 128 * s + 128] = updated[f][s : s + 1, :]
    source[...] = jnp.zeros_like(source)

    def deposit(b, carry):
        first = pl.multiple_of(4 * b, 4)
        row = lambda load: jnp.concatenate([load(pl.ds(first + s, 1)) for s in range(4)], axis=1)
        where = row(lambda at: cells[at, :])
        source[...] += deposit_block([row(lambda at: terms[k, at, :]) for k in range(4)], where)
        return carry

    lax.fori_loop(0, blocks, deposit, 0)
    lane = lax.broadcasted_iota(jnp.int32, (CY, CZ), 0)

    def component(c, carry):
        slot = jnp.where(c < 3, c, jnp.where(c == 5, 0, c - 1))
        scale = jnp.where(c == 3, 0.0, 1.0)
        layers = [gas[c, CY * i : CY * i + CY, :] for i in range(CX)]
        for i in range(CX):
            rows = slice(CY * i, CY * i + CY)
            x = layers[i]
            zero = jnp.zeros_like(x)
            ax = [layers[i + k] if 0 <= i + k < CX else zero for k in (-2, -1, 1, 2)]
            ra = []
            for k in (-2, -1, 1, 2):
                moved = pltpu.roll(x, (-k) % CY, axis=0)
                ok = (lane + k >= 0) & (lane + k < CY)
                ra.append(jnp.where(ok, moved, 0.0))
            az = [pltpu.roll(x, (-k) % CZ, axis=1) for k in (-2, -1, 1, 2)]
            near = (ax[1] + ax[2]) + (ra[1] + ra[2]) + (az[1] + az[2])
            far = (ax[0] + ax[3]) + (ra[0] + ra[3]) + (az[0] + az[3])
            laplace = (16.0 * near - far - 90.0 * x) * (1.0 / 12.0)
            transport = zero
            for j, n in enumerate((ax, ra, az)):
                slope = (8.0 * (n[2] - n[1]) - (n[3] - n[0])) * (1.0 / 12.0)
                transport = transport + speed[j, rows, :] * slope
            advanced = x + time_step * (viscosity[rows, :] * laplace - transport)
            out[c, rows, :] = advanced + scale * source[pl.ds(pl.multiple_of(slot * ROWS + CY * i, CY), CY), :]
        return carry

    lax.fori_loop(0, C, component, 0)


def is_last():
    a, r = lax.axis_index("ax"), lax.axis_index("rad")
    return ((lax.rem(a, WRAP) == WRAP - 1) & (a < lax.axis_size("ax") - 1)) | ((a == 0) & (r == 0))


def soon_kernel(*refs):
    pl.when(jnp.logical_not(is_last()))(lambda: final_kernel(None, *refs))


def last_kernel(late, part, updated, gas, viscosity, table, axial_a, axial_b, radial_a, radial_b, *refs):
    given = (part, updated, gas, viscosity, table, axial_a, axial_b, radial_a, radial_b)
    pl.when(is_last())(lambda: final_kernel(late, *given, *refs[3:]))


def final_kernel(
    late, part, updated_in, gas, viscosity, table, axial_a, axial_b_in, radial_a_in, radial_b,
    out_hbm, drops_hbm, arrivals_hbm, out, arrivals, axial_b, radial_a, weights, sems,
):
    copies = [
        pltpu.make_async_copy(updated_in, drops_hbm, sems.at[0]),
        pltpu.make_async_copy(arrivals, arrivals_hbm, sems.at[1]),
    ] + [pltpu.make_async_copy(out.at[c], out_hbm.at[c], sems.at[2 + c]) for c in range(C)]
    copies[0].start()
    odd_ax, odd_rad = parity("ax"), parity("rad")
    if late is None:
        axial_b, radial_a = axial_b_in, radial_a_in
    else:
        corner = lax.axis_index("ax") == 0
        axial_b[...] = jnp.where(corner, axial_b_in[...], late[...])
        radial_a[0:104, :] = jnp.where(corner, late[0:104, :], radial_a_in[0:104, :])
    got = []
    for odd, a, b, base in ((odd_ax, axial_a, axial_b, 192), (odd_rad, radial_a, radial_b, 96)):
        in_a, in_b = a[base : base + 8, 0:CAP], b[base : base + 8, 0:CAP]
        got.append(jnp.where(odd == 1, in_a, in_b))
        got.append(jnp.where(odd == 1, in_b, in_a))
    got = jnp.concatenate(got, axis=1)
    where = got[4:5].astype(jnp.int32)
    samples = gather_block(table, where)
    changed, terms = evaporate(got[0:1], got[1:2], got[2:3], got[3:4], samples)
    arrivals[...] = jnp.concatenate(changed, axis=0)
    copies[1].start()
    source = deposit_block(terms, where)
    lane = lax.broadcasted_iota(jnp.int32, (CY, CZ), 0)
    for i in range(CX):
        rows = slice(CY * i, CY * i + CY)
        factor = viscosity[rows, :] * (time_step / 12.0)
        radial = gas[2, rows, :] / gas[0, rows, :] * (time_step / 12.0)
        for n, last in enumerate((odd_rad == 0, odd_rad == 1)):
            speed = jnp.where(last, -1.0, 1.0) * radial
            first, second = jnp.where(last, CY - 1, 0), jnp.where(last, CY - 2, 1)
            near, far = 16.0 * factor + 8.0 * speed, -(factor + speed)
            weights[2 * n, rows, :] = jnp.where(lane == first, near, jnp.where(lane == second, far, 0.0))
            weights[2 * n + 1, rows, :] = jnp.where(lane == first, far, 0.0)
    edges = []
    for message, last in ((axial_a, odd_ax == 0), (axial_b, odd_ax == 1)):
        sign = jnp.where(last, -1.0, 1.0)
        for k in range(2):
            rows = pl.ds(pl.multiple_of(jnp.where(last, (CX - 1 - k) * CY, k * CY), CY), CY)
            edges.append((message, k, rows, sign))
    for c in range(C):
        for i in range(CX):
            rows = slice(CY * i, CY * i + CY)
            at = c * CX + i
            value = part[c, rows, :]
            for n, message in enumerate((radial_a, radial_b)):
                value = value + weights[2 * n, rows, :] * message[at : at + 1, :]
                value = value + weights[2 * n + 1, rows, :] * message[48 + at : 49 + at, :]
            slot = (0, 1, 2, None, 3, 0)[c]
            if slot is not None:
                value = value + source[slot * ROWS + CY * i : slot * ROWS + CY * i + CY, :]
            out[c, rows, :] = value
        for message, k, rows, sign in edges:
            factor = viscosity[rows, :] * (time_step / 12.0)
            speed = sign * (gas[1, rows, :] / gas[0, rows, :] * (time_step / 12.0))
            near, far = 16.0 * factor + 8.0 * speed, -(factor + speed)
            if k == 0:
                change = near * message[32 * c : 32 * c + CY, :] + far * message[32 * c + CY : 32 * c + 2 * CY, :]
            else:
                change = far * message[32 * c : 32 * c + CY, :]
            out[c, rows, :] += change
        copies[2 + c].start()
    for copy in copies:
        copy.wait()


def routes(n_ax, n_rad):
    flat = lambda a, r: a * n_rad + r
    axial_a, axial_b, radial_a, radial_b, late = [], [], [], [], []
    for a in range(n_ax):
        for r in range(n_rad):
            if a + 1 < n_ax:
                up = (flat(a, r), flat(a + 1, r))
                (axial_a if a % 2 == 0 else axial_b).append(up)
                down = late if (a + 1) % WRAP == 0 else axial_a if a % 2 == 0 else axial_b
                down.append(up[::-1])
            if r + 1 < n_rad:
                out = (flat(a, r), flat(a, r + 1))
                (radial_a if r % 2 == 0 else radial_b).append(out)
                back = late if a == 0 and r == 0 else radial_a if r % 2 == 0 else radial_b
                back.append(out[::-1])
    return axial_a, axial_b, radial_a, radial_b, late


def body(gas_state, viscosity, droplets, drop_cells, move_lists, move_counts):
    gas = gas_state.reshape(C, ROWS, CZ)
    thick = viscosity.reshape(ROWS, CZ)
    cells = drop_cells.reshape(32, 128)
    shape = jax.ShapeDtypeStruct
    axial_b, axial_a, radial_b, radial_a, kept, gas, drops, cells = pl.pallas_call(
        prep_kernel,
        out_shape=(
            shape((200, CZ), f32),
            shape((200, CZ), f32),
            shape((104, CZ), f32),
            shape((104, CZ), f32),
            shape((32, 128), f32),
            shape((C, ROWS, CZ), f32),
            shape((4, SLOTS), f32),
            shape((32, 128), jnp.int32),
        ),
        in_specs=[HB] * 5,
        out_specs=(VM,) * 8,
        scratch_shapes=[
            pltpu.VMEM((1, 4, CAP), jnp.int32),
            pltpu.SMEM((1, 4), jnp.int32),
            pltpu.SemaphoreType.DMA((10,)),
        ],
        compiler_params=params,
        name="prep",
    )(*(pltpu.with_memory_space_constraint(x, pltpu.HBM) for x in (gas, droplets, cells, move_lists, move_counts)))
    both = ("ax", "rad")
    to_a, to_b, to_c, to_d, to_late = routes(lax.axis_size("ax"), lax.axis_size("rad"))
    came_b = lax.ppermute(axial_b, both, to_b)
    came_a = lax.ppermute(axial_a, both, to_a)
    came_d = lax.ppermute(radial_b, both, to_d)
    came_c = lax.ppermute(radial_a, both, to_c)

    results = (shape((C, ROWS, CZ), f32), shape((4, SLOTS), f32), shape((8 * ROWS, CZ), bf16))
    scratch = [
        pltpu.VMEM((3, ROWS, CZ), f32),
        pltpu.VMEM((4, 32, 128), f32),
        pltpu.VMEM((4, 32, 128), f32),
        pltpu.VMEM((4 * ROWS, CZ), f32),
    ]
    late, *first = pl.pallas_call(
        early_kernel,
        out_shape=(shape((200, CZ), f32), *results),
        in_specs=[VM] * 7,
        out_specs=(VM,) * 4,
        scratch_shapes=scratch,
        compiler_params=params,
        cost_estimate=pl.CostEstimate(flops=40000000000, bytes_accessed=6_000_000, transcendentals=0),
        name="early",
    )(gas, thick, drops, cells, kept, axial_b, radial_a)
    came_late = lax.ppermute(late, both, to_late)
    part, updated, table = pl.pallas_call(
        late_kernel,
        out_shape=results,
        in_specs=[VM] * 8,
        out_specs=(VM,) * 3,
        scratch_shapes=scratch,
        compiler_params=params,
        input_output_aliases={5: 0, 6: 1, 7: 2},
        cost_estimate=pl.CostEstimate(flops=0, bytes_accessed=0, transcendentals=0),
        name="late",
    )(gas, thick, drops, cells, kept, *first)
    finals = (shape((C, ROWS, CZ), f32), shape((4, SLOTS), f32), shape((4, 4 * CAP), f32))
    scratch = [
        pltpu.VMEM((C, ROWS, CZ), f32),
        pltpu.VMEM((4, 4 * CAP), f32),
        pltpu.VMEM((200, CZ), f32),
        pltpu.VMEM((104, CZ), f32),
        pltpu.VMEM((4, ROWS, CZ), f32),
        pltpu.SemaphoreType.DMA((8,)),
    ]
    common = (part, updated, gas, thick, table, came_a, came_b, came_c, came_d)
    finals_soon = pl.pallas_call(
        soon_kernel,
        out_shape=finals,
        in_specs=[VM] * 9,
        out_specs=(HB,) * 3,
        scratch_shapes=scratch,
        compiler_params=params,
        cost_estimate=pl.CostEstimate(flops=4_000_000_000, bytes_accessed=3_000_000, transcendentals=0),
        name="soon",
    )(*common)
    out, drops_out, arrivals_out = pl.pallas_call(
        last_kernel,
        out_shape=finals,
        in_specs=[VM] * 10 + [HB] * 3,
        out_specs=(HB,) * 3,
        scratch_shapes=scratch,
        compiler_params=params,
        input_output_aliases={10: 0, 11: 1, 12: 2},
        cost_estimate=pl.CostEstimate(flops=0, bytes_accessed=0, transcendentals=0),
        name="last",
    )(came_late, *common, *finals_soon)
    return out.reshape(gas_state.shape), drops_out, arrivals_out


def solution(mesh):
    placed = (
        P(None, "ax", "rad", None),
        P("ax", "rad", None),
        P(None, ("ax", "rad")),
        P(("ax", "rad")),
        P(("ax", "rad"), None, None),
        P(("ax", "rad"), None),
    )
    return jax.shard_map(
        body,
        mesh=mesh,
        in_specs=placed,
        out_specs=(P(None, "ax", "rad", None), P(None, ("ax", "rad")), P(None, ("ax", "rad"))),
        check_vma=False,
    )
```

```python
import functools

import jax
import jax.numpy as jnp
from jax import lax
from jax.experimental import pallas as pl
from jax.experimental.pallas import tpu as pltpu
from jax.sharding import PartitionSpec as P

time_step = 0.2
f32 = jnp.float32
bf16 = jnp.bfloat16
VM = pl.BlockSpec(memory_space=pltpu.VMEM)
HB = pl.BlockSpec(memory_space=pltpu.HBM)
C, CX, CY, CZ = 6, 8, 16, 512
ROWS = CX * CY
SLOTS, CAP = 4096, 64
params = pltpu.CompilerParams(vmem_limit_bytes=30 << 20)


def split2(x):
    hi = x.astype(bf16)
    return hi, (x - hi.astype(f32)).astype(bf16)


def split3(x):
    hi = x.astype(bf16)
    rest = x - hi.astype(f32)
    mid = rest.astype(bf16)
    return hi, mid, (rest - mid.astype(f32)).astype(bf16)


WRAP = 16


def parity(axis):
    return lax.rem(lax.axis_index(axis), 2)


def is_early():
    a = lax.axis_index("ax")
    return (a > 0) & (lax.rem(a, WRAP) == 0)


def prep_kernel(
    gas_in, drops_in, cells_in, lists_in, counts_in,
    axial_b, axial_a, picks, kept, gas, drops, cells, lists, counts, sems,
):
    small = [
        pltpu.make_async_copy(source, target, sems.at[n])
        for n, (source, target) in enumerate(
            ((drops_in, drops), (cells_in, cells), (lists_in, lists), (counts_in, counts))
        )
    ]
    large = [pltpu.make_async_copy(gas_in.at[c], gas.at[c], sems.at[4 + c]) for c in range(C)]
    for copy in small + large:
        copy.start()
    for copy in small:
        copy.wait()
    slots = lists[0]
    entry = jnp.concatenate([slots[d : d + 1, :] for d in range(4)], axis=1)
    lane = lax.broadcasted_iota(jnp.int32, (1, CAP), 1)
    used = jnp.concatenate([(lane < counts[0, d]).astype(jnp.int32) for d in range(4)], axis=1)
    low = (lax.broadcasted_iota(jnp.int32, (128, 4 * CAP), 0) == (entry & 127)).astype(f32).astype(bf16)
    place = jnp.where(used > 0, entry >> 7, -1)
    high = (lax.broadcasted_iota(jnp.int32, (32, 4 * CAP), 0) == place).astype(f32)
    fields = []
    for f in range(4):
        fields.append(jnp.concatenate([drops[f : f + 1, 128 * s : 128 * s + 128] for s in range(32)], axis=0))
    parts = []
    for f in range(4):
        parts.extend(split3(fields[f]))
    parts.extend(split2(cells[...].astype(f32)))
    picked = jnp.dot(jnp.concatenate(parts, axis=0), low, preferred_element_type=f32)
    chosen = []
    for f in range(5):
        count = 3 if f < 4 else 2
        total = picked[96 * f : 96 * f + 32]
        for k in range(1, count):
            total = total + picked[96 * f + 32 * k : 96 * f + 32 * k + 32]
        chosen.append(jnp.sum(jnp.where(high > 0, total, 0.0), axis=0, keepdims=True))
    chosen = jnp.concatenate(chosen + [jnp.zeros((3, 4 * CAP), f32)], axis=0)
    gone = lax.dot_general(high.astype(bf16), low, (((1,), (1,)), ((), ())), preferred_element_type=f32)
    kept[...] = fields[0] * (1.0 - gone)
    picks[...] = chosen
    for copy in large:
        copy.wait()
    pack_axial(gas, picks, axial_b, parity("ax") == 1)
    pack_axial(gas, picks, axial_a, parity("ax") == 0)


def pick_way(picks, axis, last):
    first = 0 if axis == "ax" else 2 * CAP
    return jnp.where(last, picks[:, first : first + CAP], picks[:, first + CAP : first + 2 * CAP])


def pack_axial(gas, picks, message, last):
    near = pl.multiple_of(jnp.where(last, (CX - 1) * CY, 0), CY)
    far = pl.multiple_of(jnp.where(last, (CX - 2) * CY, CY), CY)
    for c in range(C):
        message[32 * c : 32 * c + 16, :] = gas[c, pl.ds(near, CY), :]
        message[32 * c + 16 : 32 * c + 32, :] = gas[c, pl.ds(far, CY), :]
    message[192:200, 0:CAP] = pick_way(picks, "ax", last)


def pack_radial(gas, picks, message, last):
    near, far = jnp.where(last, CY - 1, 0), jnp.where(last, CY - 2, 1)
    for c in range(C):
        for i in range(CX):
            at = c * CX + i
            message[at : at + 1, :] = gas[c, pl.ds(i * CY + near, 1), :]
            message[48 + at : 49 + at, :] = gas[c, pl.ds(i * CY + far, 1), :]
    message[96:104, 0:CAP] = pick_way(picks, "rad", last)


def evaporate(mass, temp, axial, radial, samples):
    axial_gas, radial_gas, gas_temp, fuel = samples
    living = mass > 0.0
    safe_temp = jnp.where(living, temp, 1.0)
    root = jnp.where(living, jnp.exp(jnp.log(jnp.where(living, mass, 1.0)) * (1.0 / 3.0)), 0.0)
    balance = jnp.exp(-1.0 / safe_temp)
    slip = (axial_gas - axial) ** 2 + (radial_gas - radial) ** 2
    wind = jnp.sqrt(jnp.sqrt(1.0 + slip))
    evaporated = 0.1 * root * (jnp.log(1.0 - fuel) - jnp.log(1.0 - balance)) * (1.0 + 0.3 * wind)
    updated = (
        mass - evaporated,
        temp + 0.1 * (gas_temp - temp) - 0.5 * evaporated,
        axial + 0.2 * (axial_gas - axial),
        radial + 0.2 * (radial_gas - radial),
    )
    updated = tuple(jnp.where(living, u, 0.0) for u in updated)
    terms = (
        evaporated,
        evaporated * axial + 0.2 * mass * (axial - axial_gas),
        evaporated * radial + 0.2 * mass * (radial - radial_gas),
        evaporated * temp + 0.1 * mass * (temp - gas_temp),
    )
    return updated, terms


def one_hot(index, size):
    width = index.shape[1]
    return (lax.broadcasted_iota(jnp.int32, (size, width), 0) == index).astype(f32).astype(bf16)


def gather_block(table, where):
    around = one_hot(where & (CZ - 1), CZ)
    got = jnp.dot(table[...], around, preferred_element_type=f32)
    mask = lax.broadcasted_iota(jnp.int32, (ROWS, where.shape[1]), 0) == (where >> 9)
    samples = []
    for k in range(4):
        both = got[2 * ROWS * k : 2 * ROWS * k + ROWS] + got[2 * ROWS * k + ROWS : 2 * ROWS * k + 2 * ROWS]
        samples.append(jnp.sum(jnp.where(mask, both, 0.0), axis=0, keepdims=True))
    return samples


def deposit_block(terms, where):
    around = one_hot(where & (CZ - 1), CZ)
    mask = lax.broadcasted_iota(jnp.int32, (ROWS, where.shape[1]), 0) == (where >> 9)
    halves = [split2(t) for t in terms]
    spread = jnp.concatenate(
        [
            jnp.concatenate([jnp.where(mask, h[side].astype(f32), 0.0).astype(bf16) for h in halves], axis=0)
            for side in range(2)
        ],
        axis=1,
    )
    twice = jnp.concatenate([around, around], axis=1)
    return lax.dot_general(spread, twice, (((1,), (1,)), ((), ())), preferred_element_type=f32)


def early_kernel(gas, viscosity, drops, cells, kept, picks, axial_b, late, radial_a, radial_b, *refs):
    pack_radial(gas, picks, radial_a, parity("rad") == 0)
    pack_radial(gas, picks, radial_b, parity("rad") == 1)

    @pl.when(is_early())
    def _():
        late[...] = axial_b[...]
        main_kernel(gas, viscosity, drops, cells, kept, *refs)


def late_kernel(gas, viscosity, drops, cells, kept, out_in, drops_in, table_in, *refs):
    pl.when(jnp.logical_not(is_early()))(lambda: main_kernel(gas, viscosity, drops, cells, kept, *refs))


def main_kernel(gas, viscosity, drops, cells, kept, out, drops_out, table, speed, samples, terms, source):
    inverse = 1.0 / gas[0]
    for k, c in enumerate((1, 2, 4, 5)):
        quotient = gas[c] * inverse
        if k < 2:
            speed[k] = quotient
        hi, lo = split2(quotient)
        table[2 * ROWS * k : 2 * ROWS * k + ROWS, :] = hi
        table[2 * ROWS * k + ROWS : 2 * ROWS * k + 2 * ROWS, :] = lo
    speed[2] = gas[3] * inverse

    slot = lax.broadcasted_iota(jnp.int32, (1, SLOTS), 1)
    filled = jnp.max(jnp.where(drops[0:1, :] > 0.0, slot + 1, 0))
    blocks = lax.div(filled + 1023, 1024)

    def sample(b, carry):
        first = pl.multiple_of(8 * b, 8)
        where = jnp.concatenate([cells[pl.ds(first + s, 1), :] for s in range(8)], axis=1)
        got = gather_block(table, where)
        for k in range(4):
            for s in range(8):
                samples[k, pl.ds(first + s, 1), :] = got[k][:, 128 * s : 128 * s + 128]
        return carry

    lax.fori_loop(0, blocks, sample, 0)
    fields = [
        jnp.concatenate([drops[f : f + 1, 128 * s : 128 * s + 128] for s in range(32)], axis=0) for f in range(1, 4)
    ]
    updated, new_terms = evaporate(kept[...], *fields, [samples[k] for k in range(4)])
    for f in range(4):
        terms[f] = new_terms[f]
        for s in range(32):
            drops_out[f : f + 1, 128 * s : 128 * s + 128] = updated[f][s : s + 1, :]
    source[...] = jnp.zeros_like(source)

    def deposit(b, carry):
        first = pl.multiple_of(8 * b, 8)
        row = lambda load: jnp.concatenate([load(pl.ds(first + s, 1)) for s in range(8)], axis=1)
        where = row(lambda at: cells[at, :])
        source[...] += deposit_block([row(lambda at: terms[k, at, :]) for k in range(4)], where)
        return carry

    lax.fori_loop(0, blocks, deposit, 0)
    lane = lax.broadcasted_iota(jnp.int32, (CY, CZ), 0)

    def component(c, carry):
        slot = jnp.where(c < 3, c, jnp.where(c == 5, 0, c - 1))
        scale = jnp.where(c == 3, 0.0, 1.0)
        layers = [gas[c, CY * i : CY * i + CY, :] for i in range(CX)]
        for i in range(CX):
            rows = slice(CY * i, CY * i + CY)
            x = layers[i]
            zero = jnp.zeros_like(x)
            ax = [layers[i + k] if 0 <= i + k < CX else zero for k in (-2, -1, 1, 2)]
            ra = []
            for k in (-2, -1, 1, 2):
                moved = pltpu.roll(x, (-k) % CY, axis=0)
                ok = (lane + k >= 0) & (lane + k < CY)
                ra.append(jnp.where(ok, moved, 0.0))
            az = [pltpu.roll(x, (-k) % CZ, axis=1) for k in (-2, -1, 1, 2)]
            near = (ax[1] + ax[2]) + (ra[1] + ra[2]) + (az[1] + az[2])
            far = (ax[0] + ax[3]) + (ra[0] + ra[3]) + (az[0] + az[3])
            laplace = (16.0 * near - far - 90.0 * x) * (1.0 / 12.0)
            transport = zero
            for j, n in enumerate((ax, ra, az)):
                slope = (8.0 * (n[2] - n[1]) - (n[3] - n[0])) * (1.0 / 12.0)
                transport = transport + speed[j, rows, :] * slope
            advanced = x + time_step * (viscosity[rows, :] * laplace - transport)
            out[c, rows, :] = advanced + scale * source[pl.ds(pl.multiple_of(slot * ROWS + CY * i, CY), CY), :]
        return carry

    lax.fori_loop(0, C, component, 0)


def is_last():
    a = lax.axis_index("ax")
    return (lax.rem(a, WRAP) == WRAP - 1) & (a < lax.axis_size("ax") - 1)


def soon_kernel(*refs):
    pl.when(jnp.logical_not(is_last()))(lambda: final_kernel(None, *refs))


def last_kernel(late, part, updated, gas, viscosity, table, axial_a, axial_b, radial_a, radial_b, *refs):
    given = (part, updated, gas, viscosity, table, axial_a, axial_b, radial_a, radial_b)
    pl.when(is_last())(lambda: final_kernel(late, *given, *refs[3:]))


def final_kernel(
    late, part, updated_in, gas, viscosity, table, axial_a, axial_b_in, radial_a, radial_b,
    out_hbm, drops_hbm, arrivals_hbm, out, arrivals, weights, sems,
):
    copies = [
        pltpu.make_async_copy(updated_in, drops_hbm, sems.at[0]),
        pltpu.make_async_copy(arrivals, arrivals_hbm, sems.at[1]),
    ] + [pltpu.make_async_copy(out.at[c], out_hbm.at[c], sems.at[2 + c]) for c in range(C)]
    copies[0].start()
    odd_ax, odd_rad = parity("ax"), parity("rad")
    if late is None:
        axial_b = axial_b_in
    else:
        axial_b = late
    got = []
    for odd, a, b, base in ((odd_ax, axial_a, axial_b, 192), (odd_rad, radial_a, radial_b, 96)):
        in_a, in_b = a[base : base + 8, 0:CAP], b[base : base + 8, 0:CAP]
        got.append(jnp.where(odd == 1, in_a, in_b))
        got.append(jnp.where(odd == 1, in_b, in_a))
    got = jnp.concatenate(got, axis=1)
    where = got[4:5].astype(jnp.int32)
    samples = gather_block(table, where)
    changed, terms = evaporate(got[0:1], got[1:2], got[2:3], got[3:4], samples)
    arrivals[...] = jnp.concatenate(changed, axis=0)
    copies[1].start()
    source = deposit_block(terms, where)
    lane = lax.broadcasted_iota(jnp.int32, (CY, CZ), 0)
    for i in range(CX):
        rows = slice(CY * i, CY * i + CY)
        factor = viscosity[rows, :] * (time_step / 12.0)
        radial = gas[2, rows, :] / gas[0, rows, :] * (time_step / 12.0)
        for n, last in enumerate((odd_rad == 0, odd_rad == 1)):
            speed = jnp.where(last, -1.0, 1.0) * radial
            first, second = jnp.where(last, CY - 1, 0), jnp.where(last, CY - 2, 1)
            near, far = 16.0 * factor + 8.0 * speed, -(factor + speed)
            weights[2 * n, rows, :] = jnp.where(lane == first, near, jnp.where(lane == second, far, 0.0))
            weights[2 * n + 1, rows, :] = jnp.where(lane == first, far, 0.0)
    edges = []
    for message, last in ((axial_a, odd_ax == 0), (axial_b, odd_ax == 1)):
        sign = jnp.where(last, -1.0, 1.0)
        for k in range(2):
            rows = pl.ds(pl.multiple_of(jnp.where(last, (CX - 1 - k) * CY, k * CY), CY), CY)
            edges.append((message, k, rows, sign))
    for c in range(C):
        for i in range(CX):
            rows = slice(CY * i, CY * i + CY)
            at = c * CX + i
            value = part[c, rows, :]
            for n, message in enumerate((radial_a, radial_b)):
                value = value + weights[2 * n, rows, :] * message[at : at + 1, :]
                value = value + weights[2 * n + 1, rows, :] * message[48 + at : 49 + at, :]
            slot = (0, 1, 2, None, 3, 0)[c]
            if slot is not None:
                value = value + source[slot * ROWS + CY * i : slot * ROWS + CY * i + CY, :]
            out[c, rows, :] = value
        for message, k, rows, sign in edges:
            factor = viscosity[rows, :] * (time_step / 12.0)
            speed = sign * (gas[1, rows, :] / gas[0, rows, :] * (time_step / 12.0))
            near, far = 16.0 * factor + 8.0 * speed, -(factor + speed)
            if k == 0:
                change = near * message[32 * c : 32 * c + CY, :] + far * message[32 * c + CY : 32 * c + 2 * CY, :]
            else:
                change = far * message[32 * c : 32 * c + CY, :]
            out[c, rows, :] += change
        copies[2 + c].start()
    for copy in copies:
        copy.wait()


def routes(n_ax, n_rad):
    flat = lambda a, r: a * n_rad + r
    axial_a, axial_b, radial_a, radial_b, late = [], [], [], [], []
    for a in range(n_ax):
        for r in range(n_rad):
            if a + 1 < n_ax:
                up = (flat(a, r), flat(a + 1, r))
                (axial_a if a % 2 == 0 else axial_b).append(up)
                down = late if (a + 1) % WRAP == 0 else axial_a if a % 2 == 0 else axial_b
                down.append(up[::-1])
            if r + 1 < n_rad:
                out = (flat(a, r), flat(a, r + 1))
                (radial_a if r % 2 == 0 else radial_b).append(out)
                back = radial_a if r % 2 == 0 else radial_b
                back.append(out[::-1])
    return axial_a, axial_b, radial_a, radial_b, late


def body(gas_state, viscosity, droplets, drop_cells, move_lists, move_counts):
    gas = gas_state.reshape(C, ROWS, CZ)
    thick = viscosity.reshape(ROWS, CZ)
    cells = drop_cells.reshape(32, 128)
    shape = jax.ShapeDtypeStruct
    axial_b, axial_a, picks, kept, gas, drops, cells = pl.pallas_call(
        prep_kernel,
        out_shape=(
            shape((200, CZ), f32),
            shape((200, CZ), f32),
            shape((8, 4 * CAP), f32),
            shape((32, 128), f32),
            shape((C, ROWS, CZ), f32),
            shape((4, SLOTS), f32),
            shape((32, 128), jnp.int32),
        ),
        in_specs=[HB] * 5,
        out_specs=(VM,) * 7,
        scratch_shapes=[
            pltpu.VMEM((1, 4, CAP), jnp.int32),
            pltpu.SMEM((1, 4), jnp.int32),
            pltpu.SemaphoreType.DMA((10,)),
        ],
        compiler_params=params,
        name="prep",
    )(*(pltpu.with_memory_space_constraint(x, pltpu.HBM) for x in (gas, droplets, cells, move_lists, move_counts)))
    both = ("ax", "rad")
    to_a, to_b, to_c, to_d, to_late = routes(lax.axis_size("ax"), lax.axis_size("rad"))
    came_b = lax.ppermute(axial_b, both, to_b)
    came_a = lax.ppermute(axial_a, both, to_a)
    results = (shape((C, ROWS, CZ), f32), shape((4, SLOTS), f32), shape((8 * ROWS, CZ), bf16))
    scratch = [
        pltpu.VMEM((3, ROWS, CZ), f32),
        pltpu.VMEM((4, 32, 128), f32),
        pltpu.VMEM((4, 32, 128), f32),
        pltpu.VMEM((4 * ROWS, CZ), f32),
    ]
    late, radial_a, radial_b, *first = pl.pallas_call(
        early_kernel,
        out_shape=(shape((200, CZ), f32), shape((104, CZ), f32), shape((104, CZ), f32), *results),
        in_specs=[VM] * 7,
        out_specs=(VM,) * 6,
        scratch_shapes=scratch,
        compiler_params=params,
        cost_estimate=pl.CostEstimate(flops=40000000000, bytes_accessed=6_000_000, transcendentals=0),
        name="early",
    )(gas, thick, drops, cells, kept, picks, axial_b)
    came_late = lax.ppermute(late, both, to_late)
    came_d = lax.ppermute(radial_b, both, to_d)
    came_c = lax.ppermute(radial_a, both, to_c)
    part, updated, table = pl.pallas_call(
        late_kernel,
        out_shape=results,
        in_specs=[VM] * 8,
        out_specs=(VM,) * 3,
        scratch_shapes=scratch,
        compiler_params=params,
        input_output_aliases={5: 0, 6: 1, 7: 2},
        cost_estimate=pl.CostEstimate(flops=0, bytes_accessed=0, transcendentals=0),
        name="late",
    )(gas, thick, drops, cells, kept, *first)
    finals = (shape((C, ROWS, CZ), f32), shape((4, SLOTS), f32), shape((4, 4 * CAP), f32))
    scratch = [
        pltpu.VMEM((C, ROWS, CZ), f32),
        pltpu.VMEM((4, 4 * CAP), f32),
        pltpu.VMEM((4, ROWS, CZ), f32),
        pltpu.SemaphoreType.DMA((8,)),
    ]
    common = (part, updated, gas, thick, table, came_a, came_b, came_c, came_d)
    finals_soon = pl.pallas_call(
        soon_kernel,
        out_shape=finals,
        in_specs=[VM] * 9,
        out_specs=(HB,) * 3,
        scratch_shapes=scratch,
        compiler_params=params,
        cost_estimate=pl.CostEstimate(flops=0, bytes_accessed=0, transcendentals=0),
        name="soon",
    )(*common)
    out, drops_out, arrivals_out = pl.pallas_call(
        last_kernel,
        out_shape=finals,
        in_specs=[VM] * 10 + [HB] * 3,
        out_specs=(HB,) * 3,
        scratch_shapes=scratch,
        compiler_params=params,
        input_output_aliases={10: 0, 11: 1, 12: 2},
        cost_estimate=pl.CostEstimate(flops=0, bytes_accessed=0, transcendentals=0),
        name="last",
    )(came_late, *common, *finals_soon)
    return out.reshape(gas_state.shape), drops_out, arrivals_out


def solution(mesh):
    placed = (
        P(None, "ax", "rad", None),
        P("ax", "rad", None),
        P(None, ("ax", "rad")),
        P(("ax", "rad")),
        P(("ax", "rad"), None, None),
        P(("ax", "rad"), None),
    )
    return jax.shard_map(
        body,
        mesh=mesh,
        in_specs=placed,
        out_specs=(P(None, "ax", "rad", None), P(None, ("ax", "rad")), P(None, ("ax", "rad"))),
        check_vma=False,
    )
```

```python
import functools

import jax
import jax.numpy as jnp
from jax import lax
from jax.experimental import pallas as pl
from jax.experimental.pallas import tpu as pltpu
from jax.sharding import PartitionSpec as P

time_step = 0.2
f32 = jnp.float32
bf16 = jnp.bfloat16
VM = pl.BlockSpec(memory_space=pltpu.VMEM)
HB = pl.BlockSpec(memory_space=pltpu.HBM)
C, CX, CY, CZ = 6, 8, 16, 512
ROWS = CX * CY
SLOTS, CAP = 4096, 64
params = pltpu.CompilerParams(vmem_limit_bytes=30 << 20)


def split2(x):
    hi = x.astype(bf16)
    return hi, (x - hi.astype(f32)).astype(bf16)


def split3(x):
    hi = x.astype(bf16)
    rest = x - hi.astype(f32)
    mid = rest.astype(bf16)
    return hi, mid, (rest - mid.astype(f32)).astype(bf16)


WRAP = 16


def parity(axis):
    return lax.rem(lax.axis_index(axis), 2)


def is_early():
    a = lax.axis_index("ax")
    return (a > 0) & (lax.rem(a, WRAP) == 0)


def prep_kernel(
    gas_in, drops_in, cells_in, lists_in, counts_in,
    axial_a, picks, kept, gas, drops, cells, lists, counts, sems,
):
    small = [
        pltpu.make_async_copy(source, target, sems.at[n])
        for n, (source, target) in enumerate(
            ((drops_in, drops), (cells_in, cells), (lists_in, lists), (counts_in, counts))
        )
    ]
    large = [pltpu.make_async_copy(gas_in.at[c], gas.at[c], sems.at[4 + c]) for c in range(C)]
    for copy in small + large:
        copy.start()
    for copy in small:
        copy.wait()
    slots = lists[0]
    entry = jnp.concatenate([slots[d : d + 1, :] for d in range(4)], axis=1)
    lane = lax.broadcasted_iota(jnp.int32, (1, CAP), 1)
    used = jnp.concatenate([(lane < counts[0, d]).astype(jnp.int32) for d in range(4)], axis=1)
    low = (lax.broadcasted_iota(jnp.int32, (128, 4 * CAP), 0) == (entry & 127)).astype(f32).astype(bf16)
    place = jnp.where(used > 0, entry >> 7, -1)
    high = (lax.broadcasted_iota(jnp.int32, (32, 4 * CAP), 0) == place).astype(f32)
    fields = []
    for f in range(4):
        fields.append(jnp.concatenate([drops[f : f + 1, 128 * s : 128 * s + 128] for s in range(32)], axis=0))
    parts = []
    for f in range(4):
        parts.extend(split3(fields[f]))
    parts.extend(split2(cells[...].astype(f32)))
    picked = jnp.dot(jnp.concatenate(parts, axis=0), low, preferred_element_type=f32)
    chosen = []
    for f in range(5):
        count = 3 if f < 4 else 2
        total = picked[96 * f : 96 * f + 32]
        for k in range(1, count):
            total = total + picked[96 * f + 32 * k : 96 * f + 32 * k + 32]
        chosen.append(jnp.sum(jnp.where(high > 0, total, 0.0), axis=0, keepdims=True))
    chosen = jnp.concatenate(chosen + [jnp.zeros((3, 4 * CAP), f32)], axis=0)
    gone = lax.dot_general(high.astype(bf16), low, (((1,), (1,)), ((), ())), preferred_element_type=f32)
    kept[...] = fields[0] * (1.0 - gone)
    picks[...] = chosen
    for copy in large:
        copy.wait()
    pack_axial(gas, picks, axial_a, parity("ax") == 0)


def pick_way(picks, axis, last):
    first = 0 if axis == "ax" else 2 * CAP
    return jnp.where(last, picks[:, first : first + CAP], picks[:, first + CAP : first + 2 * CAP])


def pack_axial(gas, picks, message, last):
    near = pl.multiple_of(jnp.where(last, (CX - 1) * CY, 0), CY)
    far = pl.multiple_of(jnp.where(last, (CX - 2) * CY, CY), CY)
    for c in range(C):
        message[32 * c : 32 * c + 16, :] = gas[c, pl.ds(near, CY), :]
        message[32 * c + 16 : 32 * c + 32, :] = gas[c, pl.ds(far, CY), :]
    message[192:200, 0:CAP] = pick_way(picks, "ax", last)


def pack_radial(gas, picks, message, last):
    near, far = jnp.where(last, CY - 1, 0), jnp.where(last, CY - 2, 1)
    for c in range(C):
        for i in range(CX):
            at = c * CX + i
            message[at : at + 1, :] = gas[c, pl.ds(i * CY + near, 1), :]
            message[48 + at : 49 + at, :] = gas[c, pl.ds(i * CY + far, 1), :]
    message[96:104, 0:CAP] = pick_way(picks, "rad", last)


def evaporate(mass, temp, axial, radial, samples):
    axial_gas, radial_gas, gas_temp, fuel = samples
    living = mass > 0.0
    safe_temp = jnp.where(living, temp, 1.0)
    root = jnp.where(living, jnp.exp(jnp.log(jnp.where(living, mass, 1.0)) * (1.0 / 3.0)), 0.0)
    balance = jnp.exp(-1.0 / safe_temp)
    slip = (axial_gas - axial) ** 2 + (radial_gas - radial) ** 2
    wind = jnp.sqrt(jnp.sqrt(1.0 + slip))
    evaporated = 0.1 * root * (jnp.log(1.0 - fuel) - jnp.log(1.0 - balance)) * (1.0 + 0.3 * wind)
    updated = (
        mass - evaporated,
        temp + 0.1 * (gas_temp - temp) - 0.5 * evaporated,
        axial + 0.2 * (axial_gas - axial),
        radial + 0.2 * (radial_gas - radial),
    )
    updated = tuple(jnp.where(living, u, 0.0) for u in updated)
    terms = (
        evaporated,
        evaporated * axial + 0.2 * mass * (axial - axial_gas),
        evaporated * radial + 0.2 * mass * (radial - radial_gas),
        evaporated * temp + 0.1 * mass * (temp - gas_temp),
    )
    return updated, terms


def one_hot(index, size):
    width = index.shape[1]
    return (lax.broadcasted_iota(jnp.int32, (size, width), 0) == index).astype(f32).astype(bf16)


def gather_block(table, where):
    around = one_hot(where & (CZ - 1), CZ)
    got = jnp.dot(table[...], around, preferred_element_type=f32)
    mask = lax.broadcasted_iota(jnp.int32, (ROWS, where.shape[1]), 0) == (where >> 9)
    samples = []
    for k in range(4):
        both = got[2 * ROWS * k : 2 * ROWS * k + ROWS] + got[2 * ROWS * k + ROWS : 2 * ROWS * k + 2 * ROWS]
        samples.append(jnp.sum(jnp.where(mask, both, 0.0), axis=0, keepdims=True))
    return samples


def deposit_block(terms, where):
    around = one_hot(where & (CZ - 1), CZ)
    mask = lax.broadcasted_iota(jnp.int32, (ROWS, where.shape[1]), 0) == (where >> 9)
    halves = [split2(t) for t in terms]
    spread = jnp.concatenate(
        [
            jnp.concatenate([jnp.where(mask, h[side].astype(f32), 0.0).astype(bf16) for h in halves], axis=0)
            for side in range(2)
        ],
        axis=1,
    )
    twice = jnp.concatenate([around, around], axis=1)
    return lax.dot_general(spread, twice, (((1,), (1,)), ((), ())), preferred_element_type=f32)


def early_kernel(gas, viscosity, drops, cells, kept, picks, late, axial_b, radial_a, radial_b, *refs):
    pack_axial(gas, picks, axial_b, parity("ax") == 1)
    pl.when(is_early())(lambda: pack_axial(gas, picks, late, parity("ax") == 1))
    pack_radial(gas, picks, radial_a, parity("rad") == 0)
    pack_radial(gas, picks, radial_b, parity("rad") == 1)
    pl.when(is_early() | (parity("ax") == 1))(lambda: stencil_part(gas, viscosity, *refs))
    pl.when(is_early())(lambda: droplet_part(drops, cells, kept, *refs))


def late_kernel(gas, viscosity, drops, cells, kept, out_in, drops_in, table_in, *refs):
    @pl.when(jnp.logical_not(is_early()))
    def _():
        pl.when(parity("ax") == 0)(lambda: stencil_part(gas, viscosity, *refs))
        droplet_part(drops, cells, kept, *refs)


def droplet_part(drops, cells, kept, out, drops_out, table, speed, samples, terms, source):
    slot = lax.broadcasted_iota(jnp.int32, (1, SLOTS), 1)
    filled = jnp.max(jnp.where(drops[0:1, :] > 0.0, slot + 1, 0))
    blocks = lax.div(filled + 1023, 1024)

    def join(load, first, rows):
        return jnp.concatenate([load(pl.ds(first + s, 1)) for s in range(rows)], axis=1)

    def sample(first, rows):
        got = gather_block(table, join(lambda at: cells[at, :], first, rows))
        for k in range(4):
            for s in range(rows):
                samples[k, pl.ds(first + s, 1), :] = got[k][:, 128 * s : 128 * s + 128]

    def deposit(first, rows):
        where = join(lambda at: cells[at, :], first, rows)
        return deposit_block([join(lambda at: terms[k, at, :], first, rows) for k in range(4)], where)

    def sample_loop(b, carry):
        sample(pl.multiple_of(8 * b, 8), 8)
        return carry

    def deposit_loop(b, carry):
        source[...] += deposit(pl.multiple_of(8 * b, 8), 8)
        return carry

    @pl.when(blocks == 4)
    def _():
        for b in range(8):
            sample(4 * b, 4)

    @pl.when(blocks < 4)
    def _():
        lax.fori_loop(0, blocks, sample_loop, 0)

    fields = [
        jnp.concatenate([drops[f : f + 1, 128 * s : 128 * s + 128] for s in range(32)], axis=0) for f in range(1, 4)
    ]
    updated, new_terms = evaporate(kept[...], *fields, [samples[k] for k in range(4)])
    for f in range(4):
        terms[f] = new_terms[f]
        for s in range(32):
            drops_out[f : f + 1, 128 * s : 128 * s + 128] = updated[f][s : s + 1, :]

    @pl.when(blocks == 4)
    def _():
        source[...] = deposit(0, 4)
        for b in range(1, 8):
            source[...] += deposit(4 * b, 4)

    @pl.when(blocks < 4)
    def _():
        source[...] = jnp.zeros_like(source)
        lax.fori_loop(0, blocks, deposit_loop, 0)

    for c, slot in ((0, 0), (1, 1), (2, 2), (4, 3), (5, 0)):
        out[c] += source[slot * ROWS : slot * ROWS + ROWS, :]


def stencil_part(gas, viscosity, out, drops_out, table, speed, samples, terms, source):
    inverse = 1.0 / gas[0]
    for k, c in enumerate((1, 2, 4, 5)):
        quotient = gas[c] * inverse
        if k < 2:
            speed[k] = quotient
        hi, lo = split2(quotient)
        table[2 * ROWS * k : 2 * ROWS * k + ROWS, :] = hi
        table[2 * ROWS * k + ROWS : 2 * ROWS * k + 2 * ROWS, :] = lo
    speed[2] = gas[3] * inverse
    lane = lax.broadcasted_iota(jnp.int32, (CY, CZ), 0)

    def component(c, carry):
        layers = [gas[c, CY * i : CY * i + CY, :] for i in range(CX)]
        for i in range(CX):
            rows = slice(CY * i, CY * i + CY)
            x = layers[i]
            zero = jnp.zeros_like(x)
            ax = [layers[i + k] if 0 <= i + k < CX else zero for k in (-2, -1, 1, 2)]
            ra = []
            for k in (-2, -1, 1, 2):
                moved = pltpu.roll(x, (-k) % CY, axis=0)
                ok = (lane + k >= 0) & (lane + k < CY)
                ra.append(jnp.where(ok, moved, 0.0))
            az = [pltpu.roll(x, (-k) % CZ, axis=1) for k in (-2, -1, 1, 2)]
            near = (ax[1] + ax[2]) + (ra[1] + ra[2]) + (az[1] + az[2])
            far = (ax[0] + ax[3]) + (ra[0] + ra[3]) + (az[0] + az[3])
            laplace = (16.0 * near - far - 90.0 * x) * (1.0 / 12.0)
            transport = zero
            for j, n in enumerate((ax, ra, az)):
                slope = (8.0 * (n[2] - n[1]) - (n[3] - n[0])) * (1.0 / 12.0)
                transport = transport + speed[j, rows, :] * slope
            out[c, rows, :] = x + time_step * (viscosity[rows, :] * laplace - transport)
        return carry

    lax.fori_loop(0, C, component, 0)


def is_last():
    a = lax.axis_index("ax")
    return (lax.rem(a, WRAP) == WRAP - 1) & (a < lax.axis_size("ax") - 1)


def soon_kernel(*refs):
    pl.when(jnp.logical_not(is_last()))(lambda: final_kernel(None, *refs))


def last_kernel(late, part, updated, gas, viscosity, table, axial_a, axial_b, radial_a, radial_b, *refs):
    given = (part, updated, gas, viscosity, table, axial_a, axial_b, radial_a, radial_b)
    pl.when(is_last())(lambda: final_kernel(late, *given, *refs[3:]))


def final_kernel(
    late, part, updated_in, gas, viscosity, table, axial_a, axial_b_in, radial_a, radial_b,
    out_hbm, drops_hbm, arrivals_hbm, out, arrivals, weights, sems,
):
    copies = [
        pltpu.make_async_copy(updated_in, drops_hbm, sems.at[0]),
        pltpu.make_async_copy(arrivals, arrivals_hbm, sems.at[1]),
    ] + [pltpu.make_async_copy(out.at[c], out_hbm.at[c], sems.at[2 + c]) for c in range(C)]
    copies[0].start()
    odd_ax, odd_rad = parity("ax"), parity("rad")
    if late is None:
        axial_b = axial_b_in
    else:
        axial_b = late
    got = []
    for odd, a, b, base in ((odd_ax, axial_a, axial_b, 192), (odd_rad, radial_a, radial_b, 96)):
        in_a, in_b = a[base : base + 8, 0:CAP], b[base : base + 8, 0:CAP]
        got.append(jnp.where(odd == 1, in_a, in_b))
        got.append(jnp.where(odd == 1, in_b, in_a))
    got = jnp.concatenate(got, axis=1)
    where = got[4:5].astype(jnp.int32)
    samples = gather_block(table, where)
    changed, terms = evaporate(got[0:1], got[1:2], got[2:3], got[3:4], samples)
    arrivals[...] = jnp.concatenate(changed, axis=0)
    copies[1].start()
    source = deposit_block(terms, where)
    lane = lax.broadcasted_iota(jnp.int32, (CY, CZ), 0)
    for i in range(CX):
        rows = slice(CY * i, CY * i + CY)
        factor = viscosity[rows, :] * (time_step / 12.0)
        radial = gas[2, rows, :] / gas[0, rows, :] * (time_step / 12.0)
        for n, last in enumerate((odd_rad == 0, odd_rad == 1)):
            speed = jnp.where(last, -1.0, 1.0) * radial
            first, second = jnp.where(last, CY - 1, 0), jnp.where(last, CY - 2, 1)
            near, far = 16.0 * factor + 8.0 * speed, -(factor + speed)
            weights[2 * n, rows, :] = jnp.where(lane == first, near, jnp.where(lane == second, far, 0.0))
            weights[2 * n + 1, rows, :] = jnp.where(lane == first, far, 0.0)
    edges = []
    for message, last in ((axial_a, odd_ax == 0), (axial_b, odd_ax == 1)):
        sign = jnp.where(last, -1.0, 1.0)
        for k in range(2):
            rows = pl.ds(pl.multiple_of(jnp.where(last, (CX - 1 - k) * CY, k * CY), CY), CY)
            edges.append((message, k, rows, sign))
    for c in range(C):
        for i in range(CX):
            rows = slice(CY * i, CY * i + CY)
            at = c * CX + i
            value = part[c, rows, :]
            for n, message in enumerate((radial_a, radial_b)):
                value = value + weights[2 * n, rows, :] * message[at : at + 1, :]
                value = value + weights[2 * n + 1, rows, :] * message[48 + at : 49 + at, :]
            slot = (0, 1, 2, None, 3, 0)[c]
            if slot is not None:
                value = value + source[slot * ROWS + CY * i : slot * ROWS + CY * i + CY, :]
            out[c, rows, :] = value
        for message, k, rows, sign in edges:
            factor = viscosity[rows, :] * (time_step / 12.0)
            speed = sign * (gas[1, rows, :] / gas[0, rows, :] * (time_step / 12.0))
            near, far = 16.0 * factor + 8.0 * speed, -(factor + speed)
            if k == 0:
                change = near * message[32 * c : 32 * c + CY, :] + far * message[32 * c + CY : 32 * c + 2 * CY, :]
            else:
                change = far * message[32 * c : 32 * c + CY, :]
            out[c, rows, :] += change
        copies[2 + c].start()
    for copy in copies:
        copy.wait()


def routes(n_ax, n_rad):
    flat = lambda a, r: a * n_rad + r
    axial_a, axial_b, radial_a, radial_b, late = [], [], [], [], []
    for a in range(n_ax):
        for r in range(n_rad):
            if a + 1 < n_ax:
                up = (flat(a, r), flat(a + 1, r))
                (axial_a if a % 2 == 0 else axial_b).append(up)
                down = late if (a + 1) % WRAP == 0 else axial_a if a % 2 == 0 else axial_b
                down.append(up[::-1])
            if r + 1 < n_rad:
                out = (flat(a, r), flat(a, r + 1))
                (radial_a if r % 2 == 0 else radial_b).append(out)
                back = radial_a if r % 2 == 0 else radial_b
                back.append(out[::-1])
    return axial_a, axial_b, radial_a, radial_b, late


def body(gas_state, viscosity, droplets, drop_cells, move_lists, move_counts):
    gas = gas_state.reshape(C, ROWS, CZ)
    thick = viscosity.reshape(ROWS, CZ)
    cells = drop_cells.reshape(32, 128)
    shape = jax.ShapeDtypeStruct
    axial_a, picks, kept, gas, drops, cells = pl.pallas_call(
        prep_kernel,
        out_shape=(
            shape((208, CZ), f32),
            shape((8, 4 * CAP), f32),
            shape((32, 128), f32),
            shape((C, ROWS, CZ), f32),
            shape((4, SLOTS), f32),
            shape((32, 128), jnp.int32),
        ),
        in_specs=[HB] * 5,
        out_specs=(VM,) * 6,
        scratch_shapes=[
            pltpu.VMEM((1, 4, CAP), jnp.int32),
            pltpu.SMEM((1, 4), jnp.int32),
            pltpu.SemaphoreType.DMA((10,)),
        ],
        compiler_params=params,
        name="prep",
    )(*(pltpu.with_memory_space_constraint(x, pltpu.HBM) for x in (gas, droplets, cells, move_lists, move_counts)))
    both = ("ax", "rad")
    to_a, to_b, to_c, to_d, to_late = routes(lax.axis_size("ax"), lax.axis_size("rad"))
    came_a = lax.ppermute(axial_a, both, to_a)
    results = (shape((C, ROWS, CZ), f32), shape((4, SLOTS), f32), shape((8 * ROWS, CZ), bf16))
    scratch = [
        pltpu.VMEM((3, ROWS, CZ), f32),
        pltpu.VMEM((4, 32, 128), f32),
        pltpu.VMEM((4, 32, 128), f32),
        pltpu.VMEM((4 * ROWS, CZ), f32),
    ]
    late, axial_b, radial_a, radial_b, *first = pl.pallas_call(
        early_kernel,
        out_shape=(shape((208, CZ), f32), shape((200, CZ), f32), shape((104, CZ), f32), shape((104, CZ), f32), *results),
        in_specs=[VM] * 6,
        out_specs=(VM,) * 7,
        scratch_shapes=scratch,
        compiler_params=params,
        cost_estimate=pl.CostEstimate(flops=40000000000, bytes_accessed=6_000_000, transcendentals=0),
        name="early",
    )(gas, thick, drops, cells, kept, picks)
    came_late = lax.ppermute(late, both, to_late)
    came_b = lax.ppermute(axial_b, both, to_b)
    came_d = lax.ppermute(radial_b, both, to_d)
    came_c = lax.ppermute(radial_a, both, to_c)
    part, updated, table = pl.pallas_call(
        late_kernel,
        out_shape=results,
        in_specs=[VM] * 8,
        out_specs=(VM,) * 3,
        scratch_shapes=scratch,
        compiler_params=params,
        input_output_aliases={5: 0, 6: 1, 7: 2},
        cost_estimate=pl.CostEstimate(flops=0, bytes_accessed=0, transcendentals=0),
        name="late",
    )(gas, thick, drops, cells, kept, *first)
    finals = (shape((C, ROWS, CZ), f32), shape((4, SLOTS), f32), shape((4, 4 * CAP), f32))
    scratch = [
        pltpu.VMEM((C, ROWS, CZ), f32),
        pltpu.VMEM((4, 4 * CAP), f32),
        pltpu.VMEM((4, ROWS, CZ), f32),
        pltpu.SemaphoreType.DMA((8,)),
    ]
    common = (part, updated, gas, thick, table, came_a, came_b, came_c, came_d)
    finals_soon = pl.pallas_call(
        soon_kernel,
        out_shape=finals,
        in_specs=[VM] * 9,
        out_specs=(HB,) * 3,
        scratch_shapes=scratch,
        compiler_params=params,
        cost_estimate=pl.CostEstimate(flops=0, bytes_accessed=0, transcendentals=0),
        name="soon",
    )(*common)
    out, drops_out, arrivals_out = pl.pallas_call(
        last_kernel,
        out_shape=finals,
        in_specs=[VM] * 10 + [HB] * 3,
        out_specs=(HB,) * 3,
        scratch_shapes=scratch,
        compiler_params=params,
        input_output_aliases={10: 0, 11: 1, 12: 2},
        cost_estimate=pl.CostEstimate(flops=0, bytes_accessed=0, transcendentals=0),
        name="last",
    )(came_late, *common, *finals_soon)
    return out.reshape(gas_state.shape), drops_out, arrivals_out


def solution(mesh):
    placed = (
        P(None, "ax", "rad", None),
        P("ax", "rad", None),
        P(None, ("ax", "rad")),
        P(("ax", "rad")),
        P(("ax", "rad"), None, None),
        P(("ax", "rad"), None),
    )
    return jax.shard_map(
        body,
        mesh=mesh,
        in_specs=placed,
        out_specs=(P(None, "ax", "rad", None), P(None, ("ax", "rad")), P(None, ("ax", "rad"))),
        check_vma=False,
    )
```

```python
import functools

import jax
import jax.numpy as jnp
from jax import lax
from jax.experimental import pallas as pl
from jax.experimental.pallas import tpu as pltpu
from jax.sharding import PartitionSpec as P

time_step = 0.2
f32 = jnp.float32
bf16 = jnp.bfloat16
VM = pl.BlockSpec(memory_space=pltpu.VMEM)
HB = pl.BlockSpec(memory_space=pltpu.HBM)
C, CX, CY, CZ = 6, 8, 16, 512
ROWS = CX * CY
SLOTS, CAP = 4096, 64
params = pltpu.CompilerParams(vmem_limit_bytes=30 << 20)


def split2(x):
    hi = x.astype(bf16)
    return hi, (x - hi.astype(f32)).astype(bf16)


def split3(x):
    hi = x.astype(bf16)
    rest = x - hi.astype(f32)
    mid = rest.astype(bf16)
    return hi, mid, (rest - mid.astype(f32)).astype(bf16)


WRAP = 16


def parity(axis):
    return lax.rem(lax.axis_index(axis), 2)


def is_early():
    a = lax.axis_index("ax")
    return (a > 0) & (lax.rem(a, WRAP) == 0)


def prep_kernel(
    gas_in, drops_in, cells_in, lists_in, counts_in,
    axial_a, picks, kept, gas, drops, cells, lists, counts, sems,
):
    small = [
        pltpu.make_async_copy(source, target, sems.at[n])
        for n, (source, target) in enumerate(
            ((drops_in, drops), (cells_in, cells), (lists_in, lists), (counts_in, counts))
        )
    ]
    large = [pltpu.make_async_copy(gas_in.at[c], gas.at[c], sems.at[4 + c]) for c in range(C)]
    for copy in small + large:
        copy.start()
    for copy in small:
        copy.wait()
    slots = lists[0]
    entry = jnp.concatenate([slots[d : d + 1, :] for d in range(4)], axis=1)
    lane = lax.broadcasted_iota(jnp.int32, (1, CAP), 1)
    used = jnp.concatenate([(lane < counts[0, d]).astype(jnp.int32) for d in range(4)], axis=1)
    low = (lax.broadcasted_iota(jnp.int32, (128, 4 * CAP), 0) == (entry & 127)).astype(f32).astype(bf16)
    place = jnp.where(used > 0, entry >> 7, -1)
    high = (lax.broadcasted_iota(jnp.int32, (32, 4 * CAP), 0) == place).astype(f32)
    fields = []
    for f in range(4):
        fields.append(jnp.concatenate([drops[f : f + 1, 128 * s : 128 * s + 128] for s in range(32)], axis=0))
    parts = []
    for f in range(4):
        parts.extend(split3(fields[f]))
    parts.extend(split2(cells[...].astype(f32)))
    picked = jnp.dot(jnp.concatenate(parts, axis=0), low, preferred_element_type=f32)
    chosen = []
    for f in range(5):
        count = 3 if f < 4 else 2
        total = picked[96 * f : 96 * f + 32]
        for k in range(1, count):
            total = total + picked[96 * f + 32 * k : 96 * f + 32 * k + 32]
        chosen.append(jnp.sum(jnp.where(high > 0, total, 0.0), axis=0, keepdims=True))
    chosen = jnp.concatenate(chosen + [jnp.zeros((3, 4 * CAP), f32)], axis=0)
    gone = lax.dot_general(high.astype(bf16), low, (((1,), (1,)), ((), ())), preferred_element_type=f32)
    kept[...] = fields[0] * (1.0 - gone)
    picks[...] = chosen
    for copy in large:
        copy.wait()
    pack_axial(gas, picks, axial_a, parity("ax") == 0)


def pick_way(picks, axis, last):
    first = 0 if axis == "ax" else 2 * CAP
    return jnp.where(last, picks[:, first : first + CAP], picks[:, first + CAP : first + 2 * CAP])


def pack_axial(gas, picks, message, last):
    near = pl.multiple_of(jnp.where(last, (CX - 1) * CY, 0), CY)
    far = pl.multiple_of(jnp.where(last, (CX - 2) * CY, CY), CY)
    for c in range(C):
        message[32 * c : 32 * c + 16, :] = gas[c, pl.ds(near, CY), :]
        message[32 * c + 16 : 32 * c + 32, :] = gas[c, pl.ds(far, CY), :]
    message[192:200, 0:CAP] = pick_way(picks, "ax", last)


def pack_radial(gas, picks, message, last):
    near, far = jnp.where(last, CY - 1, 0), jnp.where(last, CY - 2, 1)
    for c in range(C):
        for i in range(CX):
            at = c * CX + i
            message[at : at + 1, :] = gas[c, pl.ds(i * CY + near, 1), :]
            message[48 + at : 49 + at, :] = gas[c, pl.ds(i * CY + far, 1), :]
    message[96:104, 0:CAP] = pick_way(picks, "rad", last)


def evaporate(mass, temp, axial, radial, samples):
    axial_gas, radial_gas, gas_temp, fuel = samples
    living = mass > 0.0
    safe_temp = jnp.where(living, temp, 1.0)
    root = jnp.where(living, jnp.exp(jnp.log(jnp.where(living, mass, 1.0)) * (1.0 / 3.0)), 0.0)
    balance = jnp.exp(-1.0 / safe_temp)
    slip = (axial_gas - axial) ** 2 + (radial_gas - radial) ** 2
    wind = jnp.sqrt(jnp.sqrt(1.0 + slip))
    evaporated = 0.1 * root * (jnp.log(1.0 - fuel) - jnp.log(1.0 - balance)) * (1.0 + 0.3 * wind)
    updated = (
        mass - evaporated,
        temp + 0.1 * (gas_temp - temp) - 0.5 * evaporated,
        axial + 0.2 * (axial_gas - axial),
        radial + 0.2 * (radial_gas - radial),
    )
    updated = tuple(jnp.where(living, u, 0.0) for u in updated)
    terms = (
        evaporated,
        evaporated * axial + 0.2 * mass * (axial - axial_gas),
        evaporated * radial + 0.2 * mass * (radial - radial_gas),
        evaporated * temp + 0.1 * mass * (temp - gas_temp),
    )
    return updated, terms


def one_hot(index, size):
    width = index.shape[1]
    return (lax.broadcasted_iota(jnp.int32, (size, width), 0) == index).astype(f32).astype(bf16)


def gather_block(table, where):
    around = one_hot(where & (CZ - 1), CZ)
    got = jnp.dot(table[...], around, preferred_element_type=f32)
    mask = lax.broadcasted_iota(jnp.int32, (ROWS, where.shape[1]), 0) == (where >> 9)
    samples = []
    for k in range(4):
        both = got[2 * ROWS * k : 2 * ROWS * k + ROWS] + got[2 * ROWS * k + ROWS : 2 * ROWS * k + 2 * ROWS]
        samples.append(jnp.sum(jnp.where(mask, both, 0.0), axis=0, keepdims=True))
    return samples


def deposit_block(terms, where):
    around = one_hot(where & (CZ - 1), CZ)
    mask = lax.broadcasted_iota(jnp.int32, (ROWS, where.shape[1]), 0) == (where >> 9)
    halves = [split2(t) for t in terms]
    spread = jnp.concatenate(
        [
            jnp.concatenate([jnp.where(mask, h[side].astype(f32), 0.0).astype(bf16) for h in halves], axis=0)
            for side in range(2)
        ],
        axis=1,
    )
    twice = jnp.concatenate([around, around], axis=1)
    return lax.dot_general(spread, twice, (((1,), (1,)), ((), ())), preferred_element_type=f32)


def stencil_soon():
    a = lax.axis_index("ax")
    return is_early() | ((lax.rem(a, 2) == 1) & (lax.rem(a, WRAP) != WRAP - 1))


def first_kernel(gas, viscosity, picks, axial_b, radial_a, radial_b, out, table, speed):
    pack_axial(gas, picks, axial_b, parity("ax") == 1)
    pack_radial(gas, picks, radial_a, parity("rad") == 0)
    pack_radial(gas, picks, radial_b, parity("rad") == 1)
    pl.when(stencil_soon())(lambda: stencil_part(gas, viscosity, out, table, speed))


def early_kernel(gas, picks, drops, cells, kept, out_in, table, late, out, drops_out, *scratch):
    @pl.when(is_early())
    def _():
        pack_axial(gas, picks, late, parity("ax") == 1)
        droplet_part(drops, cells, kept, table, out, drops_out, *scratch)


def late_kernel(gas, viscosity, drops, cells, kept, out_in, drops_in, table_in, out, drops_out, table, speed, *scratch):
    pl.when(jnp.logical_not(stencil_soon()))(lambda: stencil_part(gas, viscosity, out, table, speed))
    pl.when(jnp.logical_not(is_early()))(lambda: droplet_part(drops, cells, kept, table, out, drops_out, *scratch))


def droplet_part(drops, cells, kept, table, out, drops_out, samples, terms, source):
    slot = lax.broadcasted_iota(jnp.int32, (1, SLOTS), 1)
    filled = jnp.max(jnp.where(drops[0:1, :] > 0.0, slot + 1, 0))
    blocks = lax.div(filled + 1023, 1024)

    def join(load, first, rows):
        return jnp.concatenate([load(pl.ds(first + s, 1)) for s in range(rows)], axis=1)

    def sample(first, rows):
        got = gather_block(table, join(lambda at: cells[at, :], first, rows))
        for k in range(4):
            for s in range(rows):
                samples[k, pl.ds(first + s, 1), :] = got[k][:, 128 * s : 128 * s + 128]

    def deposit(first, rows):
        where = join(lambda at: cells[at, :], first, rows)
        return deposit_block([join(lambda at: terms[k, at, :], first, rows) for k in range(4)], where)

    def sample_loop(b, carry):
        sample(pl.multiple_of(8 * b, 8), 8)
        return carry

    def deposit_loop(b, carry):
        source[...] += deposit(pl.multiple_of(8 * b, 8), 8)
        return carry

    @pl.when(blocks == 4)
    def _():
        for b in range(8):
            sample(4 * b, 4)

    @pl.when(blocks < 4)
    def _():
        lax.fori_loop(0, blocks, sample_loop, 0)

    fields = [
        jnp.concatenate([drops[f : f + 1, 128 * s : 128 * s + 128] for s in range(32)], axis=0) for f in range(1, 4)
    ]
    updated, new_terms = evaporate(kept[...], *fields, [samples[k] for k in range(4)])
    for f in range(4):
        terms[f] = new_terms[f]
        for s in range(32):
            drops_out[f : f + 1, 128 * s : 128 * s + 128] = updated[f][s : s + 1, :]

    @pl.when(blocks == 4)
    def _():
        source[...] = deposit(0, 4)
        for b in range(1, 8):
            source[...] += deposit(4 * b, 4)

    @pl.when(blocks < 4)
    def _():
        source[...] = jnp.zeros_like(source)
        lax.fori_loop(0, blocks, deposit_loop, 0)

    for c, slot in ((0, 0), (1, 1), (2, 2), (4, 3), (5, 0)):
        out[c] += source[slot * ROWS : slot * ROWS + ROWS, :]


def stencil_part(gas, viscosity, out, table, speed):
    inverse = 1.0 / gas[0]
    for k, c in enumerate((1, 2, 4, 5)):
        quotient = gas[c] * inverse
        if k < 2:
            speed[k] = quotient
        hi, lo = split2(quotient)
        table[2 * ROWS * k : 2 * ROWS * k + ROWS, :] = hi
        table[2 * ROWS * k + ROWS : 2 * ROWS * k + 2 * ROWS, :] = lo
    speed[2] = gas[3] * inverse
    lane = lax.broadcasted_iota(jnp.int32, (CY, CZ), 0)

    def component(c, carry):
        layers = [gas[c, CY * i : CY * i + CY, :] for i in range(CX)]
        for i in range(CX):
            rows = slice(CY * i, CY * i + CY)
            x = layers[i]
            zero = jnp.zeros_like(x)
            ax = [layers[i + k] if 0 <= i + k < CX else zero for k in (-2, -1, 1, 2)]
            ra = []
            for k in (-2, -1, 1, 2):
                moved = pltpu.roll(x, (-k) % CY, axis=0)
                ok = (lane + k >= 0) & (lane + k < CY)
                ra.append(jnp.where(ok, moved, 0.0))
            az = [pltpu.roll(x, (-k) % CZ, axis=1) for k in (-2, -1, 1, 2)]
            near = (ax[1] + ax[2]) + (ra[1] + ra[2]) + (az[1] + az[2])
            far = (ax[0] + ax[3]) + (ra[0] + ra[3]) + (az[0] + az[3])
            laplace = (16.0 * near - far - 90.0 * x) * (1.0 / 12.0)
            transport = zero
            for j, n in enumerate((ax, ra, az)):
                slope = (8.0 * (n[2] - n[1]) - (n[3] - n[0])) * (1.0 / 12.0)
                transport = transport + speed[j, rows, :] * slope
            out[c, rows, :] = x + time_step * (viscosity[rows, :] * laplace - transport)
        return carry

    lax.fori_loop(0, C, component, 0)


def is_last():
    a = lax.axis_index("ax")
    return (lax.rem(a, WRAP) == WRAP - 1) & (a < lax.axis_size("ax") - 1)


def soon_kernel(*refs):
    pl.when(jnp.logical_not(is_last()))(lambda: final_kernel(None, *refs))


def last_kernel(late, part, updated, gas, viscosity, table, axial_a, axial_b, radial_a, radial_b, *refs):
    given = (part, updated, gas, viscosity, table, axial_a, axial_b, radial_a, radial_b)
    pl.when(is_last())(lambda: final_kernel(late, *given, *refs[3:]))


def final_kernel(
    late, part, updated_in, gas, viscosity, table, axial_a, axial_b_in, radial_a, radial_b,
    out_hbm, drops_hbm, arrivals_hbm, out, arrivals, weights, sems,
):
    copies = [
        pltpu.make_async_copy(updated_in, drops_hbm, sems.at[0]),
        pltpu.make_async_copy(arrivals, arrivals_hbm, sems.at[1]),
    ] + [pltpu.make_async_copy(out.at[c], out_hbm.at[c], sems.at[2 + c]) for c in range(C)]
    copies[0].start()
    odd_ax, odd_rad = parity("ax"), parity("rad")
    if late is None:
        axial_b = axial_b_in
    else:
        axial_b = late
    got = []
    for odd, a, b, base in ((odd_ax, axial_a, axial_b, 192), (odd_rad, radial_a, radial_b, 96)):
        in_a, in_b = a[base : base + 8, 0:CAP], b[base : base + 8, 0:CAP]
        got.append(jnp.where(odd == 1, in_a, in_b))
        got.append(jnp.where(odd == 1, in_b, in_a))
    got = jnp.concatenate(got, axis=1)
    where = got[4:5].astype(jnp.int32)
    samples = gather_block(table, where)
    changed, terms = evaporate(got[0:1], got[1:2], got[2:3], got[3:4], samples)
    arrivals[...] = jnp.concatenate(changed, axis=0)
    copies[1].start()
    source = deposit_block(terms, where)
    lane = lax.broadcasted_iota(jnp.int32, (CY, CZ), 0)
    for i in range(CX):
        rows = slice(CY * i, CY * i + CY)
        factor = viscosity[rows, :] * (time_step / 12.0)
        radial = gas[2, rows, :] / gas[0, rows, :] * (time_step / 12.0)
        for n, last in enumerate((odd_rad == 0, odd_rad == 1)):
            speed = jnp.where(last, -1.0, 1.0) * radial
            first, second = jnp.where(last, CY - 1, 0), jnp.where(last, CY - 2, 1)
            near, far = 16.0 * factor + 8.0 * speed, -(factor + speed)
            weights[2 * n, rows, :] = jnp.where(lane == first, near, jnp.where(lane == second, far, 0.0))
            weights[2 * n + 1, rows, :] = jnp.where(lane == first, far, 0.0)
    edges = []
    for message, last in ((axial_a, odd_ax == 0), (axial_b, odd_ax == 1)):
        sign = jnp.where(last, -1.0, 1.0)
        for k in range(2):
            rows = pl.ds(pl.multiple_of(jnp.where(last, (CX - 1 - k) * CY, k * CY), CY), CY)
            edges.append((message, k, rows, sign))
    for c in range(C):
        for i in range(CX):
            rows = slice(CY * i, CY * i + CY)
            at = c * CX + i
            value = part[c, rows, :]
            for n, message in enumerate((radial_a, radial_b)):
                value = value + weights[2 * n, rows, :] * message[at : at + 1, :]
                value = value + weights[2 * n + 1, rows, :] * message[48 + at : 49 + at, :]
            slot = (0, 1, 2, None, 3, 0)[c]
            if slot is not None:
                value = value + source[slot * ROWS + CY * i : slot * ROWS + CY * i + CY, :]
            out[c, rows, :] = value
        for message, k, rows, sign in edges:
            factor = viscosity[rows, :] * (time_step / 12.0)
            speed = sign * (gas[1, rows, :] / gas[0, rows, :] * (time_step / 12.0))
            near, far = 16.0 * factor + 8.0 * speed, -(factor + speed)
            if k == 0:
                change = near * message[32 * c : 32 * c + CY, :] + far * message[32 * c + CY : 32 * c + 2 * CY, :]
            else:
                change = far * message[32 * c : 32 * c + CY, :]
            out[c, rows, :] += change
        copies[2 + c].start()
    for copy in copies:
        copy.wait()


def routes(n_ax, n_rad):
    flat = lambda a, r: a * n_rad + r
    axial_a, axial_b, radial_a, radial_b, late = [], [], [], [], []
    for a in range(n_ax):
        for r in range(n_rad):
            if a + 1 < n_ax:
                up = (flat(a, r), flat(a + 1, r))
                (axial_a if a % 2 == 0 else axial_b).append(up)
                down = late if (a + 1) % WRAP == 0 else axial_a if a % 2 == 0 else axial_b
                down.append(up[::-1])
            if r + 1 < n_rad:
                out = (flat(a, r), flat(a, r + 1))
                (radial_a if r % 2 == 0 else radial_b).append(out)
                back = radial_a if r % 2 == 0 else radial_b
                back.append(out[::-1])
    return axial_a, axial_b, radial_a, radial_b, late


def body(gas_state, viscosity, droplets, drop_cells, move_lists, move_counts):
    gas = gas_state.reshape(C, ROWS, CZ)
    thick = viscosity.reshape(ROWS, CZ)
    cells = drop_cells.reshape(32, 128)
    shape = jax.ShapeDtypeStruct
    axial_a, picks, kept, gas, drops, cells = pl.pallas_call(
        prep_kernel,
        out_shape=(
            shape((208, CZ), f32),
            shape((8, 4 * CAP), f32),
            shape((32, 128), f32),
            shape((C, ROWS, CZ), f32),
            shape((4, SLOTS), f32),
            shape((32, 128), jnp.int32),
        ),
        in_specs=[HB] * 5,
        out_specs=(VM,) * 6,
        scratch_shapes=[
            pltpu.VMEM((1, 4, CAP), jnp.int32),
            pltpu.SMEM((1, 4), jnp.int32),
            pltpu.SemaphoreType.DMA((10,)),
        ],
        compiler_params=params,
        name="prep",
    )(*(pltpu.with_memory_space_constraint(x, pltpu.HBM) for x in (gas, droplets, cells, move_lists, move_counts)))
    both = ("ax", "rad")
    to_a, to_b, to_c, to_d, to_late = routes(lax.axis_size("ax"), lax.axis_size("rad"))
    came_a = lax.ppermute(axial_a, both, to_a)
    part, updated, table = shape((C, ROWS, CZ), f32), shape((4, SLOTS), f32), shape((8 * ROWS, CZ), bf16)
    speed = [pltpu.VMEM((3, ROWS, CZ), f32)]
    scratch = [pltpu.VMEM((4, 32, 128), f32), pltpu.VMEM((4, 32, 128), f32), pltpu.VMEM((4 * ROWS, CZ), f32)]
    cost = lambda flops: pl.CostEstimate(flops=flops, bytes_accessed=0, transcendentals=0)

    axial_b, radial_a, radial_b, part, table = pl.pallas_call(
        first_kernel,
        out_shape=(shape((200, CZ), f32), shape((104, CZ), f32), shape((104, CZ), f32), part, table),
        in_specs=[VM] * 3,
        out_specs=(VM,) * 5,
        scratch_shapes=speed,
        compiler_params=params,
        cost_estimate=cost(4000000000),
        name="first",
    )(gas, thick, picks)
    came_b = lax.ppermute(axial_b, both, to_b)
    came_d = lax.ppermute(radial_b, both, to_d)
    came_c = lax.ppermute(radial_a, both, to_c)
    late, part, updated = pl.pallas_call(
        early_kernel,
        out_shape=(shape((208, CZ), f32), shape(part.shape, f32), updated),
        in_specs=[VM] * 7,
        out_specs=(VM,) * 3,
        scratch_shapes=scratch,
        compiler_params=params,
        input_output_aliases={5: 1},
        cost_estimate=cost(0),
        name="early",
    )(gas, picks, drops, cells, kept, part, table)
    came_late = lax.ppermute(late, both, to_late)
    part, updated, table = pl.pallas_call(
        late_kernel,
        out_shape=tuple(shape(x.shape, x.dtype) for x in (part, updated, table)),
        in_specs=[VM] * 8,
        out_specs=(VM,) * 3,
        scratch_shapes=speed + scratch,
        compiler_params=params,
        input_output_aliases={5: 0, 6: 1, 7: 2},
        cost_estimate=cost(0),
        name="late",
    )(gas, thick, drops, cells, kept, part, updated, table)
    finals = (shape((C, ROWS, CZ), f32), shape((4, SLOTS), f32), shape((4, 4 * CAP), f32))
    scratch = [
        pltpu.VMEM((C, ROWS, CZ), f32),
        pltpu.VMEM((4, 4 * CAP), f32),
        pltpu.VMEM((4, ROWS, CZ), f32),
        pltpu.SemaphoreType.DMA((8,)),
    ]
    common = (part, updated, gas, thick, table, came_a, came_b, came_c, came_d)
    finals_soon = pl.pallas_call(
        soon_kernel,
        out_shape=finals,
        in_specs=[VM] * 9,
        out_specs=(HB,) * 3,
        scratch_shapes=scratch,
        compiler_params=params,
        cost_estimate=pl.CostEstimate(flops=4000000000, bytes_accessed=0, transcendentals=0),
        name="soon",
    )(*common)
    out, drops_out, arrivals_out = pl.pallas_call(
        last_kernel,
        out_shape=finals,
        in_specs=[VM] * 10 + [HB] * 3,
        out_specs=(HB,) * 3,
        scratch_shapes=scratch,
        compiler_params=params,
        input_output_aliases={10: 0, 11: 1, 12: 2},
        cost_estimate=pl.CostEstimate(flops=0, bytes_accessed=0, transcendentals=0),
        name="last",
    )(came_late, *common, *finals_soon)
    return out.reshape(gas_state.shape), drops_out, arrivals_out


def solution(mesh):
    placed = (
        P(None, "ax", "rad", None),
        P("ax", "rad", None),
        P(None, ("ax", "rad")),
        P(("ax", "rad")),
        P(("ax", "rad"), None, None),
        P(("ax", "rad"), None),
    )
    return jax.shard_map(
        body,
        mesh=mesh,
        in_specs=placed,
        out_specs=(P(None, "ax", "rad", None), P(None, ("ax", "rad")), P(None, ("ax", "rad"))),
        check_vma=False,
    )
```

```python
import functools

import jax
import jax.numpy as jnp
from jax import lax
from jax.experimental import pallas as pl
from jax.experimental.pallas import tpu as pltpu
from jax.sharding import PartitionSpec as P

time_step = 0.2
f32 = jnp.float32
bf16 = jnp.bfloat16
VM = pl.BlockSpec(memory_space=pltpu.VMEM)
HB = pl.BlockSpec(memory_space=pltpu.HBM)
C, CX, CY, CZ = 6, 8, 16, 512
ROWS = CX * CY
SLOTS, CAP = 4096, 64
params = pltpu.CompilerParams(vmem_limit_bytes=30 << 20)


def split2(x):
    hi = x.astype(bf16)
    return hi, (x - hi.astype(f32)).astype(bf16)


def split3(x):
    hi = x.astype(bf16)
    rest = x - hi.astype(f32)
    mid = rest.astype(bf16)
    return hi, mid, (rest - mid.astype(f32)).astype(bf16)


WRAP = 16


def parity(axis):
    return lax.rem(lax.axis_index(axis), 2)


def is_early():
    a = lax.axis_index("ax")
    return (a > 0) & (lax.rem(a, WRAP) == 0)


def prep_kernel(
    gas_in, drops_in, cells_in, lists_in, counts_in,
    axial_a, picks, kept, gas, drops, cells, lists, counts, sems,
):
    small = [
        pltpu.make_async_copy(source, target, sems.at[n])
        for n, (source, target) in enumerate(
            ((drops_in, drops), (cells_in, cells), (lists_in, lists), (counts_in, counts))
        )
    ]
    large = [pltpu.make_async_copy(gas_in.at[c], gas.at[c], sems.at[4 + c]) for c in range(C)]
    for copy in small + large:
        copy.start()
    for copy in small:
        copy.wait()
    slots = lists[0]
    entry = jnp.concatenate([slots[d : d + 1, :] for d in range(4)], axis=1)
    lane = lax.broadcasted_iota(jnp.int32, (1, CAP), 1)
    used = jnp.concatenate([(lane < counts[0, d]).astype(jnp.int32) for d in range(4)], axis=1)
    low = (lax.broadcasted_iota(jnp.int32, (128, 4 * CAP), 0) == (entry & 127)).astype(f32).astype(bf16)
    place = jnp.where(used > 0, entry >> 7, -1)
    high = (lax.broadcasted_iota(jnp.int32, (32, 4 * CAP), 0) == place).astype(f32)
    fields = []
    for f in range(4):
        fields.append(jnp.concatenate([drops[f : f + 1, 128 * s : 128 * s + 128] for s in range(32)], axis=0))
    parts = []
    for f in range(4):
        parts.extend(split3(fields[f]))
    parts.extend(split2(cells[...].astype(f32)))
    picked = jnp.dot(jnp.concatenate(parts, axis=0), low, preferred_element_type=f32)
    chosen = []
    for f in range(5):
        count = 3 if f < 4 else 2
        total = picked[96 * f : 96 * f + 32]
        for k in range(1, count):
            total = total + picked[96 * f + 32 * k : 96 * f + 32 * k + 32]
        chosen.append(jnp.sum(jnp.where(high > 0, total, 0.0), axis=0, keepdims=True))
    chosen = jnp.concatenate(chosen + [jnp.zeros((3, 4 * CAP), f32)], axis=0)
    gone = lax.dot_general(high.astype(bf16), low, (((1,), (1,)), ((), ())), preferred_element_type=f32)
    kept[...] = fields[0] * (1.0 - gone)
    picks[...] = chosen
    for copy in large:
        copy.wait()
    pack_axial(gas, picks, axial_a, parity("ax") == 0)


def pick_way(picks, axis, last):
    first = 0 if axis == "ax" else 2 * CAP
    return jnp.where(last, picks[:, first : first + CAP], picks[:, first + CAP : first + 2 * CAP])


def pack_axial(gas, picks, message, last):
    near = pl.multiple_of(jnp.where(last, (CX - 1) * CY, 0), CY)
    far = pl.multiple_of(jnp.where(last, (CX - 2) * CY, CY), CY)
    for c in range(C):
        message[32 * c : 32 * c + 16, :] = gas[c, pl.ds(near, CY), :]
        message[32 * c + 16 : 32 * c + 32, :] = gas[c, pl.ds(far, CY), :]
    message[192:200, 0:CAP] = pick_way(picks, "ax", last)


def pack_radial(gas, picks, message, last):
    near, far = jnp.where(last, CY - 1, 0), jnp.where(last, CY - 2, 1)
    for c in range(C):
        for i in range(CX):
            at = c * CX + i
            message[at : at + 1, :] = gas[c, pl.ds(i * CY + near, 1), :]
            message[48 + at : 49 + at, :] = gas[c, pl.ds(i * CY + far, 1), :]
    message[96:104, 0:CAP] = pick_way(picks, "rad", last)


def evaporate(mass, temp, axial, radial, samples):
    axial_gas, radial_gas, gas_temp, fuel = samples
    living = mass > 0.0
    safe_temp = jnp.where(living, temp, 1.0)
    root = jnp.where(living, jnp.exp(jnp.log(jnp.where(living, mass, 1.0)) * (1.0 / 3.0)), 0.0)
    balance = jnp.exp(-1.0 / safe_temp)
    slip = (axial_gas - axial) ** 2 + (radial_gas - radial) ** 2
    wind = jnp.sqrt(jnp.sqrt(1.0 + slip))
    evaporated = 0.1 * root * (jnp.log(1.0 - fuel) - jnp.log(1.0 - balance)) * (1.0 + 0.3 * wind)
    updated = (
        mass - evaporated,
        temp + 0.1 * (gas_temp - temp) - 0.5 * evaporated,
        axial + 0.2 * (axial_gas - axial),
        radial + 0.2 * (radial_gas - radial),
    )
    updated = tuple(jnp.where(living, u, 0.0) for u in updated)
    terms = (
        evaporated,
        evaporated * axial + 0.2 * mass * (axial - axial_gas),
        evaporated * radial + 0.2 * mass * (radial - radial_gas),
        evaporated * temp + 0.1 * mass * (temp - gas_temp),
    )
    return updated, terms


def one_hot(index, size):
    width = index.shape[1]
    return (lax.broadcasted_iota(jnp.int32, (size, width), 0) == index).astype(f32).astype(bf16)


def gather_block(table, around, where):
    got = jnp.dot(table[...], jnp.concatenate([around, around], axis=0), preferred_element_type=f32)
    mask = lax.broadcasted_iota(jnp.int32, (ROWS, where.shape[1]), 0) == (where >> 9)
    return [
        jnp.sum(jnp.where(mask, got[ROWS * k : ROWS * k + ROWS], 0.0), axis=0, keepdims=True) for k in range(4)
    ]


def deposit_block(terms, around, where):
    row = one_hot(where >> 9, ROWS)
    halves = [split2(t) for t in terms]
    spread = jnp.concatenate(
        [jnp.concatenate([row * h[side] for h in halves], axis=0) for side in range(2)],
        axis=1,
    )
    twice = jnp.concatenate([around, around], axis=1)
    return lax.dot_general(spread, twice, (((1,), (1,)), ((), ())), preferred_element_type=f32)


def stencil_soon():
    a = lax.axis_index("ax")
    return is_early() | ((lax.rem(a, 2) == 1) & (a > 1) & (lax.rem(a, WRAP) != WRAP - 1))


def first_kernel(gas, viscosity, picks, axial_b, radial_a, radial_b, out, table, speed):
    pack_axial(gas, picks, axial_b, parity("ax") == 1)
    pack_radial(gas, picks, radial_a, parity("rad") == 0)
    pack_radial(gas, picks, radial_b, parity("rad") == 1)
    pl.when(stencil_soon())(lambda: stencil_part(gas, viscosity, out, table, speed))


def early_kernel(gas, picks, drops, cells, kept, out_in, table, late, out, drops_out, *scratch):
    @pl.when(is_early())
    def _():
        pack_axial(gas, picks, late, parity("ax") == 1)
        droplet_part(drops, cells, kept, table, out, drops_out, *scratch)


def late_kernel(gas, viscosity, drops, cells, kept, out_in, drops_in, table_in, out, drops_out, table, speed, *scratch):
    pl.when(jnp.logical_not(stencil_soon()))(lambda: stencil_part(gas, viscosity, out, table, speed))
    pl.when(jnp.logical_not(is_early()))(lambda: droplet_part(drops, cells, kept, table, out, drops_out, *scratch))


def droplet_part(drops, cells, kept, table, out, drops_out, samples, terms, source, hots):
    slot = lax.broadcasted_iota(jnp.int32, (1, SLOTS), 1)
    filled = jnp.max(jnp.where(drops[0:1, :] > 0.0, slot + 1, 0))
    blocks = lax.div(filled + 1023, 1024)

    def join(load, first, rows):
        return jnp.concatenate([load(pl.ds(first + s, 1)) for s in range(rows)], axis=1)

    def lanes(first, rows):
        return pl.ds(first * 128 if isinstance(first, int) else pl.multiple_of(first * 128, 128 * rows), 128 * rows)

    def sample(first, rows):
        where = join(lambda at: cells[at, :], first, rows)
        around = one_hot(where & (CZ - 1), CZ)
        hots[:, lanes(first, rows)] = around
        got = gather_block(table, around, where)
        for k in range(4):
            for s in range(rows):
                samples[k, pl.ds(first + s, 1), :] = got[k][:, 128 * s : 128 * s + 128]

    def deposit(first, rows):
        where = join(lambda at: cells[at, :], first, rows)
        return deposit_block(
            [join(lambda at: terms[k, at, :], first, rows) for k in range(4)], hots[:, lanes(first, rows)], where
        )

    def sample_loop(b, carry):
        sample(pl.multiple_of(8 * b, 8), 8)
        return carry

    def deposit_loop(b, carry):
        source[...] += deposit(pl.multiple_of(8 * b, 8), 8)
        return carry

    @pl.when(blocks == 4)
    def _():
        for b in range(8):
            sample(4 * b, 4)

    @pl.when(blocks < 4)
    def _():
        lax.fori_loop(0, blocks, sample_loop, 0)

    fields = [
        jnp.concatenate([drops[f : f + 1, 128 * s : 128 * s + 128] for s in range(32)], axis=0) for f in range(1, 4)
    ]
    updated, new_terms = evaporate(kept[...], *fields, [samples[k] for k in range(4)])
    for f in range(4):
        terms[f] = new_terms[f]
        for s in range(32):
            drops_out[f : f + 1, 128 * s : 128 * s + 128] = updated[f][s : s + 1, :]

    @pl.when(blocks == 4)
    def _():
        source[...] = deposit(0, 4)
        for b in range(1, 8):
            source[...] += deposit(4 * b, 4)

    @pl.when(blocks < 4)
    def _():
        source[...] = jnp.zeros_like(source)
        lax.fori_loop(0, blocks, deposit_loop, 0)

    for c, slot in ((0, 0), (1, 1), (2, 2), (4, 3), (5, 0)):
        out[c] += source[slot * ROWS : slot * ROWS + ROWS, :]


def stencil_part(gas, viscosity, out, table, speed):
    inverse = 1.0 / gas[0]
    scale = time_step / 12.0
    for k, c in enumerate((1, 2, 4, 5)):
        quotient = gas[c] * inverse
        if k < 2:
            speed[k] = quotient * scale
        hi, lo = split2(quotient)
        table[ROWS * k : ROWS * k + ROWS, 0:CZ] = hi
        table[ROWS * k : ROWS * k + ROWS, CZ : 2 * CZ] = lo
    speed[2] = gas[3] * inverse * scale
    speed[3] = viscosity[...] * scale

    def component(c, carry):
        layers = [gas[c, CY * i : CY * i + CY, :] for i in range(CX)]
        zero = jnp.zeros_like(layers[0])
        for i in range(CX):
            rows = slice(CY * i, CY * i + CY)
            x = layers[i]
            ax = [layers[i + k] if 0 <= i + k < CX else zero for k in (-2, -1, 1, 2)]
            tall = jnp.concatenate([x, zero[0:8]], axis=0)
            ra = [pltpu.roll(tall, (-k) % (CY + 8), axis=0)[0:CY] for k in (-2, -1, 1, 2)]
            az = [pltpu.roll(x, (-k) % CZ, axis=1) for k in (-2, -1, 1, 2)]
            near = (ax[1] + ax[2]) + (ra[1] + ra[2]) + (az[1] + az[2])
            far = (ax[0] + ax[3]) + (ra[0] + ra[3]) + (az[0] + az[3])
            value = x + speed[3, rows, :] * (16.0 * near - far - 90.0 * x)
            for j, n in enumerate((ax, ra, az)):
                value = value - speed[j, rows, :] * (8.0 * (n[2] - n[1]) - (n[3] - n[0]))
            out[c, rows, :] = value
        return carry

    lax.fori_loop(0, C, component, 0)


def is_last():
    a = lax.axis_index("ax")
    return (lax.rem(a, WRAP) == WRAP - 1) & (a < lax.axis_size("ax") - 1)


def soon_kernel(*refs):
    pl.when(jnp.logical_not(is_last()))(lambda: final_kernel(None, *refs))


def last_kernel(late, part, updated, gas, viscosity, table, axial_a, axial_b, radial_a, radial_b, *refs):
    given = (part, updated, gas, viscosity, table, axial_a, axial_b, radial_a, radial_b)
    pl.when(is_last())(lambda: final_kernel(late, *given, *refs[3:]))


def final_kernel(
    late, part, updated_in, gas, viscosity, table, axial_a, axial_b_in, radial_a, radial_b,
    out_hbm, drops_hbm, arrivals_hbm, out, arrivals, weights, sems,
):
    copies = [
        pltpu.make_async_copy(updated_in, drops_hbm, sems.at[0]),
        pltpu.make_async_copy(arrivals, arrivals_hbm, sems.at[1]),
    ] + [pltpu.make_async_copy(out.at[c], out_hbm.at[c], sems.at[2 + c]) for c in range(C)]
    copies[0].start()
    odd_ax, odd_rad = parity("ax"), parity("rad")
    if late is None:
        axial_b = axial_b_in
    else:
        axial_b = late
    got = []
    for odd, a, b, base in ((odd_ax, axial_a, axial_b, 192), (odd_rad, radial_a, radial_b, 96)):
        in_a, in_b = a[base : base + 8, 0:CAP], b[base : base + 8, 0:CAP]
        got.append(jnp.where(odd == 1, in_a, in_b))
        got.append(jnp.where(odd == 1, in_b, in_a))
    got = jnp.concatenate(got, axis=1)
    where = got[4:5].astype(jnp.int32)
    around = one_hot(where & (CZ - 1), CZ)
    samples = gather_block(table, around, where)
    changed, terms = evaporate(got[0:1], got[1:2], got[2:3], got[3:4], samples)
    arrivals[...] = jnp.concatenate(changed, axis=0)
    copies[1].start()
    source = deposit_block(terms, around, where)
    lane = lax.broadcasted_iota(jnp.int32, (CY, CZ), 0)
    for i in range(CX):
        rows = slice(CY * i, CY * i + CY)
        factor = viscosity[rows, :] * (time_step / 12.0)
        radial = gas[2, rows, :] / gas[0, rows, :] * (time_step / 12.0)
        for n, last in enumerate((odd_rad == 0, odd_rad == 1)):
            speed = jnp.where(last, -1.0, 1.0) * radial
            first, second = jnp.where(last, CY - 1, 0), jnp.where(last, CY - 2, 1)
            near, far = 16.0 * factor + 8.0 * speed, -(factor + speed)
            weights[2 * n, rows, :] = jnp.where(lane == first, near, jnp.where(lane == second, far, 0.0))
            weights[2 * n + 1, rows, :] = jnp.where(lane == first, far, 0.0)
    edges = []
    for message, last in ((axial_a, odd_ax == 0), (axial_b, odd_ax == 1)):
        sign = jnp.where(last, -1.0, 1.0)
        for k in range(2):
            rows = pl.ds(pl.multiple_of(jnp.where(last, (CX - 1 - k) * CY, k * CY), CY), CY)
            edges.append((message, k, rows, sign))
    for c in range(C):
        for i in range(CX):
            rows = slice(CY * i, CY * i + CY)
            at = c * CX + i
            value = part[c, rows, :]
            for n, message in enumerate((radial_a, radial_b)):
                value = value + weights[2 * n, rows, :] * message[at : at + 1, :]
                value = value + weights[2 * n + 1, rows, :] * message[48 + at : 49 + at, :]
            slot = (0, 1, 2, None, 3, 0)[c]
            if slot is not None:
                value = value + source[slot * ROWS + CY * i : slot * ROWS + CY * i + CY, :]
            out[c, rows, :] = value
        for message, k, rows, sign in edges:
            factor = viscosity[rows, :] * (time_step / 12.0)
            speed = sign * (gas[1, rows, :] / gas[0, rows, :] * (time_step / 12.0))
            near, far = 16.0 * factor + 8.0 * speed, -(factor + speed)
            if k == 0:
                change = near * message[32 * c : 32 * c + CY, :] + far * message[32 * c + CY : 32 * c + 2 * CY, :]
            else:
                change = far * message[32 * c : 32 * c + CY, :]
            out[c, rows, :] += change
        copies[2 + c].start()
    for copy in copies:
        copy.wait()


def routes(n_ax, n_rad):
    flat = lambda a, r: a * n_rad + r
    axial_a, axial_b, radial_a, radial_b, late = [], [], [], [], []
    for a in range(n_ax):
        for r in range(n_rad):
            if a + 1 < n_ax:
                up = (flat(a, r), flat(a + 1, r))
                (axial_a if a % 2 == 0 else axial_b).append(up)
                down = late if (a + 1) % WRAP == 0 else axial_a if a % 2 == 0 else axial_b
                down.append(up[::-1])
            if r + 1 < n_rad:
                out = (flat(a, r), flat(a, r + 1))
                (radial_a if r % 2 == 0 else radial_b).append(out)
                back = radial_a if r % 2 == 0 else radial_b
                back.append(out[::-1])
    return axial_a, axial_b, radial_a, radial_b, late


def body(gas_state, viscosity, droplets, drop_cells, move_lists, move_counts):
    gas = gas_state.reshape(C, ROWS, CZ)
    thick = viscosity.reshape(ROWS, CZ)
    cells = drop_cells.reshape(32, 128)
    shape = jax.ShapeDtypeStruct
    axial_a, picks, kept, gas, drops, cells = pl.pallas_call(
        prep_kernel,
        out_shape=(
            shape((208, CZ), f32),
            shape((8, 4 * CAP), f32),
            shape((32, 128), f32),
            shape((C, ROWS, CZ), f32),
            shape((4, SLOTS), f32),
            shape((32, 128), jnp.int32),
        ),
        in_specs=[HB] * 5,
        out_specs=(VM,) * 6,
        scratch_shapes=[
            pltpu.VMEM((1, 4, CAP), jnp.int32),
            pltpu.SMEM((1, 4), jnp.int32),
            pltpu.SemaphoreType.DMA((10,)),
        ],
        compiler_params=params,
        name="prep",
    )(*(pltpu.with_memory_space_constraint(x, pltpu.HBM) for x in (gas, droplets, cells, move_lists, move_counts)))
    both = ("ax", "rad")
    to_a, to_b, to_c, to_d, to_late = routes(lax.axis_size("ax"), lax.axis_size("rad"))
    came_a = lax.ppermute(axial_a, both, to_a)
    part, updated, table = shape((C, ROWS, CZ), f32), shape((4, SLOTS), f32), shape((4 * ROWS, 2 * CZ), bf16)
    speed = [pltpu.VMEM((4, ROWS, CZ), f32)]
    scratch = [pltpu.VMEM((4, 32, 128), f32), pltpu.VMEM((4, 32, 128), f32), pltpu.VMEM((4 * ROWS, CZ), f32), pltpu.VMEM((CZ, SLOTS), bf16)]
    cost = lambda flops: pl.CostEstimate(flops=flops, bytes_accessed=0, transcendentals=0)

    axial_b, radial_a, radial_b, part, table = pl.pallas_call(
        first_kernel,
        out_shape=(shape((200, CZ), f32), shape((104, CZ), f32), shape((104, CZ), f32), part, table),
        in_specs=[VM] * 3,
        out_specs=(VM,) * 5,
        scratch_shapes=speed,
        compiler_params=params,
        cost_estimate=cost(4000000000),
        name="first",
    )(gas, thick, picks)
    came_b = lax.ppermute(axial_b, both, to_b)
    came_d = lax.ppermute(radial_b, both, to_d)
    came_c = lax.ppermute(radial_a, both, to_c)
    late, part, updated = pl.pallas_call(
        early_kernel,
        out_shape=(shape((208, CZ), f32), shape(part.shape, f32), updated),
        in_specs=[VM] * 7,
        out_specs=(VM,) * 3,
        scratch_shapes=scratch,
        compiler_params=params,
        input_output_aliases={5: 1},
        cost_estimate=cost(0),
        name="early",
    )(gas, picks, drops, cells, kept, part, table)
    came_late = lax.ppermute(late, both, to_late)
    part, updated, table = pl.pallas_call(
        late_kernel,
        out_shape=tuple(shape(x.shape, x.dtype) for x in (part, updated, table)),
        in_specs=[VM] * 8,
        out_specs=(VM,) * 3,
        scratch_shapes=speed + scratch,
        compiler_params=params,
        input_output_aliases={5: 0, 6: 1, 7: 2},
        cost_estimate=cost(0),
        name="late",
    )(gas, thick, drops, cells, kept, part, updated, table)
    finals = (shape((C, ROWS, CZ), f32), shape((4, SLOTS), f32), shape((4, 4 * CAP), f32))
    scratch = [
        pltpu.VMEM((C, ROWS, CZ), f32),
        pltpu.VMEM((4, 4 * CAP), f32),
        pltpu.VMEM((4, ROWS, CZ), f32),
        pltpu.SemaphoreType.DMA((8,)),
    ]
    common = (part, updated, gas, thick, table, came_a, came_b, came_c, came_d)
    finals_soon = pl.pallas_call(
        soon_kernel,
        out_shape=finals,
        in_specs=[VM] * 9,
        out_specs=(HB,) * 3,
        scratch_shapes=scratch,
        compiler_params=params,
        cost_estimate=pl.CostEstimate(flops=4000000000, bytes_accessed=0, transcendentals=0),
        name="soon",
    )(*common)
    out, drops_out, arrivals_out = pl.pallas_call(
        last_kernel,
        out_shape=finals,
        in_specs=[VM] * 10 + [HB] * 3,
        out_specs=(HB,) * 3,
        scratch_shapes=scratch,
        compiler_params=params,
        input_output_aliases={10: 0, 11: 1, 12: 2},
        cost_estimate=pl.CostEstimate(flops=0, bytes_accessed=0, transcendentals=0),
        name="last",
    )(came_late, *common, *finals_soon)
    return out.reshape(gas_state.shape), drops_out, arrivals_out


def solution(mesh):
    placed = (
        P(None, "ax", "rad", None),
        P("ax", "rad", None),
        P(None, ("ax", "rad")),
        P(("ax", "rad")),
        P(("ax", "rad"), None, None),
        P(("ax", "rad"), None),
    )
    return jax.shard_map(
        body,
        mesh=mesh,
        in_specs=placed,
        out_specs=(P(None, "ax", "rad", None), P(None, ("ax", "rad")), P(None, ("ax", "rad"))),
        check_vma=False,
    )
```

```python
import functools

import jax
import jax.numpy as jnp
from jax import lax
from jax.experimental import pallas as pl
from jax.experimental.pallas import tpu as pltpu
from jax.sharding import PartitionSpec as P

time_step = 0.2
f32 = jnp.float32
bf16 = jnp.bfloat16
VM = pl.BlockSpec(memory_space=pltpu.VMEM)
HB = pl.BlockSpec(memory_space=pltpu.HBM)
C, CX, CY, CZ = 6, 8, 16, 512
ROWS = CX * CY
SLOTS, CAP = 4096, 64
params = pltpu.CompilerParams(vmem_limit_bytes=30 << 20)


def split2(x):
    hi = x.astype(bf16)
    return hi, (x - hi.astype(f32)).astype(bf16)


def split3(x):
    hi = x.astype(bf16)
    rest = x - hi.astype(f32)
    mid = rest.astype(bf16)
    return hi, mid, (rest - mid.astype(f32)).astype(bf16)


WRAP = 16


def parity(axis):
    return lax.rem(lax.axis_index(axis), 2)


def is_early():
    a = lax.axis_index("ax")
    return (a > 0) & (lax.rem(a, WRAP) == 0)


def prep_kernel(
    gas_in, drops_in, cells_in, lists_in, counts_in,
    axial_a, picks, kept, gas, drops, cells, lists, counts, sems,
):
    small = [
        pltpu.make_async_copy(source, target, sems.at[n])
        for n, (source, target) in enumerate(
            ((drops_in, drops), (cells_in, cells), (lists_in, lists), (counts_in, counts))
        )
    ]
    large = [pltpu.make_async_copy(gas_in.at[c], gas.at[c], sems.at[4 + c]) for c in range(C)]
    for copy in small + large:
        copy.start()
    for copy in small:
        copy.wait()
    slots = lists[0]
    entry = jnp.concatenate([slots[d : d + 1, :] for d in range(4)], axis=1)
    lane = lax.broadcasted_iota(jnp.int32, (1, CAP), 1)
    used = jnp.concatenate([(lane < counts[0, d]).astype(jnp.int32) for d in range(4)], axis=1)
    low = (lax.broadcasted_iota(jnp.int32, (128, 4 * CAP), 0) == (entry & 127)).astype(f32).astype(bf16)
    place = jnp.where(used > 0, entry >> 7, -1)
    high = (lax.broadcasted_iota(jnp.int32, (32, 4 * CAP), 0) == place).astype(f32)
    fields = []
    for f in range(4):
        fields.append(jnp.concatenate([drops[f : f + 1, 128 * s : 128 * s + 128] for s in range(32)], axis=0))
    parts = []
    for f in range(4):
        parts.extend(split3(fields[f]))
    parts.extend(split2(cells[...].astype(f32)))
    picked = jnp.dot(jnp.concatenate(parts, axis=0), low, preferred_element_type=f32)
    chosen = []
    for f in range(5):
        count = 3 if f < 4 else 2
        total = picked[96 * f : 96 * f + 32]
        for k in range(1, count):
            total = total + picked[96 * f + 32 * k : 96 * f + 32 * k + 32]
        chosen.append(jnp.sum(jnp.where(high > 0, total, 0.0), axis=0, keepdims=True))
    chosen = jnp.concatenate(chosen + [jnp.zeros((3, 4 * CAP), f32)], axis=0)
    gone = lax.dot_general(high.astype(bf16), low, (((1,), (1,)), ((), ())), preferred_element_type=f32)
    kept[...] = fields[0] * (1.0 - gone)
    picks[...] = chosen
    for copy in large:
        copy.wait()
    pack_axial(gas, picks, axial_a, parity("ax") == 0)


def pick_way(picks, axis, last):
    first = 0 if axis == "ax" else 2 * CAP
    return jnp.where(last, picks[:, first : first + CAP], picks[:, first + CAP : first + 2 * CAP])


def pack_axial(gas, picks, message, last):
    near = pl.multiple_of(jnp.where(last, (CX - 1) * CY, 0), CY)
    far = pl.multiple_of(jnp.where(last, (CX - 2) * CY, CY), CY)
    for c in range(C):
        message[32 * c : 32 * c + 16, :] = gas[c, pl.ds(near, CY), :]
        message[32 * c + 16 : 32 * c + 32, :] = gas[c, pl.ds(far, CY), :]
    message[192:200, 0:CAP] = pick_way(picks, "ax", last)


def pack_radial(gas, picks, message, last):
    near, far = jnp.where(last, CY - 1, 0), jnp.where(last, CY - 2, 1)
    for c in range(C):
        for i in range(CX):
            at = c * CX + i
            message[at : at + 1, :] = gas[c, pl.ds(i * CY + near, 1), :]
            message[48 + at : 49 + at, :] = gas[c, pl.ds(i * CY + far, 1), :]
    message[96:104, 0:CAP] = pick_way(picks, "rad", last)


def evaporate(mass, temp, axial, radial, samples):
    axial_gas, radial_gas, gas_temp, fuel = samples
    living = mass > 0.0
    safe_temp = jnp.where(living, temp, 1.0)
    root = jnp.where(living, jnp.exp(jnp.log(jnp.where(living, mass, 1.0)) * (1.0 / 3.0)), 0.0)
    balance = jnp.exp(-1.0 / safe_temp)
    slip = (axial_gas - axial) ** 2 + (radial_gas - radial) ** 2
    wind = jnp.sqrt(jnp.sqrt(1.0 + slip))
    evaporated = 0.1 * root * (jnp.log(1.0 - fuel) - jnp.log(1.0 - balance)) * (1.0 + 0.3 * wind)
    updated = (
        mass - evaporated,
        temp + 0.1 * (gas_temp - temp) - 0.5 * evaporated,
        axial + 0.2 * (axial_gas - axial),
        radial + 0.2 * (radial_gas - radial),
    )
    updated = tuple(jnp.where(living, u, 0.0) for u in updated)
    terms = (
        evaporated,
        evaporated * axial + 0.2 * mass * (axial - axial_gas),
        evaporated * radial + 0.2 * mass * (radial - radial_gas),
        evaporated * temp + 0.1 * mass * (temp - gas_temp),
    )
    return updated, terms


def one_hot(index, size):
    width = index.shape[1]
    return (lax.broadcasted_iota(jnp.int32, (size, width), 0) == index).astype(f32).astype(bf16)


def gather_block(table, around, where):
    got = jnp.dot(table[...], jnp.concatenate([around, around], axis=0), preferred_element_type=f32)
    mask = lax.broadcasted_iota(jnp.int32, (ROWS, where.shape[1]), 0) == (where >> 9)
    return [
        jnp.sum(jnp.where(mask, got[ROWS * k : ROWS * k + ROWS], 0.0), axis=0, keepdims=True) for k in range(4)
    ]


def deposit_block(terms, around, where):
    row = one_hot(where >> 9, ROWS)
    halves = [split2(t) for t in terms]
    spread = jnp.concatenate(
        [jnp.concatenate([row * h[side] for h in halves], axis=0) for side in range(2)],
        axis=1,
    )
    twice = jnp.concatenate([around, around], axis=1)
    return lax.dot_general(spread, twice, (((1,), (1,)), ((), ())), preferred_element_type=f32)


def stencil_soon():
    a, r = lax.axis_index("ax"), lax.axis_index("rad")
    near_first = ((a == 0) & (r == 1)) | ((a == 1) & (r == 1)) | ((a == 2) & (r <= 1))
    return is_early() | near_first | ((lax.rem(a, 2) == 1) & (a > 1) & (lax.rem(a, WRAP) != WRAP - 1))


def first_kernel(gas, viscosity, picks, axial_b, radial_a, radial_b, out, table, speed):
    pack_axial(gas, picks, axial_b, parity("ax") == 1)
    pack_radial(gas, picks, radial_a, parity("rad") == 0)
    pack_radial(gas, picks, radial_b, parity("rad") == 1)
    pl.when(stencil_soon())(lambda: stencil_part(gas, viscosity, out, table, speed))


def early_kernel(gas, picks, drops, cells, kept, out_in, table, late, out, drops_out, *scratch):
    @pl.when(is_early())
    def _():
        pack_axial(gas, picks, late, parity("ax") == 1)
        droplet_part(drops, cells, kept, table, out, drops_out, *scratch)


def late_kernel(gas, viscosity, drops, cells, kept, out_in, drops_in, table_in, out, drops_out, table, speed, *scratch):
    pl.when(jnp.logical_not(stencil_soon()))(lambda: stencil_part(gas, viscosity, out, table, speed))
    pl.when(jnp.logical_not(is_early()))(lambda: droplet_part(drops, cells, kept, table, out, drops_out, *scratch))


def droplet_part(drops, cells, kept, table, out, drops_out, samples, terms, source, hots):
    slot = lax.broadcasted_iota(jnp.int32, (1, SLOTS), 1)
    filled = jnp.max(jnp.where(drops[0:1, :] > 0.0, slot + 1, 0))
    blocks = lax.div(filled + 1023, 1024)

    def join(load, first, rows):
        return jnp.concatenate([load(pl.ds(first + s, 1)) for s in range(rows)], axis=1)

    def lanes(first, rows):
        return pl.ds(first * 128 if isinstance(first, int) else pl.multiple_of(first * 128, 128 * rows), 128 * rows)

    def sample(first, rows):
        where = join(lambda at: cells[at, :], first, rows)
        around = one_hot(where & (CZ - 1), CZ)
        hots[:, lanes(first, rows)] = around
        got = gather_block(table, around, where)
        for k in range(4):
            for s in range(rows):
                samples[k, pl.ds(first + s, 1), :] = got[k][:, 128 * s : 128 * s + 128]

    def deposit(first, rows):
        where = join(lambda at: cells[at, :], first, rows)
        return deposit_block(
            [join(lambda at: terms[k, at, :], first, rows) for k in range(4)], hots[:, lanes(first, rows)], where
        )

    def sample_loop(b, carry):
        sample(pl.multiple_of(8 * b, 8), 8)
        return carry

    def deposit_loop(b, carry):
        source[...] += deposit(pl.multiple_of(8 * b, 8), 8)
        return carry

    @pl.when(blocks == 4)
    def _():
        for b in range(8):
            sample(4 * b, 4)

    @pl.when(blocks < 4)
    def _():
        lax.fori_loop(0, blocks, sample_loop, 0)

    fields = [
        jnp.concatenate([drops[f : f + 1, 128 * s : 128 * s + 128] for s in range(32)], axis=0) for f in range(1, 4)
    ]
    updated, new_terms = evaporate(kept[...], *fields, [samples[k] for k in range(4)])
    for f in range(4):
        terms[f] = new_terms[f]
        for s in range(32):
            drops_out[f : f + 1, 128 * s : 128 * s + 128] = updated[f][s : s + 1, :]

    @pl.when(blocks == 4)
    def _():
        source[...] = deposit(0, 4)
        for b in range(1, 8):
            source[...] += deposit(4 * b, 4)

    @pl.when(blocks < 4)
    def _():
        source[...] = jnp.zeros_like(source)
        lax.fori_loop(0, blocks, deposit_loop, 0)

    for c, slot in ((0, 0), (1, 1), (2, 2), (4, 3), (5, 0)):
        out[c] += source[slot * ROWS : slot * ROWS + ROWS, :]


def stencil_part(gas, viscosity, out, table, speed):
    inverse = 1.0 / gas[0]
    scale = time_step / 12.0
    for k, c in enumerate((1, 2, 4, 5)):
        quotient = gas[c] * inverse
        if k < 2:
            speed[k] = quotient * scale
        hi, lo = split2(quotient)
        table[ROWS * k : ROWS * k + ROWS, 0:CZ] = hi
        table[ROWS * k : ROWS * k + ROWS, CZ : 2 * CZ] = lo
    speed[2] = gas[3] * inverse * scale
    speed[3] = viscosity[...] * scale

    def component(c, carry):
        layers = [gas[c, CY * i : CY * i + CY, :] for i in range(CX)]
        zero = jnp.zeros_like(layers[0])
        for i in range(CX):
            rows = slice(CY * i, CY * i + CY)
            x = layers[i]
            ax = [layers[i + k] if 0 <= i + k < CX else zero for k in (-2, -1, 1, 2)]
            tall = jnp.concatenate([x, zero[0:8]], axis=0)
            ra = [pltpu.roll(tall, (-k) % (CY + 8), axis=0)[0:CY] for k in (-2, -1, 1, 2)]
            az = [pltpu.roll(x, (-k) % CZ, axis=1) for k in (-2, -1, 1, 2)]
            near = (ax[1] + ax[2]) + (ra[1] + ra[2]) + (az[1] + az[2])
            far = (ax[0] + ax[3]) + (ra[0] + ra[3]) + (az[0] + az[3])
            value = x + speed[3, rows, :] * (16.0 * near - far - 90.0 * x)
            for j, n in enumerate((ax, ra, az)):
                value = value - speed[j, rows, :] * (8.0 * (n[2] - n[1]) - (n[3] - n[0]))
            out[c, rows, :] = value
        return carry

    lax.fori_loop(0, C, component, 0)


def is_last():
    a = lax.axis_index("ax")
    return (lax.rem(a, WRAP) == WRAP - 1) & (a < lax.axis_size("ax") - 1)


def soon_kernel(*refs):
    pl.when(jnp.logical_not(is_last()))(lambda: final_kernel(None, *refs))


def last_kernel(late, part, updated, gas, viscosity, table, axial_a, axial_b, radial_a, radial_b, *refs):
    given = (part, updated, gas, viscosity, table, axial_a, axial_b, radial_a, radial_b)
    pl.when(is_last())(lambda: final_kernel(late, *given, *refs[3:]))


def final_kernel(
    late, part, updated_in, gas, viscosity, table, axial_a, axial_b_in, radial_a, radial_b,
    out_hbm, drops_hbm, arrivals_hbm, out, arrivals, weights, sems,
):
    copies = [
        pltpu.make_async_copy(updated_in, drops_hbm, sems.at[0]),
        pltpu.make_async_copy(arrivals, arrivals_hbm, sems.at[1]),
    ] + [pltpu.make_async_copy(out.at[c], out_hbm.at[c], sems.at[2 + c]) for c in range(C)]
    copies[0].start()
    odd_ax, odd_rad = parity("ax"), parity("rad")
    if late is None:
        axial_b = axial_b_in
    else:
        axial_b = late
    got = []
    for odd, a, b, base in ((odd_ax, axial_a, axial_b, 192), (odd_rad, radial_a, radial_b, 96)):
        in_a, in_b = a[base : base + 8, 0:CAP], b[base : base + 8, 0:CAP]
        got.append(jnp.where(odd == 1, in_a, in_b))
        got.append(jnp.where(odd == 1, in_b, in_a))
    got = jnp.concatenate(got, axis=1)
    where = got[4:5].astype(jnp.int32)
    around = one_hot(where & (CZ - 1), CZ)
    samples = gather_block(table, around, where)
    changed, terms = evaporate(got[0:1], got[1:2], got[2:3], got[3:4], samples)
    arrivals[...] = jnp.concatenate(changed, axis=0)
    copies[1].start()
    source = deposit_block(terms, around, where)
    lane = lax.broadcasted_iota(jnp.int32, (CY, CZ), 0)
    for i in range(CX):
        rows = slice(CY * i, CY * i + CY)
        factor = viscosity[rows, :] * (time_step / 12.0)
        radial = gas[2, rows, :] / gas[0, rows, :] * (time_step / 12.0)
        for n, last in enumerate((odd_rad == 0, odd_rad == 1)):
            speed = jnp.where(last, -1.0, 1.0) * radial
            first, second = jnp.where(last, CY - 1, 0), jnp.where(last, CY - 2, 1)
            near, far = 16.0 * factor + 8.0 * speed, -(factor + speed)
            weights[2 * n, rows, :] = jnp.where(lane == first, near, jnp.where(lane == second, far, 0.0))
            weights[2 * n + 1, rows, :] = jnp.where(lane == first, far, 0.0)
    edges = []
    for message, last in ((axial_a, odd_ax == 0), (axial_b, odd_ax == 1)):
        sign = jnp.where(last, -1.0, 1.0)
        for k in range(2):
            rows = pl.ds(pl.multiple_of(jnp.where(last, (CX - 1 - k) * CY, k * CY), CY), CY)
            edges.append((message, k, rows, sign))
    for c in range(C):
        for i in range(CX):
            rows = slice(CY * i, CY * i + CY)
            at = c * CX + i
            value = part[c, rows, :]
            for n, message in enumerate((radial_a, radial_b)):
                value = value + weights[2 * n, rows, :] * message[at : at + 1, :]
                value = value + weights[2 * n + 1, rows, :] * message[48 + at : 49 + at, :]
            slot = (0, 1, 2, None, 3, 0)[c]
            if slot is not None:
                value = value + source[slot * ROWS + CY * i : slot * ROWS + CY * i + CY, :]
            out[c, rows, :] = value
        for message, k, rows, sign in edges:
            factor = viscosity[rows, :] * (time_step / 12.0)
            speed = sign * (gas[1, rows, :] / gas[0, rows, :] * (time_step / 12.0))
            near, far = 16.0 * factor + 8.0 * speed, -(factor + speed)
            if k == 0:
                change = near * message[32 * c : 32 * c + CY, :] + far * message[32 * c + CY : 32 * c + 2 * CY, :]
            else:
                change = far * message[32 * c : 32 * c + CY, :]
            out[c, rows, :] += change
        copies[2 + c].start()
    for copy in copies:
        copy.wait()


def routes(n_ax, n_rad):
    flat = lambda a, r: a * n_rad + r
    axial_a, axial_b, radial_a, radial_b, late = [], [], [], [], []
    for a in range(n_ax):
        for r in range(n_rad):
            if a + 1 < n_ax:
                up = (flat(a, r), flat(a + 1, r))
                (axial_a if a % 2 == 0 else axial_b).append(up)
                down = late if (a + 1) % WRAP == 0 else axial_a if a % 2 == 0 else axial_b
                down.append(up[::-1])
            if r + 1 < n_rad:
                out = (flat(a, r), flat(a, r + 1))
                (radial_a if r % 2 == 0 else radial_b).append(out)
                back = radial_a if r % 2 == 0 else radial_b
                back.append(out[::-1])
    return axial_a, axial_b, radial_a, radial_b, late


def body(gas_state, viscosity, droplets, drop_cells, move_lists, move_counts):
    gas = gas_state.reshape(C, ROWS, CZ)
    thick = viscosity.reshape(ROWS, CZ)
    cells = drop_cells.reshape(32, 128)
    shape = jax.ShapeDtypeStruct
    axial_a, picks, kept, gas, drops, cells = pl.pallas_call(
        prep_kernel,
        out_shape=(
            shape((208, CZ), f32),
            shape((8, 4 * CAP), f32),
            shape((32, 128), f32),
            shape((C, ROWS, CZ), f32),
            shape((4, SLOTS), f32),
            shape((32, 128), jnp.int32),
        ),
        in_specs=[HB] * 5,
        out_specs=(VM,) * 6,
        scratch_shapes=[
            pltpu.VMEM((1, 4, CAP), jnp.int32),
            pltpu.SMEM((1, 4), jnp.int32),
            pltpu.SemaphoreType.DMA((10,)),
        ],
        compiler_params=params,
        name="prep",
    )(*(pltpu.with_memory_space_constraint(x, pltpu.HBM) for x in (gas, droplets, cells, move_lists, move_counts)))
    both = ("ax", "rad")
    to_a, to_b, to_c, to_d, to_late = routes(lax.axis_size("ax"), lax.axis_size("rad"))
    came_a = lax.ppermute(axial_a, both, to_a)
    part, updated, table = shape((C, ROWS, CZ), f32), shape((4, SLOTS), f32), shape((4 * ROWS, 2 * CZ), bf16)
    speed = [pltpu.VMEM((4, ROWS, CZ), f32)]
    scratch = [pltpu.VMEM((4, 32, 128), f32), pltpu.VMEM((4, 32, 128), f32), pltpu.VMEM((4 * ROWS, CZ), f32), pltpu.VMEM((CZ, SLOTS), bf16)]
    cost = lambda flops: pl.CostEstimate(flops=flops, bytes_accessed=0, transcendentals=0)

    axial_b, radial_a, radial_b, part, table = pl.pallas_call(
        first_kernel,
        out_shape=(shape((200, CZ), f32), shape((104, CZ), f32), shape((104, CZ), f32), part, table),
        in_specs=[VM] * 3,
        out_specs=(VM,) * 5,
        scratch_shapes=speed,
        compiler_params=params,
        cost_estimate=cost(4000000000),
        name="first",
    )(gas, thick, picks)
    came_b = lax.ppermute(axial_b, both, to_b)
    came_d = lax.ppermute(radial_b, both, to_d)
    came_c = lax.ppermute(radial_a, both, to_c)
    late, part, updated = pl.pallas_call(
        early_kernel,
        out_shape=(shape((208, CZ), f32), shape(part.shape, f32), updated),
        in_specs=[VM] * 7,
        out_specs=(VM,) * 3,
        scratch_shapes=scratch,
        compiler_params=params,
        input_output_aliases={5: 1},
        cost_estimate=cost(4000000000),
        name="early",
    )(gas, picks, drops, cells, kept, part, table)
    came_late = lax.ppermute(late, both, to_late)
    part, updated, table = pl.pallas_call(
        late_kernel,
        out_shape=tuple(shape(x.shape, x.dtype) for x in (part, updated, table)),
        in_specs=[VM] * 8,
        out_specs=(VM,) * 3,
        scratch_shapes=speed + scratch,
        compiler_params=params,
        input_output_aliases={5: 0, 6: 1, 7: 2},
        cost_estimate=cost(0),
        name="late",
    )(gas, thick, drops, cells, kept, part, updated, table)
    finals = (shape((C, ROWS, CZ), f32), shape((4, SLOTS), f32), shape((4, 4 * CAP), f32))
    scratch = [
        pltpu.VMEM((C, ROWS, CZ), f32),
        pltpu.VMEM((4, 4 * CAP), f32),
        pltpu.VMEM((4, ROWS, CZ), f32),
        pltpu.SemaphoreType.DMA((8,)),
    ]
    common = (part, updated, gas, thick, table, came_a, came_b, came_c, came_d)
    finals_soon = pl.pallas_call(
        soon_kernel,
        out_shape=finals,
        in_specs=[VM] * 9,
        out_specs=(HB,) * 3,
        scratch_shapes=scratch,
        compiler_params=params,
        cost_estimate=pl.CostEstimate(flops=0, bytes_accessed=0, transcendentals=0),
        name="soon",
    )(*common)
    out, drops_out, arrivals_out = pl.pallas_call(
        last_kernel,
        out_shape=finals,
        in_specs=[VM] * 10 + [HB] * 3,
        out_specs=(HB,) * 3,
        scratch_shapes=scratch,
        compiler_params=params,
        input_output_aliases={10: 0, 11: 1, 12: 2},
        cost_estimate=pl.CostEstimate(flops=0, bytes_accessed=0, transcendentals=0),
        name="last",
    )(came_late, *common, *finals_soon)
    return out.reshape(gas_state.shape), drops_out, arrivals_out


def solution(mesh):
    placed = (
        P(None, "ax", "rad", None),
        P("ax", "rad", None),
        P(None, ("ax", "rad")),
        P(("ax", "rad")),
        P(("ax", "rad"), None, None),
        P(("ax", "rad"), None),
    )
    return jax.shard_map(
        body,
        mesh=mesh,
        in_specs=placed,
        out_specs=(P(None, "ax", "rad", None), P(None, ("ax", "rad")), P(None, ("ax", "rad"))),
        check_vma=False,
    )
```

```python
import functools

import jax
import jax.numpy as jnp
from jax import lax
from jax.experimental import pallas as pl
from jax.experimental.pallas import tpu as pltpu
from jax.sharding import PartitionSpec as P

time_step = 0.2
f32 = jnp.float32
bf16 = jnp.bfloat16
VM = pl.BlockSpec(memory_space=pltpu.VMEM)
HB = pl.BlockSpec(memory_space=pltpu.HBM)
C, CX, CY, CZ = 6, 8, 16, 512
ROWS = CX * CY
SLOTS, CAP = 4096, 64
params = pltpu.CompilerParams(vmem_limit_bytes=30 << 20)


def split2(x):
    hi = x.astype(bf16)
    return hi, (x - hi.astype(f32)).astype(bf16)


def split3(x):
    hi = x.astype(bf16)
    rest = x - hi.astype(f32)
    mid = rest.astype(bf16)
    return hi, mid, (rest - mid.astype(f32)).astype(bf16)


WRAP = 16


def parity(axis):
    return lax.rem(lax.axis_index(axis), 2)


def is_early():
    a = lax.axis_index("ax")
    return (a > 0) & (lax.rem(a, WRAP) == 0)


def prep_kernel(
    gas_in, drops_in, cells_in, lists_in, counts_in,
    axial_a, picks, kept, gas, drops, cells, lists, counts, sems,
):
    small = [
        pltpu.make_async_copy(source, target, sems.at[n])
        for n, (source, target) in enumerate(
            ((drops_in, drops), (cells_in, cells), (lists_in, lists), (counts_in, counts))
        )
    ]
    large = [pltpu.make_async_copy(gas_in.at[c], gas.at[c], sems.at[4 + c]) for c in range(C)]
    for copy in small + large:
        copy.start()
    for copy in small:
        copy.wait()
    slots = lists[0]
    entry = jnp.concatenate([slots[d : d + 1, :] for d in range(4)], axis=1)
    lane = lax.broadcasted_iota(jnp.int32, (1, CAP), 1)
    used = jnp.concatenate([(lane < counts[0, d]).astype(jnp.int32) for d in range(4)], axis=1)
    low = (lax.broadcasted_iota(jnp.int32, (128, 4 * CAP), 0) == (entry & 127)).astype(f32).astype(bf16)
    place = jnp.where(used > 0, entry >> 7, -1)
    high = (lax.broadcasted_iota(jnp.int32, (32, 4 * CAP), 0) == place).astype(f32)
    fields = []
    for f in range(4):
        fields.append(jnp.concatenate([drops[f : f + 1, 128 * s : 128 * s + 128] for s in range(32)], axis=0))
    parts = []
    for f in range(4):
        parts.extend(split3(fields[f]))
    parts.extend(split2(cells[...].astype(f32)))
    picked = jnp.dot(jnp.concatenate(parts, axis=0), low, preferred_element_type=f32)
    chosen = []
    for f in range(5):
        count = 3 if f < 4 else 2
        total = picked[96 * f : 96 * f + 32]
        for k in range(1, count):
            total = total + picked[96 * f + 32 * k : 96 * f + 32 * k + 32]
        chosen.append(jnp.sum(jnp.where(high > 0, total, 0.0), axis=0, keepdims=True))
    chosen = jnp.concatenate(chosen + [jnp.zeros((3, 4 * CAP), f32)], axis=0)
    gone = lax.dot_general(high.astype(bf16), low, (((1,), (1,)), ((), ())), preferred_element_type=f32)
    kept[...] = fields[0] * (1.0 - gone)
    picks[...] = chosen
    for copy in large:
        copy.wait()
    pack_axial(gas, picks, axial_a, parity("ax") == 0)


def pick_way(picks, axis, last):
    first = 0 if axis == "ax" else 2 * CAP
    return jnp.where(last, picks[:, first : first + CAP], picks[:, first + CAP : first + 2 * CAP])


def pack_axial(gas, picks, message, last):
    near = pl.multiple_of(jnp.where(last, (CX - 1) * CY, 0), CY)
    far = pl.multiple_of(jnp.where(last, (CX - 2) * CY, CY), CY)
    for c in range(C):
        message[32 * c : 32 * c + 16, :] = gas[c, pl.ds(near, CY), :]
        message[32 * c + 16 : 32 * c + 32, :] = gas[c, pl.ds(far, CY), :]
    message[192:200, 0:CAP] = pick_way(picks, "ax", last)


def pack_radial(gas, picks, message, last):
    near, far = jnp.where(last, CY - 1, 0), jnp.where(last, CY - 2, 1)
    for c in range(C):
        for i in range(CX):
            at = c * CX + i
            message[at : at + 1, :] = gas[c, pl.ds(i * CY + near, 1), :]
            message[48 + at : 49 + at, :] = gas[c, pl.ds(i * CY + far, 1), :]
    message[96:104, 0:CAP] = pick_way(picks, "rad", last)


def evaporate(mass, temp, axial, radial, samples):
    axial_gas, radial_gas, gas_temp, fuel = samples
    living = mass > 0.0
    safe_temp = jnp.where(living, temp, 1.0)
    root = jnp.where(living, jnp.exp(jnp.log(jnp.where(living, mass, 1.0)) * (1.0 / 3.0)), 0.0)
    balance = jnp.exp(-1.0 / safe_temp)
    slip = (axial_gas - axial) ** 2 + (radial_gas - radial) ** 2
    wind = jnp.sqrt(jnp.sqrt(1.0 + slip))
    evaporated = 0.1 * root * (jnp.log(1.0 - fuel) - jnp.log(1.0 - balance)) * (1.0 + 0.3 * wind)
    updated = (
        mass - evaporated,
        temp + 0.1 * (gas_temp - temp) - 0.5 * evaporated,
        axial + 0.2 * (axial_gas - axial),
        radial + 0.2 * (radial_gas - radial),
    )
    updated = tuple(jnp.where(living, u, 0.0) for u in updated)
    terms = (
        evaporated,
        evaporated * axial + 0.2 * mass * (axial - axial_gas),
        evaporated * radial + 0.2 * mass * (radial - radial_gas),
        evaporated * temp + 0.1 * mass * (temp - gas_temp),
    )
    return updated, terms


def one_hot(index, size):
    width = index.shape[1]
    return (lax.broadcasted_iota(jnp.int32, (size, width), 0) == index).astype(f32).astype(bf16)


def gather_block(table, around, where):
    got = jnp.dot(table[...], jnp.concatenate([around, around], axis=0), preferred_element_type=f32)
    mask = lax.broadcasted_iota(jnp.int32, (ROWS, where.shape[1]), 0) == (where >> 9)
    return [
        jnp.sum(jnp.where(mask, got[ROWS * k : ROWS * k + ROWS], 0.0), axis=0, keepdims=True) for k in range(4)
    ]


def deposit_block(terms, around, where):
    row = one_hot(where >> 9, ROWS)
    halves = [split2(t) for t in terms]
    spread = jnp.concatenate(
        [jnp.concatenate([row * h[side] for h in halves], axis=0) for side in range(2)],
        axis=1,
    )
    twice = jnp.concatenate([around, around], axis=1)
    return lax.dot_general(spread, twice, (((1,), (1,)), ((), ())), preferred_element_type=f32)


def stencil_soon():
    a, r = lax.axis_index("ax"), lax.axis_index("rad")
    near_first = ((a == 0) & (r == 1)) | ((a == 1) & (r == 1)) | ((a == 2) & (r <= 1))
    return is_early() | near_first | ((lax.rem(a, 2) == 1) & (a > 1) & (lax.rem(a, WRAP) != WRAP - 1))


def first_kernel(gas, viscosity, picks, axial_b, radial_a, radial_b, out, table, speed):
    pack_axial(gas, picks, axial_b, parity("ax") == 1)
    pack_radial(gas, picks, radial_a, parity("rad") == 0)
    pack_radial(gas, picks, radial_b, parity("rad") == 1)
    pl.when(stencil_soon())(lambda: stencil_part(gas, viscosity, out, table, speed))


def early_kernel(gas, picks, drops, cells, kept, out_in, table, late, out, drops_out, *scratch):
    @pl.when(is_early())
    def _():
        pack_axial(gas, picks, late, parity("ax") == 1)
        droplet_part(drops, cells, kept, table, out, drops_out, *scratch)


def late_kernel(gas, viscosity, drops, cells, kept, out_in, drops_in, table_in, out, drops_out, table, speed, *scratch):
    pl.when(jnp.logical_not(stencil_soon()))(lambda: stencil_part(gas, viscosity, out, table, speed))
    pl.when(jnp.logical_not(is_early()))(lambda: droplet_part(drops, cells, kept, table, out, drops_out, *scratch))


def droplet_part(drops, cells, kept, table, out, drops_out, samples, terms, source, hots):
    slot = lax.broadcasted_iota(jnp.int32, (1, SLOTS), 1)
    filled = jnp.max(jnp.where(drops[0:1, :] > 0.0, slot + 1, 0))
    blocks = lax.div(filled + 1023, 1024)

    def join(load, first, rows):
        return jnp.concatenate([load(pl.ds(first + s, 1)) for s in range(rows)], axis=1)

    def lanes(first, rows):
        return pl.ds(first * 128 if isinstance(first, int) else pl.multiple_of(first * 128, 128 * rows), 128 * rows)

    def sample(first, rows):
        where = join(lambda at: cells[at, :], first, rows)
        around = one_hot(where & (CZ - 1), CZ)
        hots[:, lanes(first, rows)] = around
        got = gather_block(table, around, where)
        for k in range(4):
            for s in range(rows):
                samples[k, pl.ds(first + s, 1), :] = got[k][:, 128 * s : 128 * s + 128]

    def deposit(first, rows):
        where = join(lambda at: cells[at, :], first, rows)
        return deposit_block(
            [join(lambda at: terms[k, at, :], first, rows) for k in range(4)], hots[:, lanes(first, rows)], where
        )

    def sample_loop(b, carry):
        sample(pl.multiple_of(8 * b, 8), 8)
        return carry

    def deposit_loop(b, carry):
        source[...] += deposit(pl.multiple_of(8 * b, 8), 8)
        return carry

    @pl.when(blocks == 4)
    def _():
        for b in range(8):
            sample(4 * b, 4)

    @pl.when(blocks < 4)
    def _():
        lax.fori_loop(0, blocks, sample_loop, 0)

    fields = [
        jnp.concatenate([drops[f : f + 1, 128 * s : 128 * s + 128] for s in range(32)], axis=0) for f in range(1, 4)
    ]
    updated, new_terms = evaporate(kept[...], *fields, [samples[k] for k in range(4)])
    for f in range(4):
        terms[f] = new_terms[f]
        for s in range(32):
            drops_out[f : f + 1, 128 * s : 128 * s + 128] = updated[f][s : s + 1, :]

    @pl.when(blocks == 4)
    def _():
        source[...] = deposit(0, 4)
        for b in range(1, 8):
            source[...] += deposit(4 * b, 4)

    @pl.when(blocks < 4)
    def _():
        source[...] = jnp.zeros_like(source)
        lax.fori_loop(0, blocks, deposit_loop, 0)

    for c, slot in ((0, 0), (1, 1), (2, 2), (4, 3), (5, 0)):
        out[c] += source[slot * ROWS : slot * ROWS + ROWS, :]


def stencil_part(gas, viscosity, out, table, speed):
    inverse = 1.0 / gas[0]
    scale = time_step / 12.0
    for k, c in enumerate((1, 2, 4, 5)):
        quotient = gas[c] * inverse
        if k < 2:
            speed[k] = quotient * scale
        hi, lo = split2(quotient)
        table[ROWS * k : ROWS * k + ROWS, 0:CZ] = hi
        table[ROWS * k : ROWS * k + ROWS, CZ : 2 * CZ] = lo
    speed[2] = gas[3] * inverse * scale
    speed[3] = viscosity[...] * scale

    def component(c, carry):
        layers = [gas[c, CY * i : CY * i + CY, :] for i in range(CX)]
        zero = jnp.zeros_like(layers[0])
        for i in range(CX):
            rows = slice(CY * i, CY * i + CY)
            x = layers[i]
            ax = [layers[i + k] if 0 <= i + k < CX else zero for k in (-2, -1, 1, 2)]
            tall = jnp.concatenate([x, zero[0:8]], axis=0)
            ra = [pltpu.roll(tall, (-k) % (CY + 8), axis=0)[0:CY] for k in (-2, -1, 1, 2)]
            az = [pltpu.roll(x, (-k) % CZ, axis=1) for k in (-2, -1, 1, 2)]
            near = (ax[1] + ax[2]) + (ra[1] + ra[2]) + (az[1] + az[2])
            far = (ax[0] + ax[3]) + (ra[0] + ra[3]) + (az[0] + az[3])
            value = x + speed[3, rows, :] * (16.0 * near - far - 90.0 * x)
            for j, n in enumerate((ax, ra, az)):
                value = value - speed[j, rows, :] * (8.0 * (n[2] - n[1]) - (n[3] - n[0]))
            out[c, rows, :] = value
        return carry

    lax.fori_loop(0, C, component, 0)


def is_last():
    a = lax.axis_index("ax")
    return (lax.rem(a, WRAP) == WRAP - 1) & (a < lax.axis_size("ax") - 1)


def soon_kernel(*refs):
    pl.when(jnp.logical_not(is_last()))(lambda: final_kernel(None, *refs))


def last_kernel(late, part, updated, gas, viscosity, table, axial_a, axial_b, radial_a, radial_b, *refs):
    given = (part, updated, gas, viscosity, table, axial_a, axial_b, radial_a, radial_b)
    pl.when(is_last())(lambda: final_kernel(late, *given, *refs[3:]))


def final_kernel(
    late, part, updated_in, gas, viscosity, table, axial_a, axial_b_in, radial_a, radial_b,
    out_hbm, drops_hbm, arrivals_hbm, out, arrivals, weights, sems,
):
    copies = [
        pltpu.make_async_copy(updated_in, drops_hbm, sems.at[0]),
        pltpu.make_async_copy(arrivals, arrivals_hbm, sems.at[1]),
    ] + [pltpu.make_async_copy(out.at[c], out_hbm.at[c], sems.at[2 + c]) for c in range(C)]
    copies[0].start()
    odd_ax, odd_rad = parity("ax"), parity("rad")
    if late is None:
        axial_b = axial_b_in
    else:
        axial_b = late
    got = []
    for odd, a, b, base in ((odd_ax, axial_a, axial_b, 192), (odd_rad, radial_a, radial_b, 96)):
        in_a, in_b = a[base : base + 8, 0:CAP], b[base : base + 8, 0:CAP]
        got.append(jnp.where(odd == 1, in_a, in_b))
        got.append(jnp.where(odd == 1, in_b, in_a))
    got = jnp.concatenate(got, axis=1)
    where = got[4:5].astype(jnp.int32)
    around = one_hot(where & (CZ - 1), CZ)
    samples = gather_block(table, around, where)
    changed, terms = evaporate(got[0:1], got[1:2], got[2:3], got[3:4], samples)
    arrivals[...] = jnp.concatenate(changed, axis=0)
    copies[1].start()
    source = deposit_block(terms, around, where)
    lane = lax.broadcasted_iota(jnp.int32, (CY, CZ), 0)
    for i in range(CX):
        rows = slice(CY * i, CY * i + CY)
        factor = viscosity[rows, :] * (time_step / 12.0)
        radial = gas[2, rows, :] / gas[0, rows, :] * (time_step / 12.0)
        for n, last in enumerate((odd_rad == 0, odd_rad == 1)):
            speed = jnp.where(last, -1.0, 1.0) * radial
            first, second = jnp.where(last, CY - 1, 0), jnp.where(last, CY - 2, 1)
            near, far = 16.0 * factor + 8.0 * speed, -(factor + speed)
            weights[2 * n, rows, :] = jnp.where(lane == first, near, jnp.where(lane == second, far, 0.0))
            weights[2 * n + 1, rows, :] = jnp.where(lane == first, far, 0.0)
    edges = []
    for message, last in ((axial_a, odd_ax == 0), (axial_b, odd_ax == 1)):
        sign = jnp.where(last, -1.0, 1.0)
        for k in range(2):
            rows = pl.ds(pl.multiple_of(jnp.where(last, (CX - 1 - k) * CY, k * CY), CY), CY)
            edges.append((message, k, rows, sign))
    for c in range(C):
        for i in range(CX):
            rows = slice(CY * i, CY * i + CY)
            at = c * CX + i
            value = part[c, rows, :]
            for n, message in enumerate((radial_a, radial_b)):
                value = value + weights[2 * n, rows, :] * message[at : at + 1, :]
                value = value + weights[2 * n + 1, rows, :] * message[48 + at : 49 + at, :]
            slot = (0, 1, 2, None, 3, 0)[c]
            if slot is not None:
                value = value + source[slot * ROWS + CY * i : slot * ROWS + CY * i + CY, :]
            out[c, rows, :] = value
        for message, k, rows, sign in edges:
            factor = viscosity[rows, :] * (time_step / 12.0)
            speed = sign * (gas[1, rows, :] / gas[0, rows, :] * (time_step / 12.0))
            near, far = 16.0 * factor + 8.0 * speed, -(factor + speed)
            if k == 0:
                change = near * message[32 * c : 32 * c + CY, :] + far * message[32 * c + CY : 32 * c + 2 * CY, :]
            else:
                change = far * message[32 * c : 32 * c + CY, :]
            out[c, rows, :] += change
        copies[2 + c].start()
    for copy in copies:
        copy.wait()


def routes(n_ax, n_rad):
    flat = lambda a, r: a * n_rad + r
    axial_a, axial_b, radial_a, radial_b, late = [], [], [], [], []
    for a in range(n_ax):
        for r in range(n_rad):
            if a + 1 < n_ax:
                up = (flat(a, r), flat(a + 1, r))
                (axial_a if a % 2 == 0 else axial_b).append(up)
                down = late if (a + 1) % WRAP == 0 else axial_a if a % 2 == 0 else axial_b
                down.append(up[::-1])
            if r + 1 < n_rad:
                out = (flat(a, r), flat(a, r + 1))
                (radial_a if r % 2 == 0 else radial_b).append(out)
                back = radial_a if r % 2 == 0 else radial_b
                back.append(out[::-1])
    return axial_a, axial_b, radial_a, radial_b, late


def body(gas_state, viscosity, droplets, drop_cells, move_lists, move_counts):
    gas = gas_state.reshape(C, ROWS, CZ)
    thick = viscosity.reshape(ROWS, CZ)
    cells = drop_cells.reshape(32, 128)
    shape = jax.ShapeDtypeStruct
    axial_a, picks, kept, gas, drops, cells = pl.pallas_call(
        prep_kernel,
        out_shape=(
            shape((200, CZ), f32),
            shape((8, 4 * CAP), f32),
            shape((32, 128), f32),
            shape((C, ROWS, CZ), f32),
            shape((4, SLOTS), f32),
            shape((32, 128), jnp.int32),
        ),
        in_specs=[HB] * 5,
        out_specs=(VM,) * 6,
        scratch_shapes=[
            pltpu.VMEM((1, 4, CAP), jnp.int32),
            pltpu.SMEM((1, 4), jnp.int32),
            pltpu.SemaphoreType.DMA((10,)),
        ],
        compiler_params=params,
        name="prep",
    )(*(pltpu.with_memory_space_constraint(x, pltpu.HBM) for x in (gas, droplets, cells, move_lists, move_counts)))
    both = ("ax", "rad")
    to_a, to_b, to_c, to_d, to_late = routes(lax.axis_size("ax"), lax.axis_size("rad"))
    came_a = lax.ppermute(axial_a, both, to_a)
    part, updated, table = shape((C, ROWS, CZ), f32), shape((4, SLOTS), f32), shape((4 * ROWS, 2 * CZ), bf16)
    speed = [pltpu.VMEM((4, ROWS, CZ), f32)]
    scratch = [pltpu.VMEM((4, 32, 128), f32), pltpu.VMEM((4, 32, 128), f32), pltpu.VMEM((4 * ROWS, CZ), f32), pltpu.VMEM((CZ, SLOTS), bf16)]
    cost = lambda flops: pl.CostEstimate(flops=flops, bytes_accessed=0, transcendentals=0)

    axial_b, radial_a, radial_b, part, table = pl.pallas_call(
        first_kernel,
        out_shape=(shape((200, CZ), f32), shape((104, CZ), f32), shape((104, CZ), f32), part, table),
        in_specs=[VM] * 3,
        out_specs=(VM,) * 5,
        scratch_shapes=speed,
        compiler_params=params,
        cost_estimate=cost(4000000000),
        name="first",
    )(gas, thick, picks)
    came_b = lax.ppermute(axial_b, both, to_b)
    came_d = lax.ppermute(radial_b, both, to_d)
    came_c = lax.ppermute(radial_a, both, to_c)
    late, part, updated = pl.pallas_call(
        early_kernel,
        out_shape=(shape((200, CZ), f32), shape(part.shape, f32), updated),
        in_specs=[VM] * 7,
        out_specs=(VM,) * 3,
        scratch_shapes=scratch,
        compiler_params=params,
        input_output_aliases={5: 1},
        cost_estimate=cost(0),
        name="early",
    )(gas, picks, drops, cells, kept, part, table)
    came_late = lax.ppermute(late, both, to_late)
    part, updated, table = pl.pallas_call(
        late_kernel,
        out_shape=tuple(shape(x.shape, x.dtype) for x in (part, updated, table)),
        in_specs=[VM] * 8,
        out_specs=(VM,) * 3,
        scratch_shapes=speed + scratch,
        compiler_params=params,
        input_output_aliases={5: 0, 6: 1, 7: 2},
        cost_estimate=cost(0),
        name="late",
    )(gas, thick, drops, cells, kept, part, updated, table)
    finals = (shape((C, ROWS, CZ), f32), shape((4, SLOTS), f32), shape((4, 4 * CAP), f32))
    scratch = [
        pltpu.VMEM((C, ROWS, CZ), f32),
        pltpu.VMEM((4, 4 * CAP), f32),
        pltpu.VMEM((4, ROWS, CZ), f32),
        pltpu.SemaphoreType.DMA((8,)),
    ]
    common = (part, updated, gas, thick, table, came_a, came_b, came_c, came_d)
    finals_soon = pl.pallas_call(
        soon_kernel,
        out_shape=finals,
        in_specs=[VM] * 9,
        out_specs=(HB,) * 3,
        scratch_shapes=scratch,
        compiler_params=params,
        cost_estimate=pl.CostEstimate(flops=4000000000, bytes_accessed=0, transcendentals=0),
        name="soon",
    )(*common)
    out, drops_out, arrivals_out = pl.pallas_call(
        last_kernel,
        out_shape=finals,
        in_specs=[VM] * 10 + [HB] * 3,
        out_specs=(HB,) * 3,
        scratch_shapes=scratch,
        compiler_params=params,
        input_output_aliases={10: 0, 11: 1, 12: 2},
        cost_estimate=pl.CostEstimate(flops=0, bytes_accessed=0, transcendentals=0),
        name="last",
    )(came_late, *common, *finals_soon)
    return out.reshape(gas_state.shape), drops_out, arrivals_out


def solution(mesh):
    placed = (
        P(None, "ax", "rad", None),
        P("ax", "rad", None),
        P(None, ("ax", "rad")),
        P(("ax", "rad")),
        P(("ax", "rad"), None, None),
        P(("ax", "rad"), None),
    )
    return jax.shard_map(
        body,
        mesh=mesh,
        in_specs=placed,
        out_specs=(P(None, "ax", "rad", None), P(None, ("ax", "rad")), P(None, ("ax", "rad"))),
        check_vma=False,
    )
```

```python
import functools

import jax
import jax.numpy as jnp
from jax import lax
from jax.experimental import pallas as pl
from jax.experimental.pallas import tpu as pltpu
from jax.sharding import PartitionSpec as P

time_step = 0.2
f32 = jnp.float32
bf16 = jnp.bfloat16
VM = pl.BlockSpec(memory_space=pltpu.VMEM)
HB = pl.BlockSpec(memory_space=pltpu.HBM)
C, CX, CY, CZ = 6, 8, 16, 512
ROWS = CX * CY
SLOTS, CAP = 4096, 64
params = pltpu.CompilerParams(vmem_limit_bytes=30 << 20)


def split2(x):
    hi = x.astype(bf16)
    return hi, (x - hi.astype(f32)).astype(bf16)


def split3(x):
    hi = x.astype(bf16)
    rest = x - hi.astype(f32)
    mid = rest.astype(bf16)
    return hi, mid, (rest - mid.astype(f32)).astype(bf16)


WRAP = 16


def parity(axis):
    return lax.rem(lax.axis_index(axis), 2)


def is_early():
    a = lax.axis_index("ax")
    return (a > 0) & (lax.rem(a, WRAP) == 0)


def prep_kernel(
    gas_in, drops_in, cells_in, lists_in, counts_in,
    axial_a, picks, kept, gas, drops, cells, lists, counts, sems,
):
    small = [
        pltpu.make_async_copy(source, target, sems.at[n])
        for n, (source, target) in enumerate(
            ((drops_in, drops), (cells_in, cells), (lists_in, lists), (counts_in, counts))
        )
    ]
    large = [pltpu.make_async_copy(gas_in.at[c], gas.at[c], sems.at[4 + c]) for c in range(C)]
    for copy in small + large:
        copy.start()
    for copy in small:
        copy.wait()
    slots = lists[0]
    entry = jnp.concatenate([slots[d : d + 1, :] for d in range(4)], axis=1)
    lane = lax.broadcasted_iota(jnp.int32, (1, CAP), 1)
    used = jnp.concatenate([(lane < counts[0, d]).astype(jnp.int32) for d in range(4)], axis=1)
    low = (lax.broadcasted_iota(jnp.int32, (128, 4 * CAP), 0) == (entry & 127)).astype(f32).astype(bf16)
    place = jnp.where(used > 0, entry >> 7, -1)
    high = (lax.broadcasted_iota(jnp.int32, (32, 4 * CAP), 0) == place).astype(f32)
    fields = []
    for f in range(4):
        fields.append(jnp.concatenate([drops[f : f + 1, 128 * s : 128 * s + 128] for s in range(32)], axis=0))
    parts = []
    for f in range(4):
        parts.extend(split3(fields[f]))
    parts.extend(split2(cells[...].astype(f32)))
    picked = jnp.dot(jnp.concatenate(parts, axis=0), low, preferred_element_type=f32)
    chosen = []
    for f in range(5):
        count = 3 if f < 4 else 2
        total = picked[96 * f : 96 * f + 32]
        for k in range(1, count):
            total = total + picked[96 * f + 32 * k : 96 * f + 32 * k + 32]
        chosen.append(jnp.sum(jnp.where(high > 0, total, 0.0), axis=0, keepdims=True))
    chosen = jnp.concatenate(chosen + [jnp.zeros((3, 4 * CAP), f32)], axis=0)
    gone = lax.dot_general(high.astype(bf16), low, (((1,), (1,)), ((), ())), preferred_element_type=f32)
    kept[...] = fields[0] * (1.0 - gone)
    picks[...] = chosen
    for copy in large:
        copy.wait()
    pack_axial(gas, picks, axial_a, parity("ax") == 0)


def pick_way(picks, axis, last):
    first = 0 if axis == "ax" else 2 * CAP
    return jnp.where(last, picks[:, first : first + CAP], picks[:, first + CAP : first + 2 * CAP])


def pack_axial(gas, picks, message, last):
    near = pl.multiple_of(jnp.where(last, (CX - 1) * CY, 0), CY)
    far = pl.multiple_of(jnp.where(last, (CX - 2) * CY, CY), CY)
    for c in range(C):
        message[32 * c : 32 * c + 16, :] = gas[c, pl.ds(near, CY), :]
        message[32 * c + 16 : 32 * c + 32, :] = gas[c, pl.ds(far, CY), :]
    message[192:200, 0:CAP] = pick_way(picks, "ax", last)


def pack_radial(gas, picks, message, last):
    near, far = jnp.where(last, CY - 1, 0), jnp.where(last, CY - 2, 1)
    for c in range(C):
        for i in range(CX):
            at = c * CX + i
            message[at : at + 1, :] = gas[c, pl.ds(i * CY + near, 1), :]
            message[48 + at : 49 + at, :] = gas[c, pl.ds(i * CY + far, 1), :]
    message[96:104, 0:CAP] = pick_way(picks, "rad", last)


def evaporate(mass, temp, axial, radial, samples):
    axial_gas, radial_gas, gas_temp, fuel = samples
    living = mass > 0.0
    safe_temp = jnp.where(living, temp, 1.0)
    root = jnp.where(living, jnp.exp(jnp.log(jnp.where(living, mass, 1.0)) * (1.0 / 3.0)), 0.0)
    balance = jnp.exp(-1.0 / safe_temp)
    slip = (axial_gas - axial) ** 2 + (radial_gas - radial) ** 2
    wind = jnp.sqrt(jnp.sqrt(1.0 + slip))
    evaporated = 0.1 * root * (jnp.log(1.0 - fuel) - jnp.log(1.0 - balance)) * (1.0 + 0.3 * wind)
    updated = (
        mass - evaporated,
        temp + 0.1 * (gas_temp - temp) - 0.5 * evaporated,
        axial + 0.2 * (axial_gas - axial),
        radial + 0.2 * (radial_gas - radial),
    )
    updated = tuple(jnp.where(living, u, 0.0) for u in updated)
    terms = (
        evaporated,
        evaporated * axial + 0.2 * mass * (axial - axial_gas),
        evaporated * radial + 0.2 * mass * (radial - radial_gas),
        evaporated * temp + 0.1 * mass * (temp - gas_temp),
    )
    return updated, terms


def one_hot(index, size):
    width = index.shape[1]
    return (lax.broadcasted_iota(jnp.int32, (size, width), 0) == index).astype(f32).astype(bf16)


def gather_block(table, around, where):
    got = jnp.dot(table[...], jnp.concatenate([around, around], axis=0), preferred_element_type=f32)
    mask = lax.broadcasted_iota(jnp.int32, (ROWS, where.shape[1]), 0) == (where >> 9)
    return [
        jnp.sum(jnp.where(mask, got[ROWS * k : ROWS * k + ROWS], 0.0), axis=0, keepdims=True) for k in range(4)
    ]


def deposit_block(terms, around, where):
    row = one_hot(where >> 9, ROWS)
    halves = [split2(t) for t in terms]
    spread = jnp.concatenate(
        [jnp.concatenate([row * h[side] for h in halves], axis=0) for side in range(2)],
        axis=1,
    )
    twice = jnp.concatenate([around, around], axis=1)
    return lax.dot_general(spread, twice, (((1,), (1,)), ((), ())), preferred_element_type=f32)


def stencil_soon():
    a, r = lax.axis_index("ax"), lax.axis_index("rad")
    near_first = (a == 0) & (r == 1)
    return is_early() | near_first | ((lax.rem(a, 2) == 1) & (a > 1) & (lax.rem(a, WRAP) != WRAP - 1))


def first_kernel(gas, viscosity, picks, axial_b, radial_a, radial_b, out, table, speed):
    pack_axial(gas, picks, axial_b, parity("ax") == 1)
    pack_radial(gas, picks, radial_a, parity("rad") == 0)
    pack_radial(gas, picks, radial_b, parity("rad") == 1)
    pl.when(stencil_soon())(lambda: stencil_part(gas, viscosity, out, table, speed))


def early_kernel(gas, picks, drops, cells, kept, out_in, table, late, out, drops_out, *scratch):
    @pl.when(is_early())
    def _():
        pack_axial(gas, picks, late, parity("ax") == 1)
        droplet_part(drops, cells, kept, table, out, drops_out, *scratch)


def late_kernel(gas, viscosity, drops, cells, kept, out_in, drops_in, table_in, out, drops_out, table, speed, *scratch):
    pl.when(jnp.logical_not(stencil_soon()))(lambda: stencil_part(gas, viscosity, out, table, speed))
    pl.when(jnp.logical_not(is_early()))(lambda: droplet_part(drops, cells, kept, table, out, drops_out, *scratch))


def droplet_part(drops, cells, kept, table, out, drops_out, samples, terms, source, hots):
    slot = lax.broadcasted_iota(jnp.int32, (1, SLOTS), 1)
    filled = jnp.max(jnp.where(drops[0:1, :] > 0.0, slot + 1, 0))
    blocks = lax.div(filled + 1023, 1024)

    def join(load, first, rows):
        return jnp.concatenate([load(pl.ds(first + s, 1)) for s in range(rows)], axis=1)

    def lanes(first, rows):
        return pl.ds(first * 128 if isinstance(first, int) else pl.multiple_of(first * 128, 128 * rows), 128 * rows)

    def sample(first, rows):
        where = join(lambda at: cells[at, :], first, rows)
        around = one_hot(where & (CZ - 1), CZ)
        hots[:, lanes(first, rows)] = around
        got = gather_block(table, around, where)
        for k in range(4):
            for s in range(rows):
                samples[k, pl.ds(first + s, 1), :] = got[k][:, 128 * s : 128 * s + 128]

    def deposit(first, rows):
        where = join(lambda at: cells[at, :], first, rows)
        return deposit_block(
            [join(lambda at: terms[k, at, :], first, rows) for k in range(4)], hots[:, lanes(first, rows)], where
        )

    def sample_loop(b, carry):
        sample(pl.multiple_of(8 * b, 8), 8)
        return carry

    def deposit_loop(b, carry):
        source[...] += deposit(pl.multiple_of(8 * b, 8), 8)
        return carry

    @pl.when(blocks == 4)
    def _():
        for b in range(8):
            sample(4 * b, 4)

    @pl.when(blocks < 4)
    def _():
        lax.fori_loop(0, blocks, sample_loop, 0)

    fields = [
        jnp.concatenate([drops[f : f + 1, 128 * s : 128 * s + 128] for s in range(32)], axis=0) for f in range(1, 4)
    ]
    updated, new_terms = evaporate(kept[...], *fields, [samples[k] for k in range(4)])
    for f in range(4):
        terms[f] = new_terms[f]
        for s in range(32):
            drops_out[f : f + 1, 128 * s : 128 * s + 128] = updated[f][s : s + 1, :]

    @pl.when(blocks == 4)
    def _():
        source[...] = deposit(0, 4)
        for b in range(1, 8):
            source[...] += deposit(4 * b, 4)

    @pl.when(blocks < 4)
    def _():
        source[...] = jnp.zeros_like(source)
        lax.fori_loop(0, blocks, deposit_loop, 0)

    for c, slot in ((0, 0), (1, 1), (2, 2), (4, 3), (5, 0)):
        out[c] += source[slot * ROWS : slot * ROWS + ROWS, :]


def stencil_part(gas, viscosity, out, table, speed):
    inverse = 1.0 / gas[0]
    scale = time_step / 12.0
    for k, c in enumerate((1, 2, 4, 5)):
        quotient = gas[c] * inverse
        if k < 2:
            speed[k] = quotient * scale
        hi, lo = split2(quotient)
        table[ROWS * k : ROWS * k + ROWS, 0:CZ] = hi
        table[ROWS * k : ROWS * k + ROWS, CZ : 2 * CZ] = lo
    speed[2] = gas[3] * inverse * scale
    speed[3] = viscosity[...] * scale

    def component(c, carry):
        layers = [gas[c, CY * i : CY * i + CY, :] for i in range(CX)]
        zero = jnp.zeros_like(layers[0])
        for i in range(CX):
            rows = slice(CY * i, CY * i + CY)
            x = layers[i]
            ax = [layers[i + k] if 0 <= i + k < CX else zero for k in (-2, -1, 1, 2)]
            tall = jnp.concatenate([x, zero[0:8]], axis=0)
            ra = [pltpu.roll(tall, (-k) % (CY + 8), axis=0)[0:CY] for k in (-2, -1, 1, 2)]
            az = [pltpu.roll(x, (-k) % CZ, axis=1) for k in (-2, -1, 1, 2)]
            near = (ax[1] + ax[2]) + (ra[1] + ra[2]) + (az[1] + az[2])
            far = (ax[0] + ax[3]) + (ra[0] + ra[3]) + (az[0] + az[3])
            value = x + speed[3, rows, :] * (16.0 * near - far - 90.0 * x)
            for j, n in enumerate((ax, ra, az)):
                value = value - speed[j, rows, :] * (8.0 * (n[2] - n[1]) - (n[3] - n[0]))
            out[c, rows, :] = value
        return carry

    lax.fori_loop(0, C, component, 0)


def is_last():
    a = lax.axis_index("ax")
    return (lax.rem(a, WRAP) == WRAP - 1) & (a < lax.axis_size("ax") - 1)


def soon_kernel(*refs):
    pl.when(jnp.logical_not(is_last()))(lambda: final_kernel(None, *refs))


def last_kernel(late, part, updated, gas, viscosity, table, axial_a, axial_b, radial_a, radial_b, *refs):
    given = (part, updated, gas, viscosity, table, axial_a, axial_b, radial_a, radial_b)
    pl.when(is_last())(lambda: final_kernel(late, *given, *refs[3:]))


def final_kernel(
    late, part, updated_in, gas, viscosity, table, axial_a, axial_b_in, radial_a, radial_b,
    out_hbm, drops_hbm, arrivals_hbm, out, arrivals, weights, sems,
):
    copies = [
        pltpu.make_async_copy(updated_in, drops_hbm, sems.at[0]),
        pltpu.make_async_copy(arrivals, arrivals_hbm, sems.at[1]),
    ] + [pltpu.make_async_copy(out.at[c], out_hbm.at[c], sems.at[2 + c]) for c in range(C)]
    copies[0].start()
    odd_ax, odd_rad = parity("ax"), parity("rad")
    if late is None:
        axial_b = axial_b_in
    else:
        axial_b = late
    got = []
    for odd, a, b, base in ((odd_ax, axial_a, axial_b, 192), (odd_rad, radial_a, radial_b, 96)):
        in_a, in_b = a[base : base + 8, 0:CAP], b[base : base + 8, 0:CAP]
        got.append(jnp.where(odd == 1, in_a, in_b))
        got.append(jnp.where(odd == 1, in_b, in_a))
    got = jnp.concatenate(got, axis=1)
    where = got[4:5].astype(jnp.int32)
    around = one_hot(where & (CZ - 1), CZ)
    samples = gather_block(table, around, where)
    changed, terms = evaporate(got[0:1], got[1:2], got[2:3], got[3:4], samples)
    arrivals[...] = jnp.concatenate(changed, axis=0)
    copies[1].start()
    source = deposit_block(terms, around, where)
    lane = lax.broadcasted_iota(jnp.int32, (CY, CZ), 0)
    for i in range(CX):
        rows = slice(CY * i, CY * i + CY)
        factor = viscosity[rows, :] * (time_step / 12.0)
        radial = gas[2, rows, :] / gas[0, rows, :] * (time_step / 12.0)
        for n, last in enumerate((odd_rad == 0, odd_rad == 1)):
            speed = jnp.where(last, -1.0, 1.0) * radial
            first, second = jnp.where(last, CY - 1, 0), jnp.where(last, CY - 2, 1)
            near, far = 16.0 * factor + 8.0 * speed, -(factor + speed)
            weights[2 * n, rows, :] = jnp.where(lane == first, near, jnp.where(lane == second, far, 0.0))
            weights[2 * n + 1, rows, :] = jnp.where(lane == first, far, 0.0)
    edges = []
    for message, last in ((axial_a, odd_ax == 0), (axial_b, odd_ax == 1)):
        sign = jnp.where(last, -1.0, 1.0)
        for k in range(2):
            rows = pl.ds(pl.multiple_of(jnp.where(last, (CX - 1 - k) * CY, k * CY), CY), CY)
            edges.append((message, k, rows, sign))
    for c in range(C):
        for i in range(CX):
            rows = slice(CY * i, CY * i + CY)
            at = c * CX + i
            value = part[c, rows, :]
            for n, message in enumerate((radial_a, radial_b)):
                value = value + weights[2 * n, rows, :] * message[at : at + 1, :]
                value = value + weights[2 * n + 1, rows, :] * message[48 + at : 49 + at, :]
            slot = (0, 1, 2, None, 3, 0)[c]
            if slot is not None:
                value = value + source[slot * ROWS + CY * i : slot * ROWS + CY * i + CY, :]
            out[c, rows, :] = value
        for message, k, rows, sign in edges:
            factor = viscosity[rows, :] * (time_step / 12.0)
            speed = sign * (gas[1, rows, :] / gas[0, rows, :] * (time_step / 12.0))
            near, far = 16.0 * factor + 8.0 * speed, -(factor + speed)
            if k == 0:
                change = near * message[32 * c : 32 * c + CY, :] + far * message[32 * c + CY : 32 * c + 2 * CY, :]
            else:
                change = far * message[32 * c : 32 * c + CY, :]
            out[c, rows, :] += change
        copies[2 + c].start()
    for copy in copies:
        copy.wait()


def routes(n_ax, n_rad):
    flat = lambda a, r: a * n_rad + r
    axial_a, axial_b, radial_a, radial_b, late = [], [], [], [], []
    for a in range(n_ax):
        for r in range(n_rad):
            if a + 1 < n_ax:
                up = (flat(a, r), flat(a + 1, r))
                (axial_a if a % 2 == 0 else axial_b).append(up)
                down = late if (a + 1) % WRAP == 0 else axial_a if a % 2 == 0 else axial_b
                down.append(up[::-1])
            if r + 1 < n_rad:
                out = (flat(a, r), flat(a, r + 1))
                (radial_a if r % 2 == 0 else radial_b).append(out)
                back = radial_a if r % 2 == 0 else radial_b
                back.append(out[::-1])
    return axial_a, axial_b, radial_a, radial_b, late


def body(gas_state, viscosity, droplets, drop_cells, move_lists, move_counts):
    gas = gas_state.reshape(C, ROWS, CZ)
    thick = viscosity.reshape(ROWS, CZ)
    cells = drop_cells.reshape(32, 128)
    shape = jax.ShapeDtypeStruct
    axial_a, picks, kept, gas, drops, cells = pl.pallas_call(
        prep_kernel,
        out_shape=(
            shape((200, CZ), f32),
            shape((8, 4 * CAP), f32),
            shape((32, 128), f32),
            shape((C, ROWS, CZ), f32),
            shape((4, SLOTS), f32),
            shape((32, 128), jnp.int32),
        ),
        in_specs=[HB] * 5,
        out_specs=(VM,) * 6,
        scratch_shapes=[
            pltpu.VMEM((1, 4, CAP), jnp.int32),
            pltpu.SMEM((1, 4), jnp.int32),
            pltpu.SemaphoreType.DMA((10,)),
        ],
        compiler_params=params,
        name="prep",
    )(*(pltpu.with_memory_space_constraint(x, pltpu.HBM) for x in (gas, droplets, cells, move_lists, move_counts)))
    both = ("ax", "rad")
    to_a, to_b, to_c, to_d, to_late = routes(lax.axis_size("ax"), lax.axis_size("rad"))
    came_a = lax.ppermute(axial_a, both, to_a)
    part, updated, table = shape((C, ROWS, CZ), f32), shape((4, SLOTS), f32), shape((4 * ROWS, 2 * CZ), bf16)
    speed = [pltpu.VMEM((4, ROWS, CZ), f32)]
    scratch = [pltpu.VMEM((4, 32, 128), f32), pltpu.VMEM((4, 32, 128), f32), pltpu.VMEM((4 * ROWS, CZ), f32), pltpu.VMEM((CZ, SLOTS), bf16)]
    cost = lambda flops: pl.CostEstimate(flops=flops, bytes_accessed=0, transcendentals=0)

    axial_b, radial_a, radial_b, part, table = pl.pallas_call(
        first_kernel,
        out_shape=(shape((200, CZ), f32), shape((104, CZ), f32), shape((104, CZ), f32), part, table),
        in_specs=[VM] * 3,
        out_specs=(VM,) * 5,
        scratch_shapes=speed,
        compiler_params=params,
        cost_estimate=cost(4000000000),
        name="first",
    )(gas, thick, picks)
    came_b = lax.ppermute(axial_b, both, to_b)
    came_d = lax.ppermute(radial_b, both, to_d)
    came_c = lax.ppermute(radial_a, both, to_c)
    late, part, updated = pl.pallas_call(
        early_kernel,
        out_shape=(shape((200, CZ), f32), shape(part.shape, f32), updated),
        in_specs=[VM] * 7,
        out_specs=(VM,) * 3,
        scratch_shapes=scratch,
        compiler_params=params,
        input_output_aliases={5: 1},
        cost_estimate=cost(0),
        name="early",
    )(gas, picks, drops, cells, kept, part, table)
    came_late = lax.ppermute(late, both, to_late)
    part, updated, table = pl.pallas_call(
        late_kernel,
        out_shape=tuple(shape(x.shape, x.dtype) for x in (part, updated, table)),
        in_specs=[VM] * 8,
        out_specs=(VM,) * 3,
        scratch_shapes=speed + scratch,
        compiler_params=params,
        input_output_aliases={5: 0, 6: 1, 7: 2},
        cost_estimate=cost(0),
        name="late",
    )(gas, thick, drops, cells, kept, part, updated, table)
    finals = (shape((C, ROWS, CZ), f32), shape((4, SLOTS), f32), shape((4, 4 * CAP), f32))
    scratch = [
        pltpu.VMEM((C, ROWS, CZ), f32),
        pltpu.VMEM((4, 4 * CAP), f32),
        pltpu.VMEM((4, ROWS, CZ), f32),
        pltpu.SemaphoreType.DMA((8,)),
    ]
    common = (part, updated, gas, thick, table, came_a, came_b, came_c, came_d)
    finals_soon = pl.pallas_call(
        soon_kernel,
        out_shape=finals,
        in_specs=[VM] * 9,
        out_specs=(HB,) * 3,
        scratch_shapes=scratch,
        compiler_params=params,
        cost_estimate=pl.CostEstimate(flops=4000000000, bytes_accessed=0, transcendentals=0),
        name="soon",
    )(*common)
    out, drops_out, arrivals_out = pl.pallas_call(
        last_kernel,
        out_shape=finals,
        in_specs=[VM] * 10 + [HB] * 3,
        out_specs=(HB,) * 3,
        scratch_shapes=scratch,
        compiler_params=params,
        input_output_aliases={10: 0, 11: 1, 12: 2},
        cost_estimate=pl.CostEstimate(flops=0, bytes_accessed=0, transcendentals=0),
        name="last",
    )(came_late, *common, *finals_soon)
    return out.reshape(gas_state.shape), drops_out, arrivals_out


def solution(mesh):
    placed = (
        P(None, "ax", "rad", None),
        P("ax", "rad", None),
        P(None, ("ax", "rad")),
        P(("ax", "rad")),
        P(("ax", "rad"), None, None),
        P(("ax", "rad"), None),
    )
    return jax.shard_map(
        body,
        mesh=mesh,
        in_specs=placed,
        out_specs=(P(None, "ax", "rad", None), P(None, ("ax", "rad")), P(None, ("ax", "rad"))),
        check_vma=False,
    )
```
